32 devices in a mesh: dp: 4 (over y, x), expert: 8 (over z, core).
Axes of the slice: x: 2, y: 2, z: 4, core: 2. Of those that a mesh axis runs over, the one named last changes fastest.
Arguments:
- tokens: bfloat16 [8, 1024, 2048], P('expert', 'dp'), may hold values from -6 to 6
- segment_ids: int32 [8, 1024], P('expert'), may hold values from 0 to 2, as said below
- routes: int32 [8, 1024, 8], P('expert', 'dp'), may hold values from 0 to 31, all different within a row; in each aligned block of 256 rows (0 to 255, 256 to 511, ..., all dimensions but the last counted through in order) at most 80 rows name the same one
- w_query: bfloat16 [2048, 4096], P(('dp', 'expert')), may hold values from -0.125 to 0.125
- w_key: bfloat16 [2048, 512], P(('dp', 'expert')), may hold values from -0.125 to 0.125
- w_value: bfloat16 [2048, 512], P(('dp', 'expert')), may hold values from -0.125 to 0.125
- w_output: bfloat16 [4096, 2048], P(('dp', 'expert')), may hold values from -1.5 to 1.5
- w_router: bfloat16 [2048, 32], P(('dp', 'expert')), may hold values from -0.0625 to 0.0625
- gain_attn: bfloat16 [2048], P(('dp', 'expert')), may hold values from 0.5 to 1.5
- gain_moe: bfloat16 [2048], P(('dp', 'expert')), may hold values from 0.5 to 1.5
- gain_query: bfloat16 [128], P(('dp', 'expert')), may hold values from 0.5 to 1.5
- gain_key: bfloat16 [128], P(('dp', 'expert')), may hold values from 0.5 to 1.5
- w_gate: bfloat16 [32, 2048, 768], P('expert'), may hold values from -0.125 to 0.125
- w_up: bfloat16 [32, 2048, 768], P('expert'), may hold values from -0.125 to 0.125
- w_down: bfloat16 [32, 768, 2048], P('expert'), may hold values from -0.875 to 0.875
- cotangent: bfloat16 [8, 1024, 2048], P('expert', 'dp'), may hold values from -6 to 6
Outputs:
- block_out: bfloat16 [8, 1024, 2048], P('expert', 'dp')
- grad_tokens: float32 [8, 1024, 2048], P('expert', 'dp')
- grad_query: float32 [2048, 4096], P(('dp', 'expert'))
- grad_key: float32 [2048, 512], P(('dp', 'expert'))
- grad_value: float32 [2048, 512], P(('dp', 'expert'))
- grad_output: float32 [4096, 2048], P(('dp', 'expert'))
- grad_router: float32 [2048, 32], P(('dp', 'expert'))
- grad_gain_attn: float32 [2048], P(('dp', 'expert'))
- grad_gain_moe: float32 [2048], P(('dp', 'expert'))
- grad_gain_query: float32 [128], P(('dp', 'expert'))
- grad_gain_key: float32 [128], P(('dp', 'expert'))
- grad_gate: float32 [32, 2048, 768], P('expert')
- grad_up: float32 [32, 2048, 768], P('expert')
- grad_down: float32 [32, 768, 2048], P('expert')
The draws below stay inside these ranges and needn't reach their ends.
Inputs may be any that keep to these rules, and one draw needn't show every extreme that they name: `routes`: each row names 8 different experts; in the 256 rows of one device no expert is named by more than 80 rows, and in some device one expert is named by exactly 80. `segment_ids`: never falling along a sequence; every sequence holds documents 0, 1 and 2: document 0 has 128 or more tokens and ends within the first 256 positions, document 1 ends within the last 256 positions, document 2 has 128 or more tokens.
All inputs are finite; a program needn't handle non-finite values.
Results may differ from the reference program's by a relative error of at most 0.02.
Values may be sent and summed in bfloat16 or wider, within the bound.
A program may use at most 384 MiB of HBM per device.

```python
import math
from functools import partial
import jax
import jax.numpy as jnp
import numpy as np
from jax import lax

D = 2048
HEADS = 32
KV_HEADS = 4
HD = 128
FF = 768
TOP = 8
EXPERTS = 32
TOK_DEV = 256
SEQLEN = 1024
SEQS = 8
CAP = 80
MIN_DOC = 128
N_DP = 4


def draw_segment_ids(key, part):
    key = jax.random.fold_in(key, 7)
    first_key, second_key = jax.random.split(key)
    first_end = jax.random.randint(first_key, (SEQS,), MIN_DOC, TOK_DEV)
    second_end = jax.random.randint(second_key, (SEQS,), (N_DP - 1) * TOK_DEV + 1, SEQLEN - MIN_DOC + 1)
    positions = jnp.arange(SEQLEN, dtype=jnp.int32)
    segment = (positions[None, :] >= first_end[:, None]).astype(jnp.int32) + (positions[None, :] >= second_end[:, None]).astype(jnp.int32)
    return segment.astype(jnp.int32)


def block_levels(key, dims, shards, least, high):
    level, own = 1.0, jax.random.fold_in(key, 6)
    for dim, shards_of in shards:
        heights = jnp.exp(jax.random.uniform(jax.random.fold_in(own, dim), (shards_of,), jnp.float32, least / len(shards), high / len(shards)))
        level = level * jnp.repeat(heights, dims[dim] // shards_of).reshape([-1 if axis == dim else 1 for axis in range(len(dims))])
    return level


def shared_out(own_key, own, number, rows, count, top, limit, lean):
    order = jax.random.permutation(own_key, count)
    heavy_load, usual = portions_of(count, rows * top, limit, lean, True), portions_of(count, rows * top, limit, lean, False)
    places = jnp.arange(count)

    def named(tallies, rotation):
        used = int((tallies > 0).sum())
        fixed = max(1, used // 4)
        passed = fixed + (places - fixed + rotation * (used - fixed)) % max(1, count - fixed)
        return jnp.zeros((count,), jnp.int32).at[order[jnp.where(places < fixed, places, passed)]].set(jnp.asarray(tallies, jnp.int32))

    tallies = jnp.where(number % 4 == 0, named(heavy_load, number // 4), named(usual, number - number // 4 - 1))
    mixed = jax.random.permutation(jax.random.fold_in(own, 3), count)
    source_of, receiver = mixed[0:count // 2 * 2:2], mixed[1:count // 2 * 2:2]
    room = jnp.minimum(tallies[source_of] - 1, limit - tallies[receiver]) // 2
    room = jnp.where((source_of == order[0]) | (receiver == order[0]) | (tallies[receiver] == 0), 0, jnp.maximum(room, 0))
    passed = jax.random.randint(jax.random.fold_in(own, 4), (count // 2,), 0, 1 << 20) % (room + 1)
    tallies = tallies.at[source_of].add(-passed).at[receiver].add(passed)
    labels = jnp.searchsorted(jnp.cumsum(tallies), jnp.arange(rows * top), side="right").astype(jnp.int32)
    table = labels.reshape(top, rows).T
    table = table[jax.random.permutation(jax.random.fold_in(own, 1), rows)]
    rotation = jax.random.randint(jax.random.fold_in(own, 2), (rows, 1), 0, top)
    return jnp.take_along_axis(table, (jnp.arange(top)[None, :] + rotation) % top, axis=1)


def portions_of(amount, total, most, slope, full):
    portions = [(1 << 20) // math.isqrt(rank ** slope) + 1 for rank in range(1, amount + 1)]
    largest = most if full else min(most, max(-(-total // amount), total * portions[0] // sum(portions)))
    least = 1 if total - largest >= amount - 1 else 0
    given, rest = [largest] + [least] * (amount - 1), total - largest - least * (amount - 1)
    while rest > 0:
        candidates = [i for i in range(1, amount) if given[i] < largest] or [i for i in range(1, amount) if given[i] < most]
        pool, remaining = sum([portions[i] for i in candidates]), rest
        for i in candidates:
            extra = min(most - given[i], max(1, remaining * portions[i] // pool), rest)
            given[i] = given[i] + extra
            rest = rest - extra
    return np.array(given)


def noise(rng, extent, deviation, most, cuts=(), held_as=jnp.bfloat16):
    values = jax.random.normal(rng, extent, jnp.float32) * deviation
    if len(cuts) > 0:
        values = block_levels(rng, extent, cuts, -0.22, 0.18) * values
    return jnp.clip(values, min=-most, max=most).astype(held_as)


def setup_inputs(seed: int = 0) -> dict:
    seeds = jax.random.split(jax.random.key(seed), 17)
    tokens = noise(seeds[0], (SEQS, SEQLEN, D), 1.0, 6.0, ((0, 8), (1, 4)))
    segment_ids = draw_segment_ids(jax.random.fold_in(seeds[16], 71), 0)
    routes_keys = jax.random.split(jax.random.fold_in(seeds[2], 1), SEQS * SEQLEN // TOK_DEV)
    routes_turns = jax.random.permutation(jax.random.fold_in(seeds[2], 3), SEQS * SEQLEN // TOK_DEV)
    routes = jax.vmap(lambda own, number: shared_out(jax.random.fold_in(seeds[2], 2), own, number, TOK_DEV, EXPERTS, TOP, CAP, 1))(routes_keys, routes_turns).reshape((SEQS, SEQLEN, TOP))
    w_query = noise(seeds[3], (D, HEADS * HD), D ** -0.5, 0.125, ((0, 32),))
    w_key = noise(seeds[4], (D, KV_HEADS * HD), D ** -0.5, 0.125, ((0, 32),))
    w_value = noise(seeds[5], (D, KV_HEADS * HD), D ** -0.5, 0.125, ((0, 32),))
    w_output = noise(seeds[6], (HEADS * HD, D), (HEADS * HD // 256) ** -0.5, 1.5, ((0, 32),))
    w_router = noise(seeds[7], (D, EXPERTS), (4 * D) ** -0.5, 0.0625, ((0, 32),))
    gain_attn = jnp.clip(1.0 + 0.1 * jax.random.normal(seeds[8], (D,), jnp.float32), 0.5, 1.5).astype(jnp.bfloat16)
    gain_moe = jnp.clip(1.0 + 0.1 * jax.random.normal(seeds[9], (D,), jnp.float32), 0.5, 1.5).astype(jnp.bfloat16)
    gain_query = jnp.clip(1.0 + 0.1 * jax.random.normal(seeds[10], (HD,), jnp.float32), 0.5, 1.5).astype(jnp.bfloat16)
    gain_key = jnp.clip(1.0 + 0.1 * jax.random.normal(seeds[11], (HD,), jnp.float32), 0.5, 1.5).astype(jnp.bfloat16)
    w_gate = noise(seeds[12], (EXPERTS, D, FF), D ** -0.5, 0.125, ((0, 8),))
    w_up = noise(seeds[13], (EXPERTS, D, FF), D ** -0.5, 0.125, ((0, 8),))
    w_down = noise(seeds[14], (EXPERTS, FF, D), (FF // 16) ** -0.5, 0.875, ((0, 8),))
    cotangent = noise(seeds[15], (SEQS, SEQLEN, D), 1.0, 6.0, ((0, 8), (1, 4)))
    return {"tokens": tokens, "segment_ids": segment_ids, "routes": routes, "w_query": w_query, "w_key": w_key, "w_value": w_value, "w_output": w_output, "w_router": w_router, "gain_attn": gain_attn, "gain_moe": gain_moe, "gain_query": gain_query, "gain_key": gain_key, "w_gate": w_gate, "w_up": w_up, "w_down": w_down, "cotangent": cotangent}


EPSILON = 1e-06
ROPE_BASE = 1000000.0
PRECISE = lax.Precision.HIGHEST

@jax.custom_vjp
def low(v):
    return lax.optimization_barrier(v.astype(jnp.bfloat16)).astype(jnp.float32)

@jax.custom_vjp
def low_back(v):
    return v

def low_keep(v):
    return (low(v), None)

def low_pass(kept, grad):
    return (grad,)

def back_keep(v):
    return (v, None)

def back_low(kept, grad):
    return (low(grad),)
low.defvjp(low_keep, low_pass)
low_back.defvjp(back_keep, back_low)

def norm_rows(values, gain_row):
    return values * lax.rsqrt(lax.optimization_barrier(jnp.mean(values * values, axis=-1, keepdims=True)) + EPSILON) * gain_row

def rotate(values, places):
    half_size = values.shape[-1] // 2
    frequency = ROPE_BASE ** (-jnp.arange(half_size, dtype=jnp.float32) * 2.0 / values.shape[-1])
    angles = places[:, None] * frequency[None, :]
    angles = jnp.concatenate([angles, angles], axis=-1)[:, None, :]
    turned = jnp.concatenate([-values[..., half_size:], values[..., :half_size]], axis=-1)
    return values * jnp.cos(angles) + turned * jnp.sin(angles)

def softmax_rows(scores):
    largest = lax.optimization_barrier(jnp.max(scores, axis=-1, keepdims=True))
    raised = jnp.exp(scores - largest)
    return raised / lax.optimization_barrier(jnp.sum(raised, axis=-1, keepdims=True))

def attend(pieces):
    queries, key_rows, value_rows, segment = pieces
    length = queries.shape[0]
    groups = key_rows.shape[1]
    grouped = queries.reshape(length, groups, -1, queries.shape[-1])
    scores = jnp.einsum('tgjd,kgd->gjtk', grouped, key_rows, precision=PRECISE) * queries.shape[-1] ** (-0.5)
    positions = jnp.arange(length, dtype=jnp.int32)
    allowed = (positions[None, :] <= positions[:, None]) & (segment[:, None] == segment[None, :])
    scores = low_back(jnp.where(allowed[None, None], scores, -1e+30))
    weights = low(softmax_rows(scores))
    attended = jnp.einsum('gjtk,kgd->tgjd', weights, value_rows, precision=PRECISE)
    return attended.reshape(length, -1, attended.shape[-1])

def experts_block(pieces, w_gate, w_up, w_down):
    normed, chosen, gate_probs = pieces
    experts = w_gate.shape[0]
    tok_count, top_count = chosen.shape
    model_width = normed.shape[1]
    flat_routes = chosen.reshape(-1)
    onehot = (flat_routes[:, None] == jnp.arange(experts, dtype=jnp.int32)[None, :]).astype(jnp.int32)
    rank_in = lax.optimization_barrier(jnp.sum(jnp.cumsum(onehot, axis=0) * onehot, axis=1)) - 1
    slot_index = (flat_routes * CAP + rank_in).astype(jnp.int32)
    rows_in = low_back(jnp.broadcast_to(normed[:, None, :], (tok_count, top_count, model_width))).reshape(-1, model_width)
    buffer = jnp.zeros((experts * CAP, model_width), normed.dtype).at[slot_index].set(rows_in)
    buffer = buffer.reshape(experts, CAP, model_width)
    gate_in = low_back(jnp.einsum('ecd,edf->ecf', buffer, w_gate, precision=PRECISE))
    up_in = low_back(jnp.einsum('ecd,edf->ecf', buffer, w_up, precision=PRECISE))
    active = low(gate_in * jax.nn.sigmoid(gate_in) * up_in)
    result = jnp.einsum('ecf,efd->ecd', active, w_down, precision=PRECISE).reshape(experts * CAP, model_width)
    returned = low_back(low(result[slot_index])).reshape(tok_count, top_count, model_width)
    return lax.optimization_barrier(jnp.sum(gate_probs[:, :, None] * returned, axis=1))

def forward(tokens, w_query, w_key, w_value, w_output, w_router, gain_attn, gain_moe, gain_query, gain_key, w_gate, w_up, w_down, segment_ids, routes):
    seq_count, length, model_width = tokens.shape
    head_size = gain_query.shape[0]
    head_count = w_query.shape[1] // head_size
    groups = w_key.shape[1] // head_size
    normed = low(norm_rows(tokens, gain_attn))
    query_pre = low_back(jnp.dot(normed, w_query, precision=PRECISE)).reshape(seq_count, length, head_count, head_size)
    key_pre = low_back(jnp.dot(normed, w_key, precision=PRECISE)).reshape(seq_count, length, groups, head_size)
    value_rows = low_back(low(jnp.dot(normed, w_value, precision=PRECISE))).reshape(seq_count, length, groups, head_size)
    places = jnp.arange(length, dtype=jnp.float32)
    query_rot = low_back(low(rotate(norm_rows(query_pre, gain_query), places)))
    key_rot = low_back(low(rotate(norm_rows(key_pre, gain_key), places)))
    attended = lax.map(jax.checkpoint(attend), (query_rot, key_rot, value_rows, segment_ids))
    attended = low_back(low(attended)).reshape(seq_count, length, head_count * head_size)
    branch = low_back(jnp.dot(attended, w_output, precision=PRECISE))
    hidden = tokens + branch
    normed_moe = low(norm_rows(hidden, gain_moe))
    logits = jnp.dot(normed_moe, w_router, precision=PRECISE)
    gate_probs = softmax_rows(jnp.take_along_axis(logits, routes, axis=-1))
    blocks = seq_count * length // TOK_DEV
    moe_sum = lax.map(jax.checkpoint(lambda pieces: experts_block(pieces, w_gate, w_up, w_down)), (normed_moe.reshape(blocks, TOK_DEV, model_width), routes.reshape(blocks, TOK_DEV, -1), gate_probs.reshape(blocks, TOK_DEV, -1)))
    return hidden + moe_sum.reshape(seq_count, length, model_width)

def reference(tokens, segment_ids, routes, w_query, w_key, w_value, w_output, w_router, gain_attn, gain_moe, gain_query, gain_key, w_gate, w_up, w_down, cotangent):
    floats = [a.astype(jnp.float32) for a in (tokens, w_query, w_key, w_value, w_output, w_router, gain_attn, gain_moe, gain_query, gain_key, w_gate, w_up, w_down)]
    result, pullback = jax.vjp(partial(forward, segment_ids=segment_ids, routes=routes), *floats)
    grads = pullback(cotangent.astype(jnp.float32))
    return (result.astype(jnp.bfloat16), grads[0], grads[1], grads[2], grads[3], grads[4], grads[5], grads[6], grads[7], grads[8], grads[9], grads[10], grads[11], grads[12])
```

```python
import jax
import jax.numpy as jnp
from jax import lax
from jax.sharding import PartitionSpec as P

CAP = 80


EPSILON = 1e-06
ROPE_BASE = 1000000.0
PRECISE = lax.Precision.HIGHEST
F32 = jnp.float32
BF16 = jnp.bfloat16


def norm_rows(values, gain_row):
    return (
        values * lax.rsqrt(jnp.mean(values * values, axis=-1, keepdims=True) + EPSILON) * gain_row
    )


def rotate(values, places):
    half_size = values.shape[-1] // 2
    frequency = ROPE_BASE ** (-jnp.arange(half_size, dtype=F32) * 2.0 / values.shape[-1])
    angles = places[:, None] * frequency[None, :]
    angles = jnp.concatenate([angles, angles], axis=-1)[:, None, :]
    turned = jnp.concatenate([-values[..., half_size:], values[..., :half_size]], axis=-1)
    return values * jnp.cos(angles) + turned * jnp.sin(angles)


def activate(gate_vals, up_vals):
    return gate_vals * jax.nn.sigmoid(gate_vals) * up_vals


def masked_softmax(logits, mask):
    kept = jnp.where(mask, logits, -jnp.inf)
    largest = jnp.max(kept, axis=-1, keepdims=True)
    raised = jnp.where(mask, jnp.exp(logits - largest), 0.0)
    return raised / jnp.sum(raised, axis=-1, keepdims=True)


def after(value, *others):
    return lax.optimization_barrier((value, *others))[0]


def dot(spec, left, right):
    return jnp.einsum(spec, left, right, preferred_element_type=F32)


def on_device(
    tokens,
    segment_ids,
    routes,
    w_query,
    w_key,
    w_value,
    w_output,
    w_router,
    gain_attn,
    gain_moe,
    gain_query,
    gain_key,
    w_gate,
    w_up,
    w_down,
    cotangent,
):
    bands, peers = lax.axis_size("dp"), lax.axis_size("expert")
    band, peer = lax.axis_index("dp"), lax.axis_index("expert")
    own_tokens = tokens[0]
    tok_count, width = own_tokens.shape
    band_rows = w_query.shape[0]
    experts = w_router.shape[1]
    gain_rows = gain_query.shape[0]
    head_size = gain_rows * bands * peers
    heads = w_query.shape[1] // head_size // bands
    groups = w_key.shape[1] // head_size // bands
    group_size = heads // groups
    q_cols, k_cols = heads * head_size, groups * head_size
    qkv_cols = q_cols + 2 * k_cols
    owned = experts // peers

    tokens_all = lax.all_gather(own_tokens, "dp", axis=0, tiled=True)
    small = jnp.concatenate(
        [
            w_router,
            gain_attn[:, None],
            gain_moe[:, None],
            jnp.pad(gain_query, (0, band_rows - gain_rows))[:, None],
            jnp.pad(gain_key, (0, band_rows - gain_rows))[:, None],
        ],
        axis=1,
    )
    small = jnp.pad(small, ((0, 0), (0, 128 - small.shape[1])))
    packed = jnp.concatenate(
        [
            w_query.reshape(band_rows, bands, q_cols),
            w_key.reshape(band_rows, bands, k_cols),
            w_value.reshape(band_rows, bands, k_cols),
            jnp.broadcast_to(small[:, None], (band_rows, bands, 128)),
        ],
        axis=-1,
    ).transpose(1, 0, 2)
    swapped = lax.all_to_all(packed, "dp", split_axis=0, concat_axis=0, tiled=True)
    packed_all = lax.all_gather(swapped, "expert", axis=1, tiled=True).reshape(width, -1)
    qkv_w = packed_all[:, :qkv_cols]
    small_all = packed_all[:, qkv_cols:]
    router_full = small_all[:, :experts]
    attn_gain = small_all[:, experts].astype(F32)
    moe_gain = small_all[:, experts + 1].astype(F32)
    head_gains = small_all.reshape(bands * peers, band_rows, 128)[:, :gain_rows]
    query_gain = head_gains[:, :, experts + 2].reshape(-1).astype(F32)
    key_gain = head_gains[:, :, experts + 3].reshape(-1).astype(F32)
    out_w = lax.all_gather(w_output, "expert", axis=0, tiled=True)
    routes_all = lax.all_gather(routes[0], "expert", axis=0)
    cot_all = lax.all_gather(cotangent[0], "expert", axis=0)

    inputs = own_tokens.astype(F32)
    normed = norm_rows(tokens_all.astype(F32), attn_gain).astype(BF16)
    length = normed.shape[0]
    places = jnp.arange(length, dtype=jnp.int32)
    qkv = dot("td,dm->tm", normed, qkv_w)
    query_pre = qkv[:, :q_cols].reshape(length, heads, head_size)
    key_pre = qkv[:, q_cols : q_cols + k_cols].reshape(length, groups, head_size)
    value_rows = qkv[:, q_cols + k_cols :].astype(BF16).reshape(length, groups, head_size)

    def turn_norm(values, gain_row):
        return rotate(norm_rows(values, gain_row), places.astype(F32))

    query_rot, query_pull = jax.vjp(turn_norm, query_pre, query_gain)
    key_rot, key_pull = jax.vjp(turn_norm, key_pre, key_gain)
    query_low = (
        query_rot.astype(BF16).reshape(length, groups, group_size, head_size).transpose(1, 2, 0, 3)
    )
    key_low = key_rot.astype(BF16).transpose(1, 0, 2)
    value_low = value_rows.transpose(1, 0, 2)
    segment = segment_ids[0]
    allowed = (places[None, :] <= places[:, None]) & (segment[None, :] == segment[:, None])
    score_scale = head_size ** (-0.5)

    def group_scores():
        scores = dot("gjtd,gkd->gjtk", query_low, key_low) * score_scale
        return jnp.where(allowed, scores, -1e30)

    scores = group_scores()
    largest = jnp.max(scores, axis=-1, keepdims=True)
    raised = jnp.exp(scores - largest)
    row_total = jnp.sum(raised, axis=-1, keepdims=True)
    log_total = largest + jnp.log(row_total)
    attended = dot("gjtk,gkd->tgjd", (raised / row_total).astype(BF16), value_low)
    attended_low = attended.astype(BF16).reshape(length, q_cols)
    branch = lax.psum_scatter(
        dot("tm,md->td", attended_low, out_w).astype(BF16), "dp", scatter_dimension=0, tiled=True
    )
    hidden = inputs + branch.astype(F32)

    normed_moe_f, moe_pull = jax.vjp(norm_rows, hidden, moe_gain)
    normed_moe = normed_moe_f.astype(BF16)
    moe_all = lax.all_gather(normed_moe, "expert", axis=0)
    expert_ids = jnp.arange(experts, dtype=jnp.int32)
    mask_all = jnp.any(routes_all[..., None] == expert_ids, axis=2)
    gates_all = masked_softmax(dot("btd,de->bte", moe_all, router_full), mask_all)
    mask_own = lax.dynamic_slice_in_dim(mask_all, peer * owned, owned, axis=2)
    gates_own = lax.dynamic_slice_in_dim(gates_all, peer * owned, owned, axis=2)
    earlier = jnp.tril(jnp.ones((tok_count, tok_count), BF16), -1)
    ranks = dot("ts,bse->bet", earlier, mask_own.astype(BF16)).astype(jnp.int32)
    ranks = jnp.where(mask_own.transpose(0, 2, 1), ranks, -1)
    slots = jnp.arange(CAP, dtype=jnp.int32)
    chosen = ranks[:, :, None, :] == slots[None, None, :, None]
    placed = chosen.astype(BF16).reshape(peers, owned * CAP, tok_count)
    slot_gates = jnp.sum(
        jnp.where(chosen, gates_own.transpose(0, 2, 1)[:, :, None, :], 0.0), axis=-1
    )

    def dispatch(rows):
        taken = dot("bst,btd->bsd", placed, rows).astype(BF16)
        return (
            taken.reshape(peers, owned, CAP, width)
            .transpose(1, 0, 2, 3)
            .reshape(owned, peers * CAP, width)
        )

    def combine(rows):
        spread = (
            rows.reshape(owned, peers, CAP, width)
            .transpose(1, 0, 2, 3)
            .reshape(peers, owned * CAP, width)
        )
        return dot("bst,bsd->btd", placed, spread).astype(BF16)

    row_gates = slot_gates.transpose(1, 0, 2).reshape(owned, peers * CAP, 1)
    cot_rows = dispatch(cot_all)
    arrived = dispatch(moe_all)
    grad_rows = (row_gates * cot_rows.astype(F32)).astype(BF16)
    gate_in = dot("erd,edf->erf", arrived, w_gate)
    up_in = dot("erd,edf->erf", arrived, w_up)
    active_f, act_pull = jax.vjp(activate, gate_in, up_in)
    active = active_f.astype(BF16)
    grad_down_w = dot("erf,erd->efd", active, grad_rows).astype(BF16)
    down_sum = lax.psum(grad_down_w, "dp")
    grad_active = dot("erd,efd->erf", grad_rows, w_down)
    grad_gate_f, grad_up_f = act_pull(grad_active)
    gate_low = grad_gate_f.astype(BF16)
    up_low = grad_up_f.astype(BF16)
    rows_back = dot("erf,edf->erd", gate_low, w_gate) + dot("erf,edf->erd", up_low, w_up)
    back = lax.psum_scatter(
        combine(rows_back.astype(BF16)), "expert", scatter_dimension=0, tiled=True
    )[0]
    result = dot("erf,efd->erd", active, w_down).astype(BF16)
    slot_grads = jnp.sum(cot_rows.astype(F32) * result.astype(F32), axis=-1)
    slot_grads = slot_grads.reshape(owned, peers, CAP).transpose(1, 0, 2)
    token_grads = jnp.sum(jnp.where(chosen, slot_grads[..., None], 0.0), axis=2)
    gate_grads = (
        lax.all_to_all(token_grads, "expert", split_axis=0, concat_axis=0, tiled=True)
        .reshape(experts, tok_count)
        .T
    )
    grad_gate_w = dot("erd,erf->edf", arrived, gate_low).astype(BF16)
    grad_up_w = dot("erd,erf->edf", arrived, up_low).astype(BF16)

    own_gates = lax.dynamic_index_in_dim(gates_all, peer, 0, keepdims=False)
    grad_logits = own_gates * (
        gate_grads - jnp.sum(own_gates * gate_grads, axis=-1, keepdims=True)
    )
    grad_router_w = jnp.einsum("td,te->de", normed_moe.astype(F32), grad_logits, precision=PRECISE)
    grad_normed = back.astype(F32) + jnp.einsum(
        "te,de->td", grad_logits, router_full.astype(F32), precision=PRECISE
    )
    grad_hidden_n, grad_moe_gain = moe_pull(grad_normed)
    grad_hidden = cotangent[0].astype(F32) + grad_hidden_n
    grad_branch = grad_hidden.astype(BF16)
    branch_all = lax.all_gather(grad_branch, "dp", axis=0, tiled=True)
    gate_sum = lax.psum(after(grad_gate_w, branch_all), "dp")

    grad_attended = (
        dot("td,md->tm", branch_all, out_w)
        .astype(BF16)
        .reshape(length, groups, group_size, head_size)
        .transpose(1, 2, 0, 3)
    )
    weights = jnp.exp(group_scores() - log_total)
    grad_weights = dot("gjtd,gkd->gjtk", grad_attended, value_low)
    grad_values = dot("gjtk,gjtd->kgd", weights.astype(BF16), grad_attended)
    inner_sum = jnp.sum(weights * grad_weights, axis=-1, keepdims=True)
    grad_scores = (weights * (grad_weights - inner_sum)).astype(BF16)
    grad_queries = dot("gjtk,gkd->tgjd", grad_scores, key_low) * score_scale
    grad_keys = dot("gjtk,gjtd->kgd", grad_scores, query_low) * score_scale
    grad_queries = grad_queries.reshape(length, heads, head_size)
    query_pre_grad, grad_query_gain = query_pull(grad_queries.astype(BF16).astype(F32))
    key_pre_grad, grad_key_gain = key_pull(grad_keys.astype(BF16).astype(F32))
    qkv_grad = jnp.concatenate(
        [
            query_pre_grad.reshape(length, -1).astype(BF16),
            key_pre_grad.reshape(length, -1).astype(BF16),
            grad_values.reshape(length, -1).astype(BF16),
        ],
        axis=1,
    )
    grad_normed_attn = lax.psum_scatter(
        dot("tm,dm->td", qkv_grad, qkv_w).astype(BF16), "dp", scatter_dimension=0, tiled=True
    ).astype(F32)
    up_sum = lax.psum(after(grad_up_w, grad_normed_attn), "dp")
    _, attn_pull = jax.vjp(norm_rows, inputs, attn_gain)
    grad_inputs_n, grad_attn_gain = attn_pull(grad_normed_attn)
    grad_tokens = grad_hidden + grad_inputs_n

    band_qkv = dot("td,tm->dm", normed, qkv_grad).astype(BF16)
    band_qkv = band_qkv.reshape(bands, peers, band_rows, qkv_cols).transpose(1, 0, 2, 3)
    band_qkv = lax.psum_scatter(
        band_qkv.reshape(width, qkv_cols), "expert", scatter_dimension=0, tiled=True
    ).reshape(bands, band_rows, qkv_cols)
    band_qkv = lax.all_to_all(band_qkv, "dp", split_axis=0, concat_axis=0, tiled=True).transpose(
        1, 0, 2
    )
    grad_query = band_qkv[:, :, :q_cols].astype(F32).reshape(band_rows, -1)
    grad_key = band_qkv[:, :, q_cols : q_cols + k_cols].astype(F32).reshape(band_rows, -1)
    grad_value = band_qkv[:, :, q_cols + k_cols :].astype(F32).reshape(band_rows, -1)
    grad_output = lax.psum_scatter(
        dot("tm,td->md", attended_low, branch_all).astype(BF16),
        "expert",
        scatter_dimension=0,
        tiled=True,
    ).astype(F32)
    smaller = jnp.concatenate(
        [
            grad_router_w.reshape(bands * peers, -1),
            grad_attn_gain.reshape(bands * peers, -1),
            grad_moe_gain.reshape(bands * peers, -1),
            grad_query_gain.reshape(bands * peers, -1),
            grad_key_gain.reshape(bands * peers, -1),
        ],
        axis=1,
    )
    smaller = lax.psum_scatter(smaller, ("dp", "expert"), scatter_dimension=0, tiled=True)[0]
    cuts = [band_rows * experts, band_rows, band_rows, gain_rows]
    ends = [sum(cuts[: i + 1]) for i in range(4)]
    grad_router, grad_attn, grad_moe, grad_gq, grad_gk = jnp.split(smaller, ends)

    moe_sum = lax.psum_scatter(
        combine((row_gates * result.astype(F32)).astype(BF16)),
        "expert",
        scatter_dimension=0,
        tiled=True,
    )[0]
    block_out = (hidden + moe_sum.astype(F32)).astype(BF16)
    return (
        block_out[None],
        grad_tokens[None],
        grad_query,
        grad_key,
        grad_value,
        grad_output,
        grad_router.reshape(band_rows, experts),
        grad_attn,
        grad_moe,
        grad_gq,
        grad_gk,
        gate_sum.astype(F32),
        up_sum.astype(F32),
        down_sum.astype(F32),
    )


def solution(mesh):
    both = ("dp", "expert")
    return jax.shard_map(
        on_device,
        mesh=mesh,
        in_specs=(
            P("expert", "dp", None),
            P("expert", None),
            P("expert", "dp", None),
            P(both, None),
            P(both, None),
            P(both, None),
            P(both, None),
            P(both, None),
            P(both),
            P(both),
            P(both),
            P(both),
            P("expert", None, None),
            P("expert", None, None),
            P("expert", None, None),
            P("expert", "dp", None),
        ),
        out_specs=(
            P("expert", "dp", None),
            P("expert", "dp", None),
            P(both, None),
            P(both, None),
            P(both, None),
            P(both, None),
            P(both, None),
            P(both),
            P(both),
            P(both),
            P(both),
            P("expert", None, None),
            P("expert", None, None),
            P("expert", None, None),
        ),
        check_vma=False,
    )
```

```python
import jax
import jax.numpy as jnp
from jax import lax
from jax.experimental import pallas as pl
from jax.sharding import PartitionSpec as P

CAP = 80
HEAD_PARTS = 4


EPSILON = 1e-06
ROPE_BASE = 1000000.0
PRECISE = lax.Precision.HIGHEST
F32 = jnp.float32
BF16 = jnp.bfloat16


def norm_rows(values, gain_row):
    return (
        values * lax.rsqrt(jnp.mean(values * values, axis=-1, keepdims=True) + EPSILON) * gain_row
    )


def rotate(values, places):
    half_size = values.shape[-1] // 2
    frequency = ROPE_BASE ** (-jnp.arange(half_size, dtype=F32) * 2.0 / values.shape[-1])
    angles = places[:, None] * frequency[None, :]
    angles = jnp.concatenate([angles, angles], axis=-1)[:, None, :]
    turned = jnp.concatenate([-values[..., half_size:], values[..., :half_size]], axis=-1)
    return values * jnp.cos(angles) + turned * jnp.sin(angles)


def activate(gate_vals, up_vals):
    return gate_vals * jax.nn.sigmoid(gate_vals) * up_vals


def masked_softmax(logits, mask):
    kept = jnp.where(mask, logits, -jnp.inf)
    largest = jnp.max(kept, axis=-1, keepdims=True)
    raised = jnp.where(mask, jnp.exp(logits - largest), 0.0)
    return raised / jnp.sum(raised, axis=-1, keepdims=True)


def nothing(*refs):
    del refs


def after(value, *others):
    anywhere = pl.BlockSpec(memory_space=pl.ANY)
    return pl.pallas_call(
        nothing,
        out_shape=jax.ShapeDtypeStruct(value.shape, value.dtype),
        in_specs=[anywhere] * (1 + len(others)),
        out_specs=anywhere,
        input_output_aliases={0: 0},
    )(value, *others)


def shifted(value, axis, step):
    count = lax.axis_size(axis)
    return lax.ppermute(value, axis, [(i, (i + step) % count) for i in range(count)])


def gather_blocks(own, axis):
    count, me = lax.axis_size(axis), lax.axis_index(axis)
    whole = jnp.zeros((count, *own.shape), own.dtype)
    whole = lax.dynamic_update_index_in_dim(whole, own, me, 0)
    for step in range(1, count):
        source = lax.rem(me - step + count, count)
        whole = lax.dynamic_update_index_in_dim(whole, shifted(own, axis, step), source, 0)
    return whole


def sum_blocks(blocks, axis):
    count, me = lax.axis_size(axis), lax.axis_index(axis)
    total = lax.dynamic_index_in_dim(blocks, me, 0, keepdims=False).astype(F32)
    for step in range(1, count):
        target = lax.rem(me + step, count)
        sent = lax.dynamic_index_in_dim(blocks, target, 0, keepdims=False)
        total = total + shifted(sent, axis, step).astype(F32)
    return total


def sum_peers(blocks):
    count, me = lax.axis_size("expert"), lax.axis_index("expert")
    core, chip, chips = lax.rem(me, 2), lax.div(me, 2), count // 2
    paired = blocks.reshape(chips, 2, *blocks.shape[1:])
    sent = lax.dynamic_index_in_dim(paired, 1 - core, 1, keepdims=False)
    kept = lax.dynamic_index_in_dim(paired, core, 1, keepdims=False)
    got = lax.ppermute(sent, "expert", [(i, i ^ 1) for i in range(count)])
    halves = (kept.astype(F32) + got.astype(F32)).astype(BF16)
    total = lax.dynamic_index_in_dim(halves, chip, 0, keepdims=False).astype(F32)
    for step in range(1, chips):
        sent = lax.dynamic_index_in_dim(halves, lax.rem(chip + step, chips), 0, keepdims=False)
        total = total + shifted(sent, "expert", 2 * step).astype(F32)
    return total


def dot(spec, left, right):
    return jnp.einsum(spec, left, right, preferred_element_type=F32)


def on_device(
    tokens,
    segment_ids,
    routes,
    w_query,
    w_key,
    w_value,
    w_output,
    w_router,
    gain_attn,
    gain_moe,
    gain_query,
    gain_key,
    w_gate,
    w_up,
    w_down,
    cotangent,
):
    bands, peers = lax.axis_size("dp"), lax.axis_size("expert")
    band, peer = lax.axis_index("dp"), lax.axis_index("expert")
    own_tokens = tokens[0]
    tok_count, width = own_tokens.shape
    band_rows = w_query.shape[0]
    experts = w_router.shape[1]
    gain_rows = gain_query.shape[0]
    head_size = gain_rows * bands * peers
    heads = w_query.shape[1] // head_size // bands
    groups = w_key.shape[1] // head_size // bands
    group_size = heads // groups
    q_cols, k_cols = heads * head_size, groups * head_size
    qkv_cols = q_cols + 2 * k_cols
    owned = experts // peers

    tokens_all = lax.all_gather(own_tokens, "dp", axis=0, tiled=True)
    small = jnp.concatenate(
        [
            w_router,
            gain_attn[:, None],
            gain_moe[:, None],
            jnp.pad(gain_query, (0, band_rows - gain_rows))[:, None],
            jnp.pad(gain_key, (0, band_rows - gain_rows))[:, None],
        ],
        axis=1,
    )
    small = jnp.pad(small, ((0, 0), (0, 128 - small.shape[1])))
    packed = jnp.concatenate(
        [
            w_query.reshape(band_rows, bands, q_cols),
            w_key.reshape(band_rows, bands, k_cols),
            w_value.reshape(band_rows, bands, k_cols),
            jnp.broadcast_to(small[:, None], (band_rows, bands, 128)),
        ],
        axis=-1,
    ).transpose(1, 0, 2)
    swapped = lax.all_to_all(packed, "dp", split_axis=0, concat_axis=0, tiled=True)
    packed_all = lax.all_gather(swapped, "expert", axis=1, tiled=True).reshape(width, -1)
    qkv_w = packed_all[:, :qkv_cols]
    small_all = packed_all[:, qkv_cols:]
    router_full = small_all[:, :experts]
    attn_gain = small_all[:, experts].astype(F32)
    moe_gain = small_all[:, experts + 1].astype(F32)
    head_gains = small_all.reshape(bands * peers, band_rows, 128)[:, :gain_rows]
    query_gain = head_gains[:, :, experts + 2].reshape(-1).astype(F32)
    key_gain = head_gains[:, :, experts + 3].reshape(-1).astype(F32)
    out_w = lax.all_gather(w_output, "expert", axis=0, tiled=True)
    routes_all = lax.all_gather(routes[0], "expert", axis=0)
    cot_all = lax.all_gather(cotangent[0], "expert", axis=0)

    inputs = own_tokens.astype(F32)
    normed = norm_rows(tokens_all.astype(F32), attn_gain).astype(BF16)
    length = normed.shape[0]
    places = jnp.arange(length, dtype=jnp.int32)
    qkv = dot("td,dm->tm", normed, qkv_w)
    query_pre = qkv[:, :q_cols].reshape(length, heads, head_size)
    key_pre = qkv[:, q_cols : q_cols + k_cols].reshape(length, groups, head_size)
    value_rows = qkv[:, q_cols + k_cols :].astype(BF16).reshape(length, groups, head_size)

    def turn_norm(values, gain_row):
        return rotate(norm_rows(values, gain_row), places.astype(F32))

    query_rot, query_pull = jax.vjp(turn_norm, query_pre, query_gain)
    key_rot, key_pull = jax.vjp(turn_norm, key_pre, key_gain)
    query_low = (
        query_rot.astype(BF16).reshape(length, groups, group_size, head_size).transpose(1, 2, 0, 3)
    )
    key_low = key_rot.astype(BF16).transpose(1, 0, 2)
    value_low = value_rows.transpose(1, 0, 2)
    segment = segment_ids[0]
    allowed = (places[None, :] <= places[:, None]) & (segment[None, :] == segment[:, None])
    score_scale = head_size ** (-0.5)

    def group_scores(queries):
        scores = dot("gjtd,gkd->gjtk", queries, key_low) * score_scale
        return jnp.where(allowed, scores, -1e30)

    scores = group_scores(query_low)
    largest = jnp.max(scores, axis=-1, keepdims=True)
    raised = jnp.exp(scores - largest)
    row_total = jnp.sum(raised, axis=-1, keepdims=True)
    log_total = largest + jnp.log(row_total)
    attended = dot("gjtk,gkd->tgjd", (raised / row_total).astype(BF16), value_low)
    attended_low = attended.astype(BF16).reshape(length, q_cols)
    branch = lax.psum_scatter(
        after(dot("tm,md->td", attended_low, out_w).astype(BF16), cot_all, routes_all),
        "dp",
        scatter_dimension=0,
        tiled=True,
    )
    hidden = inputs + branch.astype(F32)

    normed_moe_f, moe_pull = jax.vjp(norm_rows, hidden, moe_gain)
    normed_moe = normed_moe_f.astype(BF16)
    moe_all = lax.all_gather(normed_moe, "expert", axis=0)
    expert_ids = jnp.arange(experts, dtype=jnp.int32)
    mask_all = jnp.any(routes_all[..., None] == expert_ids, axis=2)
    gates_all = masked_softmax(dot("btd,de->bte", moe_all, router_full), mask_all)
    mask_own = lax.dynamic_slice_in_dim(mask_all, peer * owned, owned, axis=2)
    gates_own = lax.dynamic_slice_in_dim(gates_all, peer * owned, owned, axis=2)
    earlier = jnp.tril(jnp.ones((tok_count, tok_count), BF16), -1)
    ranks = dot("ts,bse->bet", earlier, mask_own.astype(BF16)).astype(jnp.int32)
    ranks = jnp.where(mask_own.transpose(0, 2, 1), ranks, -1)
    slots = jnp.arange(CAP, dtype=jnp.int32)
    chosen = ranks[:, :, None, :] == slots[None, None, :, None]
    placed = chosen.astype(BF16).reshape(peers, owned * CAP, tok_count)
    slot_gates = jnp.sum(
        jnp.where(chosen, gates_own.transpose(0, 2, 1)[:, :, None, :], 0.0), axis=-1
    )

    def dispatch(rows):
        taken = dot("bst,btd->bsd", placed, rows).astype(BF16)
        return (
            taken.reshape(peers, owned, CAP, width)
            .transpose(1, 0, 2, 3)
            .reshape(owned, peers * CAP, width)
        )

    def combine(rows):
        spread = (
            rows.reshape(owned, peers, CAP, width)
            .transpose(1, 0, 2, 3)
            .reshape(peers, owned * CAP, width)
        )
        return dot("bst,bsd->btd", placed, spread).astype(BF16)

    row_gates = slot_gates.transpose(1, 0, 2).reshape(owned, peers * CAP, 1)
    cot_rows = dispatch(cot_all)
    arrived = dispatch(moe_all)
    grad_rows = (row_gates * cot_rows.astype(F32)).astype(BF16)
    gate_in = dot("erd,edf->erf", arrived, w_gate)
    up_in = dot("erd,edf->erf", arrived, w_up)
    active_f, act_pull = jax.vjp(activate, gate_in, up_in)
    active = active_f.astype(BF16)
    grad_down_w = dot("erf,erd->efd", active, grad_rows).astype(BF16)
    grad_active = dot("erd,efd->erf", grad_rows, w_down)
    grad_gate_f, grad_up_f = act_pull(grad_active)
    gate_low = grad_gate_f.astype(BF16)
    up_low = grad_up_f.astype(BF16)
    grad_gate_w = dot("erd,erf->edf", arrived, gate_low).astype(BF16)
    grad_up_w = dot("erd,erf->edf", arrived, up_low).astype(BF16)
    expert_sums = lax.psum((grad_gate_w, grad_up_w, grad_down_w), "dp")
    gate_low = after(gate_low, grad_gate_w, grad_up_w, grad_down_w)
    rows_back = dot("erf,edf->erd", gate_low, w_gate) + dot("erf,edf->erd", up_low, w_up)
    back = sum_peers(combine(rows_back.astype(BF16)))
    result = dot("erf,efd->erd", after(active, gate_low), w_down).astype(BF16)
    slot_grads = jnp.sum(cot_rows.astype(F32) * result.astype(F32), axis=-1)
    slot_grads = slot_grads.reshape(owned, peers, CAP).transpose(1, 0, 2)
    token_grads = jnp.sum(jnp.where(chosen, slot_grads[..., None], 0.0), axis=2)
    gate_grads = (
        lax.all_to_all(token_grads, "expert", split_axis=0, concat_axis=0, tiled=True)
        .reshape(experts, tok_count)
        .T
    )

    own_gates = lax.dynamic_index_in_dim(gates_all, peer, 0, keepdims=False)
    grad_logits = own_gates * (
        gate_grads - jnp.sum(own_gates * gate_grads, axis=-1, keepdims=True)
    )
    grad_router_w = jnp.einsum("td,te->de", normed_moe.astype(F32), grad_logits, precision=PRECISE)
    grad_normed = back + jnp.einsum(
        "te,de->td", grad_logits, router_full.astype(F32), precision=PRECISE
    )
    grad_hidden_n, grad_moe_gain = moe_pull(grad_normed)
    grad_hidden = cotangent[0].astype(F32) + grad_hidden_n
    grad_branch = grad_hidden.astype(BF16)
    branch_all = gather_blocks(grad_branch, "dp").reshape(length, width)

    grad_attended = (
        dot("td,md->tm", branch_all, out_w)
        .astype(BF16)
        .reshape(length, groups, group_size, head_size)
        .transpose(1, 2, 0, 3)
    )

    def backward_part(pieces):
        query_part, grad_part, log_part = pieces
        weights = jnp.exp(group_scores(query_part) - log_part)
        grad_weights = dot("gjtd,gkd->gjtk", grad_part, value_low)
        grad_values = dot("gjtk,gjtd->kgd", weights.astype(BF16), grad_part)
        inner_sum = jnp.sum(weights * grad_weights, axis=-1, keepdims=True)
        grad_scores = (weights * (grad_weights - inner_sum)).astype(BF16)
        grad_queries = dot("gjtk,gkd->gjtd", grad_scores, key_low) * score_scale
        grad_keys = dot("gjtk,gjtd->kgd", grad_scores, query_part) * score_scale
        return grad_queries, grad_keys, grad_values

    def parts_of(values):
        cut = values.reshape(groups, HEAD_PARTS, -1, *values.shape[2:])
        return jnp.moveaxis(cut, 1, 0)

    grad_queries, grad_keys, grad_values = lax.map(
        backward_part, (parts_of(query_low), parts_of(grad_attended), parts_of(log_total))
    )
    grad_queries = grad_queries.transpose(3, 1, 0, 2, 4)
    grad_keys, grad_values = jnp.sum(grad_keys, axis=0), jnp.sum(grad_values, axis=0)
    grad_queries = grad_queries.reshape(length, heads, head_size)
    query_pre_grad, grad_query_gain = query_pull(grad_queries.astype(BF16).astype(F32))
    key_pre_grad, grad_key_gain = key_pull(grad_keys.astype(BF16).astype(F32))
    qkv_grad = jnp.concatenate(
        [
            query_pre_grad.reshape(length, -1).astype(BF16),
            key_pre_grad.reshape(length, -1).astype(BF16),
            grad_values.reshape(length, -1).astype(BF16),
        ],
        axis=1,
    )
    grad_normed_attn = sum_blocks(
        dot("tm,dm->td", qkv_grad, qkv_w).astype(BF16).reshape(bands, tok_count, width), "dp"
    )
    _, attn_pull = jax.vjp(norm_rows, inputs, attn_gain)
    grad_inputs_n, grad_attn_gain = attn_pull(grad_normed_attn)
    grad_tokens = grad_hidden + grad_inputs_n

    whole_gains = jnp.stack([grad_attn_gain, grad_moe_gain], axis=1)
    head_gains = jnp.stack([grad_query_gain, grad_key_gain], axis=1)
    head_gains = jnp.pad(
        head_gains.reshape(bands * peers, gain_rows, 2),
        ((0, 0), (0, band_rows - gain_rows), (0, 0)),
    )
    small_grad = jnp.concatenate(
        [grad_router_w, whole_gains, head_gains.reshape(width, 2)], axis=1
    )
    small_grad = jnp.pad(small_grad, ((0, 0), (0, 128 - small_grad.shape[1])))
    band_qkv = jnp.concatenate([dot("td,tm->dm", normed, qkv_grad), small_grad], axis=1)
    band_qkv = band_qkv.astype(BF16).reshape(bands, peers, band_rows, -1).transpose(1, 0, 2, 3)
    band_qkv = sum_peers(band_qkv).astype(BF16)
    band_qkv = lax.all_to_all(band_qkv, "dp", split_axis=0, concat_axis=0, tiled=True).transpose(
        1, 0, 2
    )
    grad_query = band_qkv[:, :, :q_cols].astype(F32).reshape(band_rows, -1)
    grad_key = band_qkv[:, :, q_cols : q_cols + k_cols].astype(F32).reshape(band_rows, -1)
    grad_value = band_qkv[:, :, q_cols + k_cols : qkv_cols].astype(F32).reshape(band_rows, -1)
    smaller = jnp.sum(band_qkv[:, :, qkv_cols:].astype(F32), axis=1)
    grad_output = sum_peers(
        dot("tm,td->md", attended_low, branch_all).astype(BF16).reshape(peers, -1, width)
    )

    moe_sum = sum_peers(combine((row_gates * result.astype(F32)).astype(BF16)))
    block_out = (hidden + moe_sum).astype(BF16)
    return (
        block_out[None],
        grad_tokens[None],
        grad_query,
        grad_key,
        grad_value,
        grad_output,
        smaller[:, :experts],
        smaller[:, experts],
        smaller[:, experts + 1],
        smaller[:gain_rows, experts + 2],
        smaller[:gain_rows, experts + 3],
        expert_sums[0].astype(F32),
        expert_sums[1].astype(F32),
        expert_sums[2].astype(F32),
    )


def solution(mesh):
    both = ("dp", "expert")
    return jax.shard_map(
        on_device,
        mesh=mesh,
        in_specs=(
            P("expert", "dp", None),
            P("expert", None),
            P("expert", "dp", None),
            P(both, None),
            P(both, None),
            P(both, None),
            P(both, None),
            P(both, None),
            P(both),
            P(both),
            P(both),
            P(both),
            P("expert", None, None),
            P("expert", None, None),
            P("expert", None, None),
            P("expert", "dp", None),
        ),
        out_specs=(
            P("expert", "dp", None),
            P("expert", "dp", None),
            P(both, None),
            P(both, None),
            P(both, None),
            P(both, None),
            P(both, None),
            P(both),
            P(both),
            P(both),
            P(both),
            P("expert", None, None),
            P("expert", None, None),
            P("expert", None, None),
        ),
        check_vma=False,
    )
```

```python
import jax
import jax.numpy as jnp
from jax import lax
from jax.experimental import pallas as pl
from jax.experimental.pallas import tpu as pltpu
from jax.sharding import PartitionSpec as P

CAP = 80
Q_BLOCK = 256
HIDDEN_TILE = 256
ROW_TILE = 256
WIDTH_TILE = 512
ROW_PARTS = 2
VMEM_BYTES = 60 << 20


EPSILON = 1e-06
ROPE_BASE = 1000000.0
PRECISE = lax.Precision.HIGHEST
F32 = jnp.float32
BF16 = jnp.bfloat16


def norm_rows(values, gain_row):
    return (
        values * lax.rsqrt(jnp.mean(values * values, axis=-1, keepdims=True) + EPSILON) * gain_row
    )


def activate(gate_vals, up_vals):
    return gate_vals * jax.nn.sigmoid(gate_vals) * up_vals


def masked_softmax(logits, mask):
    kept = jnp.where(mask, logits, -jnp.inf)
    largest = jnp.max(kept, axis=-1, keepdims=True)
    raised = jnp.where(mask, jnp.exp(logits - largest), 0.0)
    return raised / jnp.sum(raised, axis=-1, keepdims=True)


def nothing(*refs):
    del refs


def after(value, *others):
    anywhere = pl.BlockSpec(memory_space=pl.ANY)
    return pl.pallas_call(
        nothing,
        out_shape=jax.ShapeDtypeStruct(value.shape, value.dtype),
        in_specs=[anywhere] * (1 + len(others)),
        out_specs=anywhere,
        input_output_aliases={0: 0},
    )(value, *others)


def shifted(value, axis, step):
    count = lax.axis_size(axis)
    return lax.ppermute(value, axis, [(i, (i + step) % count) for i in range(count)])


def gather_blocks(own, axis):
    count, me = lax.axis_size(axis), lax.axis_index(axis)
    whole = jnp.zeros((count, *own.shape), own.dtype)
    whole = lax.dynamic_update_index_in_dim(whole, own, me, 0)
    for step in range(1, count):
        source = lax.rem(me - step + count, count)
        whole = lax.dynamic_update_index_in_dim(whole, shifted(own, axis, step), source, 0)
    return whole


def sum_blocks(blocks, axis):
    count, me = lax.axis_size(axis), lax.axis_index(axis)
    total = lax.dynamic_index_in_dim(blocks, me, 0, keepdims=False).astype(F32)
    for step in range(1, count):
        target = lax.rem(me + step, count)
        sent = lax.dynamic_index_in_dim(blocks, target, 0, keepdims=False)
        total = total + shifted(sent, axis, step).astype(F32)
    return total


def sum_peers(blocks):
    count, me = lax.axis_size("expert"), lax.axis_index("expert")
    core, chip, chips = lax.rem(me, 2), lax.div(me, 2), count // 2
    paired = blocks.reshape(chips, 2, *blocks.shape[1:])
    sent = lax.dynamic_index_in_dim(paired, 1 - core, 1, keepdims=False)
    kept = lax.dynamic_index_in_dim(paired, core, 1, keepdims=False)
    got = lax.ppermute(sent, "expert", [(i, i ^ 1) for i in range(count)])
    halves = (kept.astype(F32) + got.astype(F32)).astype(BF16)
    total = lax.dynamic_index_in_dim(halves, chip, 0, keepdims=False).astype(F32)
    for step in range(1, chips):
        sent = lax.dynamic_index_in_dim(halves, lax.rem(chip + step, chips), 0, keepdims=False)
        total = total + shifted(sent, "expert", 2 * step).astype(F32)
    return total


def dot(spec, left, right):
    return jnp.einsum(spec, left, right, preferred_element_type=F32)


def swapped_columns(own):
    peers, peer, bands = lax.axis_size("expert"), lax.axis_index("expert"), lax.axis_size("dp")
    mine = by_core(own, lax.rem(peer, 2))
    pieces = []
    for step in range(1, bands):
        got = lax.ppermute(mine, "dp", [(i, i ^ step) for i in range(bands)])
        twin = lax.ppermute(got, "expert", [(i, i ^ 1) for i in range(peers)])
        pieces += [got, twin]
    return pieces


def by_core(values, core):
    paired = values.reshape(-1, 2, *values.shape[1:])
    return lax.dynamic_index_in_dim(paired, core, 1, keepdims=False)


def place_kernel(rank_ref, block_ref, *rest):
    rows_ref = rest[-1]
    owned, tok_count = rank_ref.shape[1:]
    slots = lax.broadcasted_iota(jnp.int32, (CAP, tok_count), 0)
    ranks = rank_ref[0]
    hot = jnp.concatenate([ranks[e : e + 1] == slots for e in range(owned)], axis=0)
    hot = jnp.where(hot, 1.0, 0.0).astype(BF16)
    width = block_ref.shape[-1]
    for start in range(0, width, WIDTH_TILE):
        cols = slice(start, start + WIDTH_TILE)
        rows = jnp.dot(hot, block_ref[0, :, cols], preferred_element_type=F32).astype(BF16)
        rows_ref[:, 0, :, cols] = rows.reshape(owned, CAP, WIDTH_TILE)


def place_rows(ranks, blocks, start, total, buffer=None):
    count, owned, tok_count = ranks.shape
    width = blocks.shape[-1]
    in_specs = [
        pl.BlockSpec((1, owned, tok_count), lambda b: (b, 0, 0)),
        pl.BlockSpec((1, tok_count, width), lambda b: (b, 0, 0)),
    ]
    given = (ranks, blocks)
    if buffer is not None:
        in_specs.append(pl.BlockSpec(memory_space=pl.ANY))
        given += (buffer,)
    return pl.pallas_call(
        place_kernel,
        grid=(count,),
        out_shape=jax.ShapeDtypeStruct((owned, total, CAP, width), BF16),
        in_specs=in_specs,
        out_specs=pl.BlockSpec((owned, 1, CAP, width), lambda b: (0, start + b, 0, 0)),
        input_output_aliases={} if buffer is None else {2: 0},
        compiler_params=pltpu.CompilerParams(vmem_limit_bytes=VMEM_BYTES),
        cost_estimate=pl.CostEstimate(
            flops=2 * count * owned * CAP * tok_count * width,
            bytes_accessed=2 * count * (tok_count + owned * CAP) * width,
            transcendentals=0,
        ),
    )(*given)


def place_all(ranks, pieces, buffer=None, start=0):
    total = ranks.shape[0]
    for piece in pieces:
        count = piece.shape[0]
        buffer = place_rows(ranks[start : start + count], piece, start, total, buffer)
        start += count
    return buffer


def dot_nt(left, right):
    return lax.dot_general(left, right, (((1,), (1,)), ((), ())), preferred_element_type=F32)


def grads_kernel(x_ref, c_ref, g_ref, wg_ref, wu_ref, wd_ref, *rest):
    dg_ref, du_ref, dd_ref, sums, pair, active, turned = rest[-7:]
    tile = HIDDEN_TILE
    rows, width = x_ref.shape[1:]
    step = pl.program_id(1)
    same = lax.broadcasted_iota(jnp.int32, (tile, tile), 0) == lax.broadcasted_iota(
        jnp.int32, (tile, tile), 1
    )
    same = jnp.where(same, 1.0, 0.0).astype(BF16)

    @pl.when(step == 0)
    def _():
        @pl.loop(0, width // tile)
        def _(c):
            cols = pl.ds(pl.multiple_of(c * tile, tile), tile)
            turned[:tile, cols] = dot_nt(same, wg_ref[0, cols, :]).astype(BF16)
            turned[tile:, cols] = dot_nt(same, wu_ref[0, cols, :]).astype(BF16)

    @pl.loop(0, rows // ROW_TILE)
    def _(r):
        part = pl.ds(pl.multiple_of(r * ROW_TILE, ROW_TILE), ROW_TILE)
        ins = dot_nt(turned[...], x_ref[0, part, :])
        raw = dot_nt(wd_ref[0], c_ref[0, part, :])
        gates = g_ref[0, :, part]
        gate_in, up_in = ins[:tile], ins[tile:]
        sig = 1.0 / (1.0 + jnp.exp(-gate_in))
        silu = gate_in * sig
        grad = raw * gates
        active[:, part] = (silu * up_in * gates).astype(BF16)
        pair[:tile, part] = (grad * up_in * (sig + silu * (1.0 - sig))).astype(BF16)
        pair[tile:, part] = (grad * silu).astype(BF16)

    @pl.loop(0, width // WIDTH_TILE)
    def _(c):
        cols = pl.ds(pl.multiple_of(c * WIDTH_TILE, WIDTH_TILE), WIDTH_TILE)
        grads = jnp.dot(pair[...], x_ref[0, :, cols], preferred_element_type=F32)
        sums[:, cols] = jnp.where(step == 0, grads, sums[:, cols] + grads)
        grads = jnp.dot(active[...], c_ref[0, :, cols], preferred_element_type=F32)
        dd_ref[0, :, cols] = jnp.where(step == 0, grads, dd_ref[0, :, cols] + grads)

    @pl.when(step == pl.num_programs(1) - 1)
    def _():
        @pl.loop(0, width // tile)
        def _(c):
            cols = pl.ds(pl.multiple_of(c * tile, tile), tile)
            dg_ref[0, cols, :] = dot_nt(same, sums[:tile, cols].astype(BF16))
            du_ref[0, cols, :] = dot_nt(same, sums[tile:, cols].astype(BF16))


def expert_grads(x_rows, c_rows, gates, w_gate, w_up, w_down, expert, buffers=None):
    owned, rows, width = x_rows.shape
    hidden = w_down.shape[1]
    tile, parts = HIDDEN_TILE, ROW_PARTS
    part = rows // parts
    whole = pl.BlockSpec(memory_space=pl.ANY)
    shapes = [(owned, width, hidden)] * 2 + [(owned, hidden, width)]
    in_specs = [
        pl.BlockSpec((1, part, width), lambda f, r: (expert, r, 0)),
        pl.BlockSpec((1, part, width), lambda f, r: (expert, r, 0)),
        pl.BlockSpec((1, 1, part), lambda f, r: (expert, 0, r)),
        pl.BlockSpec((1, width, tile), lambda f, r: (expert, 0, f)),
        pl.BlockSpec((1, width, tile), lambda f, r: (expert, 0, f)),
        pl.BlockSpec((1, tile, width), lambda f, r: (expert, f, 0)),
    ]
    given = (x_rows, c_rows, gates, w_gate, w_up, w_down)
    if buffers is not None:
        in_specs += [whole] * 3
        given += tuple(buffers)
    return pl.pallas_call(
        grads_kernel,
        grid=(hidden // tile, parts),
        out_shape=[jax.ShapeDtypeStruct(shape, F32) for shape in shapes],
        in_specs=in_specs,
        out_specs=[
            pl.BlockSpec((1, width, tile), lambda f, r: (expert, 0, f)),
            pl.BlockSpec((1, width, tile), lambda f, r: (expert, 0, f)),
            pl.BlockSpec((1, tile, width), lambda f, r: (expert, f, 0)),
        ],
        scratch_shapes=[
            pltpu.VMEM((2 * tile, width), F32),
            pltpu.VMEM((2 * tile, part), BF16),
            pltpu.VMEM((tile, part), BF16),
            pltpu.VMEM((2 * tile, width), BF16),
        ],
        input_output_aliases={} if buffers is None else {6: 0, 7: 1, 8: 2},
        compiler_params=pltpu.CompilerParams(vmem_limit_bytes=VMEM_BYTES),
        cost_estimate=pl.CostEstimate(
            flops=12 * rows * width * hidden,
            bytes_accessed=12 * rows * width + 24 * width * hidden,
            transcendentals=rows * hidden,
        ),
    )(*given)


def turn(values, cos, sin):
    return values * cos + pltpu.roll(values, values.shape[-1] // 2, 1) * sin


def qkv_kernel(
    tok_ref,
    gain_ref,
    w_ref,
    cos_ref,
    sin_ref,
    gq_ref,
    gk_ref,
    normed_ref,
    qpre_ref,
    kpre_ref,
    qrot_ref,
    krot_ref,
    value_ref,
):
    head = cos_ref.shape[1]
    heads = qpre_ref.shape[1] // head
    normed = norm_rows(tok_ref[...].astype(F32), gain_ref[...]).astype(BF16)
    normed_ref[...] = normed
    cos, sin = cos_ref[...], sin_ref[...]
    for pair in range(0, heads, 2):
        cols = slice(pair * head, (pair + 2) * head)
        pre = jnp.dot(normed, w_ref[:, cols], preferred_element_type=F32)
        qpre_ref[:, cols] = pre
        for h in range(2):
            one = slice(h * head, (h + 1) * head)
            rot = turn(norm_rows(pre[:, one], gq_ref[...]), cos, sin)
            qrot_ref[:, (pair + h) * head : (pair + h + 1) * head] = rot.astype(BF16)
    pre = jnp.dot(normed, w_ref[:, heads * head :], preferred_element_type=F32)
    kpre_ref[...] = pre[:, :head]
    krot_ref[...] = turn(norm_rows(pre[:, :head], gk_ref[...]), cos, sin).astype(BF16)
    value_ref[...] = pre[:, head:].astype(BF16)


def make_qkv(tokens, gain, weight, cos, sin, query_gain, key_gain):
    length, width = tokens.shape
    head = cos.shape[1]
    cols = weight.shape[1]
    q_cols = cols - 2 * head
    block = Q_BLOCK

    def rows(size):
        return pl.BlockSpec((block, size), lambda i: (i, 0))

    def fixed(*shape):
        return pl.BlockSpec(shape, lambda i: (0, 0))

    return pl.pallas_call(
        qkv_kernel,
        grid=(length // block,),
        in_specs=[
            rows(width),
            fixed(1, width),
            fixed(width, cols),
            rows(head),
            rows(head),
            fixed(1, head),
            fixed(1, head),
        ],
        out_specs=[rows(width), rows(q_cols), rows(head), rows(q_cols), rows(head), rows(head)],
        out_shape=[
            jax.ShapeDtypeStruct((length, width), BF16),
            jax.ShapeDtypeStruct((length, q_cols), F32),
            jax.ShapeDtypeStruct((length, head), F32),
            jax.ShapeDtypeStruct((length, q_cols), BF16),
            jax.ShapeDtypeStruct((length, head), BF16),
            jax.ShapeDtypeStruct((length, head), BF16),
        ],
        compiler_params=pltpu.CompilerParams(vmem_limit_bytes=VMEM_BYTES),
        cost_estimate=pl.CostEstimate(
            flops=2 * length * width * cols,
            bytes_accessed=2 * width * cols + 8 * length * width,
            transcendentals=0,
        ),
    )(tokens, gain[None], weight, cos, sin, query_gain[None], key_gain[None])


def masked_scores(q_ref, k_ref, seg_row_ref, seg_col_ref, block, keys):
    size = q_ref.shape[0]
    scores = dot_nt(k_ref[:keys], q_ref[...]) * q_ref.shape[1] ** (-0.5)
    key_at = lax.broadcasted_iota(jnp.int32, (keys, size), 0)
    query_at = lax.broadcasted_iota(jnp.int32, (keys, size), 1) + block * size
    allowed = (key_at <= query_at) & (seg_col_ref[:keys] == seg_row_ref[...])
    return jnp.where(allowed, scores, -1e30)


def attend_kernel(q_ref, k_ref, vt_ref, seg_row_ref, seg_col_ref, out_ref, log_ref):
    size = q_ref.shape[0]
    blocks = k_ref.shape[0] // size
    for block in range(blocks):

        @pl.when(pl.program_id(1) == block)
        def _(block=block):
            keys = (block + 1) * size
            scores = masked_scores(q_ref, k_ref, seg_row_ref, seg_col_ref, block, keys)
            largest = jnp.max(scores, axis=0, keepdims=True)
            raised = jnp.exp(scores - largest)
            total = jnp.sum(raised, axis=0, keepdims=True)
            weights = (raised * (1.0 / total)).astype(BF16)
            out = jnp.dot(vt_ref[:, :keys], weights, preferred_element_type=F32)
            out_ref[...] = out.T.astype(BF16)
            log_ref[0] = largest + jnp.log(total)


def attend(query, key, value, segment):
    length, cols = query.shape
    head = key.shape[1]
    block = Q_BLOCK
    heads = cols // head
    return pl.pallas_call(
        attend_kernel,
        grid=(heads, length // block),
        in_specs=[
            pl.BlockSpec((block, head), lambda h, i: (i, h)),
            pl.BlockSpec((length, head), lambda h, i: (0, 0)),
            pl.BlockSpec((head, length), lambda h, i: (0, 0)),
            pl.BlockSpec((1, block), lambda h, i: (0, i)),
            pl.BlockSpec((length, 1), lambda h, i: (0, 0)),
        ],
        out_specs=[
            pl.BlockSpec((block, head), lambda h, i: (i, h)),
            pl.BlockSpec((1, 1, block), lambda h, i: (h, 0, i)),
        ],
        out_shape=[
            jax.ShapeDtypeStruct((length, cols), BF16),
            jax.ShapeDtypeStruct((heads, 1, length), F32),
        ],
        compiler_params=pltpu.CompilerParams(vmem_limit_bytes=VMEM_BYTES),
        cost_estimate=pl.CostEstimate(
            flops=4 * length * length * cols,
            bytes_accessed=8 * length * cols,
            transcendentals=length * length * heads,
        ),
    )(query, key, value.T, segment[None], segment[:, None])


def attend_back_kernel(
    q_ref,
    k_ref,
    kt_ref,
    v_ref,
    do_ref,
    log_ref,
    seg_row_ref,
    seg_col_ref,
    qpre_ref,
    kpre_ref,
    cos_ref,
    sin_ref,
    gq_ref,
    gk_ref,
    dq_ref,
    dk_ref,
    dv_ref,
    dgain_ref,
    key_sum,
    value_sum,
):
    size, head = q_ref.shape
    blocks = k_ref.shape[0] // size
    scale = head ** (-0.5)
    first = (pl.program_id(0) == 0) & (pl.program_id(1) == 0)
    last = (pl.program_id(0) == pl.num_programs(0) - 1) & (pl.program_id(1) == blocks - 1)

    @pl.when(first)
    def _():
        key_sum[...] = jnp.zeros_like(key_sum)
        value_sum[...] = jnp.zeros_like(value_sum)
        dgain_ref[...] = jnp.zeros_like(dgain_ref)

    def pull(grad, pre, gain, cos, sin):
        grad = grad.astype(BF16).astype(F32)
        turned = grad * cos + pltpu.roll(grad * sin, head // 2, 1)
        scale_row = lax.rsqrt(jnp.mean(pre * pre, axis=-1, keepdims=True) + EPSILON)
        unit = pre * scale_row
        gain_grad = jnp.sum(turned * unit, axis=0, keepdims=True)
        turned = turned * gain
        inner = jnp.mean(turned * unit, axis=-1, keepdims=True)
        return scale_row * (turned - unit * inner), gain_grad

    for block in range(blocks):

        @pl.when(pl.program_id(1) == block)
        def _(block=block):
            keys = (block + 1) * size
            rows = slice(block * size, keys)
            scores = masked_scores(q_ref, k_ref, seg_row_ref, seg_col_ref, block, keys)
            weights = jnp.exp(scores - log_ref[0])
            grads = dot_nt(v_ref[:keys], do_ref[...])
            inner = jnp.sum(weights * grads, axis=0, keepdims=True)
            score_grads = (weights * (grads - inner)).astype(BF16)
            value_sum[:keys] += jnp.dot(
                weights.astype(BF16), do_ref[...], preferred_element_type=F32
            )
            key_sum[:keys] += jnp.dot(score_grads, q_ref[...], preferred_element_type=F32)
            query_grad = jnp.dot(kt_ref[:, :keys], score_grads, preferred_element_type=F32)
            pre_grad, gain_grad = pull(
                query_grad.T * scale, qpre_ref[...], gq_ref[...], cos_ref[rows], sin_ref[rows]
            )
            dq_ref[...] = pre_grad.astype(BF16)
            dgain_ref[0:1] += gain_grad

    @pl.when(last)
    def _():
        pre_grad, gain_grad = pull(
            key_sum[...] * scale, kpre_ref[...], gk_ref[...], cos_ref[...], sin_ref[...]
        )
        dk_ref[...] = pre_grad.astype(BF16)
        dgain_ref[1:2] = gain_grad
        dv_ref[...] = value_sum[...].astype(BF16)


def attend_back(query, key, value, grad, logs, segment, qpre, kpre, cos, sin, gq, gk):
    length, cols = query.shape
    head = key.shape[1]
    block = Q_BLOCK
    heads = cols // head
    tile = pl.BlockSpec((block, head), lambda h, i: (i, h))

    def fixed(*shape):
        return pl.BlockSpec(shape, lambda h, i: (0, 0))

    return pl.pallas_call(
        attend_back_kernel,
        grid=(heads, length // block),
        in_specs=[
            tile,
            fixed(length, head),
            fixed(head, length),
            fixed(length, head),
            tile,
            pl.BlockSpec((1, 1, block), lambda h, i: (h, 0, i)),
            pl.BlockSpec((1, block), lambda h, i: (0, i)),
            fixed(length, 1),
            tile,
            fixed(length, head),
            fixed(length, head),
            fixed(length, head),
            fixed(1, head),
            fixed(1, head),
        ],
        out_specs=[tile, fixed(length, head), fixed(length, head), fixed(8, head)],
        out_shape=[
            jax.ShapeDtypeStruct((length, cols), BF16),
            jax.ShapeDtypeStruct((length, head), BF16),
            jax.ShapeDtypeStruct((length, head), BF16),
            jax.ShapeDtypeStruct((8, head), F32),
        ],
        scratch_shapes=[pltpu.VMEM((length, head), F32), pltpu.VMEM((length, head), F32)],
        compiler_params=pltpu.CompilerParams(vmem_limit_bytes=VMEM_BYTES),
        cost_estimate=pl.CostEstimate(
            flops=7 * length * length * cols,
            bytes_accessed=12 * length * cols,
            transcendentals=length * length * heads,
        ),
    )(
        query,
        key,
        key.T,
        value,
        grad,
        logs,
        segment[None],
        segment[:, None],
        qpre,
        kpre,
        cos,
        sin,
        gq[None],
        gk[None],
    )


def on_device(
    tokens,
    segment_ids,
    routes,
    w_query,
    w_key,
    w_value,
    w_output,
    w_router,
    gain_attn,
    gain_moe,
    gain_query,
    gain_key,
    w_gate,
    w_up,
    w_down,
    cotangent,
):
    bands, peers = lax.axis_size("dp"), lax.axis_size("expert")
    band, peer = lax.axis_index("dp"), lax.axis_index("expert")
    own_tokens = tokens[0]
    tok_count, width = own_tokens.shape
    band_rows = w_query.shape[0]
    experts = w_router.shape[1]
    gain_rows = gain_query.shape[0]
    head_size = gain_rows * bands * peers
    heads = w_query.shape[1] // head_size // bands
    q_cols, k_cols = heads * head_size, head_size
    qkv_cols = q_cols + 2 * k_cols
    owned = experts // peers

    tokens_all = lax.all_gather(own_tokens, "dp", axis=0, tiled=True)
    small = jnp.concatenate(
        [
            w_router,
            gain_attn[:, None],
            gain_moe[:, None],
            jnp.pad(gain_query, (0, band_rows - gain_rows))[:, None],
            jnp.pad(gain_key, (0, band_rows - gain_rows))[:, None],
        ],
        axis=1,
    )
    small = jnp.pad(small, ((0, 0), (0, 128 - small.shape[1])))
    packed = jnp.concatenate(
        [
            w_query.reshape(band_rows, bands, q_cols),
            w_key.reshape(band_rows, bands, k_cols),
            w_value.reshape(band_rows, bands, k_cols),
            jnp.broadcast_to(small[:, None], (band_rows, bands, 128)),
        ],
        axis=-1,
    ).transpose(1, 0, 2)
    swapped = lax.all_to_all(packed, "dp", split_axis=0, concat_axis=0, tiled=True)
    packed_all = lax.all_gather(swapped, "expert", axis=1, tiled=True).reshape(width, -1)
    qkv_w = packed_all[:, :qkv_cols]
    small_all = packed_all[:, qkv_cols:]
    router_full = small_all[:, :experts]
    attn_gain = small_all[:, experts].astype(F32)
    moe_gain = small_all[:, experts + 1].astype(F32)
    head_gains = small_all.reshape(bands * peers, band_rows, 128)[:, :gain_rows]
    query_gain = head_gains[:, :, experts + 2].reshape(-1).astype(F32)
    key_gain = head_gains[:, :, experts + 3].reshape(-1).astype(F32)
    out_w = lax.all_gather(w_output, "expert", axis=0, tiled=True)
    shared = owned >= bands
    routes_all = lax.all_gather(routes[0], ("dp", "expert") if shared else "expert", axis=0)
    cot_all = lax.all_gather(cotangent[0], "expert", axis=0)

    core = lax.rem(peer, 2)
    expert_ids = jnp.arange(experts, dtype=jnp.int32)
    mask_all = jnp.any(routes_all[..., None] == expert_ids, axis=2)
    mask_own = lax.dynamic_slice_in_dim(mask_all, peer * owned, owned, axis=2)
    earlier = jnp.tril(jnp.ones((tok_count, tok_count), BF16), -1)
    ranks = dot("ts,bse->bet", earlier, mask_own.astype(BF16)).astype(jnp.int32)
    ranks_all = jnp.where(mask_own.transpose(0, 2, 1), ranks, -1)
    if shared:
        ordered = [lax.dynamic_slice_in_dim(ranks_all, band * peers, peers)]
        for step in range(1, bands):
            column = lax.dynamic_slice_in_dim(ranks_all, (band ^ step) * peers, peers)
            ordered += [by_core(column, core), by_core(column, 1 - core)]
        ranks_all = jnp.concatenate(ordered)
        mask_all = lax.dynamic_slice_in_dim(mask_all, band * peers, peers)
    slots = jnp.arange(CAP, dtype=jnp.int32)
    chosen = ranks_all[:peers, :, None, :] == slots[None, None, :, None]
    placed = chosen.astype(BF16).reshape(peers, owned * CAP, tok_count)
    cot_placed = place_all(ranks_all, [cot_all] + (swapped_columns(cot_all) if shared else []))

    inputs = own_tokens.astype(F32)
    length = tokens_all.shape[0]
    half = head_size // 2
    frequency = ROPE_BASE ** (-jnp.arange(half, dtype=F32) * 2.0 / head_size)
    angles = jnp.arange(length, dtype=jnp.int32).astype(F32)[:, None] * frequency[None, :]
    cos = jnp.concatenate([jnp.cos(angles)] * 2, axis=-1)
    sin = jnp.concatenate([-jnp.sin(angles), jnp.sin(angles)], axis=-1)
    normed, query_pre, key_pre, query_low, key_low, value_low = make_qkv(
        tokens_all, attn_gain, qkv_w, cos, sin, query_gain, key_gain
    )
    segment = segment_ids[0]
    attended_low, log_total = attend(query_low, key_low, value_low, segment)
    branch = lax.psum_scatter(
        after(dot("tm,md->td", attended_low, out_w).astype(BF16), cot_all, routes_all),
        "dp",
        scatter_dimension=0,
        tiled=True,
    )
    hidden = inputs + branch.astype(F32)

    normed_moe_f, moe_pull = jax.vjp(norm_rows, hidden, moe_gain)
    normed_moe = normed_moe_f.astype(BF16)
    moe_all = lax.all_gather(normed_moe, "expert", axis=0)
    gates_all = masked_softmax(dot("btd,de->bte", moe_all, router_full), mask_all)
    gates_own = lax.dynamic_slice_in_dim(gates_all, peer * owned, owned, axis=2)
    slot_gates = jnp.sum(
        jnp.where(chosen, gates_own.transpose(0, 2, 1)[:, :, None, :], 0.0), axis=-1
    )

    def combine(rows):
        spread = (
            rows.reshape(owned, peers, CAP, width)
            .transpose(1, 0, 2, 3)
            .reshape(peers, owned * CAP, width)
        )
        return dot("bst,bsd->btd", placed, spread).astype(BF16)

    def own_rows(rows):
        return rows[:, :peers].reshape(owned, peers * CAP, width)

    row_gates = slot_gates.transpose(1, 0, 2).reshape(owned, peers * CAP, 1)
    x_placed = place_all(ranks_all, [moe_all])
    arrived, cot_rows = own_rows(x_placed), own_rows(cot_placed)
    gate_in = dot("erd,edf->erf", arrived, w_gate)
    up_in = dot("erd,edf->erf", arrived, w_up)
    active_f, act_pull = jax.vjp(activate, gate_in, up_in)
    active = active_f.astype(BF16)
    raw_active = dot("erd,efd->erf", cot_rows, w_down)
    grad_gate_f, grad_up_f = act_pull(row_gates * raw_active)
    gate_low = grad_gate_f.astype(BF16)
    up_low = grad_up_f.astype(BF16)
    if not shared:
        expert_sums = lax.psum(
            (
                dot("erd,erf->edf", arrived, gate_low).astype(BF16),
                dot("erd,erf->edf", arrived, up_low).astype(BF16),
                dot("erf,erd->efd", (row_gates * active_f).astype(BF16), cot_rows).astype(BF16),
            ),
            "dp",
        )
    rows_back = dot("erf,edf->erd", gate_low, w_gate) + dot("erf,edf->erd", up_low, w_up)
    rows_back = combine(rows_back.astype(BF16))
    back = sum_peers(rows_back)
    slot_grads = jnp.sum(active.astype(F32) * raw_active, axis=-1)
    slot_grads = slot_grads.reshape(owned, peers, CAP).transpose(1, 0, 2)
    token_grads = jnp.sum(jnp.where(chosen, slot_grads[..., None], 0.0), axis=2)
    gate_grads = (
        lax.all_to_all(token_grads, "expert", split_axis=0, concat_axis=0, tiled=True)
        .reshape(experts, tok_count)
        .T
    )
    result = dot("erf,efd->erd", after(active, rows_back), w_down).astype(BF16)

    if shared:
        x_placed = place_all(ranks_all, swapped_columns(moe_all), x_placed, peers)
        all_gates = [slot_gates]
        for step in range(1, bands):
            got = lax.ppermute(slot_gates, "dp", [(i, i ^ step) for i in range(bands)])
            all_gates += [by_core(got, core), by_core(got, 1 - core)]
        all_gates = jnp.concatenate(all_gates).transpose(1, 0, 2).reshape(owned, 1, -1)
        x_rows = after(x_placed, rows_back).reshape(owned, -1, width)
        c_rows = cot_placed.reshape(owned, -1, width)
        expert_sums = None
        for expert in range(owned):
            expert_sums = expert_grads(
                x_rows, c_rows, all_gates, w_gate, w_up, w_down, expert, expert_sums
            )

    own_gates = lax.dynamic_index_in_dim(gates_all, peer, 0, keepdims=False)
    grad_logits = own_gates * (
        gate_grads - jnp.sum(own_gates * gate_grads, axis=-1, keepdims=True)
    )
    grad_router_w = jnp.einsum("td,te->de", normed_moe.astype(F32), grad_logits, precision=PRECISE)
    grad_normed = back + jnp.einsum(
        "te,de->td", grad_logits, router_full.astype(F32), precision=PRECISE
    )
    grad_hidden_n, grad_moe_gain = moe_pull(grad_normed)
    grad_hidden = cotangent[0].astype(F32) + grad_hidden_n
    grad_branch = grad_hidden.astype(BF16)
    branch_all = gather_blocks(grad_branch, "dp").reshape(length, width)

    grad_attended = dot("td,md->tm", branch_all, out_w).astype(BF16)
    query_grad, key_grad, value_grad, head_grads = attend_back(
        query_low,
        key_low,
        value_low,
        grad_attended,
        log_total,
        segment,
        query_pre,
        key_pre,
        cos,
        sin,
        query_gain,
        key_gain,
    )
    qkv_grad = jnp.concatenate([query_grad, key_grad, value_grad], axis=1)
    grad_normed_attn = sum_blocks(
        dot("tm,dm->td", qkv_grad, qkv_w).astype(BF16).reshape(bands, tok_count, width), "dp"
    )
    _, attn_pull = jax.vjp(norm_rows, inputs, attn_gain)
    grad_inputs_n, grad_attn_gain = attn_pull(grad_normed_attn)
    grad_tokens = grad_hidden + grad_inputs_n

    whole_gains = jnp.stack([grad_attn_gain, grad_moe_gain], axis=1)
    head_gains = head_grads[:2].T
    head_gains = jnp.pad(
        head_gains.reshape(bands * peers, gain_rows, 2),
        ((0, 0), (0, band_rows - gain_rows), (0, 0)),
    )
    small_grad = jnp.concatenate(
        [grad_router_w, whole_gains, head_gains.reshape(width, 2)], axis=1
    )
    small_grad = jnp.pad(small_grad, ((0, 0), (0, 128 - small_grad.shape[1])))
    band_qkv = jnp.concatenate([dot("td,tm->dm", normed, qkv_grad), small_grad], axis=1)
    band_qkv = band_qkv.astype(BF16).reshape(bands, peers, band_rows, -1).transpose(1, 0, 2, 3)
    band_qkv = sum_peers(band_qkv).astype(BF16)
    band_qkv = lax.all_to_all(band_qkv, "dp", split_axis=0, concat_axis=0, tiled=True).transpose(
        1, 0, 2
    )
    grad_query = band_qkv[:, :, :q_cols].astype(F32).reshape(band_rows, -1)
    grad_key = band_qkv[:, :, q_cols : q_cols + k_cols].astype(F32).reshape(band_rows, -1)
    grad_value = band_qkv[:, :, q_cols + k_cols : qkv_cols].astype(F32).reshape(band_rows, -1)
    smaller = jnp.sum(band_qkv[:, :, qkv_cols:].astype(F32), axis=1)
    grad_output = sum_peers(
        dot("tm,td->md", attended_low, branch_all).astype(BF16).reshape(peers, -1, width)
    )

    moe_sum = sum_peers(combine((row_gates * result.astype(F32)).astype(BF16)))
    block_out = (hidden + moe_sum).astype(BF16)
    return (
        block_out[None],
        grad_tokens[None],
        grad_query,
        grad_key,
        grad_value,
        grad_output,
        smaller[:, :experts],
        smaller[:, experts],
        smaller[:, experts + 1],
        smaller[:gain_rows, experts + 2],
        smaller[:gain_rows, experts + 3],
        expert_sums[0].astype(F32),
        expert_sums[1].astype(F32),
        expert_sums[2].astype(F32),
    )


def solution(mesh):
    both = ("dp", "expert")
    return jax.shard_map(
        on_device,
        mesh=mesh,
        in_specs=(
            P("expert", "dp", None),
            P("expert", None),
            P("expert", "dp", None),
            P(both, None),
            P(both, None),
            P(both, None),
            P(both, None),
            P(both, None),
            P(both),
            P(both),
            P(both),
            P(both),
            P("expert", None, None),
            P("expert", None, None),
            P("expert", None, None),
            P("expert", "dp", None),
        ),
        out_specs=(
            P("expert", "dp", None),
            P("expert", "dp", None),
            P(both, None),
            P(both, None),
            P(both, None),
            P(both, None),
            P(both, None),
            P(both),
            P(both),
            P(both),
            P(both),
            P("expert", None, None),
            P("expert", None, None),
            P("expert", None, None),
        ),
        check_vma=False,
    )
```

```python
import jax
import jax.numpy as jnp
from jax import lax
from jax.experimental import pallas as pl
from jax.experimental.pallas import tpu as pltpu
from jax.sharding import PartitionSpec as P

CAP = 80
Q_BLOCK = 256
HIDDEN_TILE = 256
OWN_ROWS = 8 * CAP
WIDTH_TILE = 512
ROW_PARTS = 2
VMEM_BYTES = 60 << 20


EPSILON = 1e-06
ROPE_BASE = 1000000.0
PRECISE = lax.Precision.HIGHEST
F32 = jnp.float32
BF16 = jnp.bfloat16


def norm_rows(values, gain_row):
    return (
        values * lax.rsqrt(jnp.mean(values * values, axis=-1, keepdims=True) + EPSILON) * gain_row
    )


def activate(gate_vals, up_vals):
    return gate_vals * jax.nn.sigmoid(gate_vals) * up_vals


def masked_softmax(logits, mask):
    kept = jnp.where(mask, logits, -jnp.inf)
    largest = jnp.max(kept, axis=-1, keepdims=True)
    raised = jnp.where(mask, jnp.exp(logits - largest), 0.0)
    return raised / jnp.sum(raised, axis=-1, keepdims=True)


def nothing(*refs):
    del refs


def after(value, *others):
    anywhere = pl.BlockSpec(memory_space=pl.ANY)
    return pl.pallas_call(
        nothing,
        out_shape=jax.ShapeDtypeStruct(value.shape, value.dtype),
        in_specs=[anywhere] * (1 + len(others)),
        out_specs=anywhere,
        input_output_aliases={0: 0},
    )(value, *others)


def shifted(value, axis, step):
    count = lax.axis_size(axis)
    return lax.ppermute(value, axis, [(i, (i + step) % count) for i in range(count)])


def traded(value, axis, step):
    return lax.ppermute(value, axis, [(i, i ^ step) for i in range(lax.axis_size(axis))])


def gather_blocks(own, axis):
    count, me = lax.axis_size(axis), lax.axis_index(axis)
    whole = jnp.zeros((count, *own.shape), own.dtype)
    whole = lax.dynamic_update_index_in_dim(whole, own, me, 0)
    for step in range(1, count):
        whole = lax.dynamic_update_index_in_dim(whole, traded(own, axis, step), me ^ step, 0)
    return whole


def sum_blocks(blocks, axis):
    count, me = lax.axis_size(axis), lax.axis_index(axis)
    total = lax.dynamic_index_in_dim(blocks, me, 0, keepdims=False).astype(F32)
    for step in range(1, count):
        sent = lax.dynamic_index_in_dim(blocks, me ^ step, 0, keepdims=False)
        total = total + traded(sent, axis, step).astype(F32)
    return total


def sum_peers(blocks):
    count, me = lax.axis_size("expert"), lax.axis_index("expert")
    core, chip, chips = lax.rem(me, 2), lax.div(me, 2), count // 2
    paired = blocks.reshape(chips, 2, *blocks.shape[1:])
    sent = lax.dynamic_index_in_dim(paired, 1 - core, 1, keepdims=False)
    kept = lax.dynamic_index_in_dim(paired, core, 1, keepdims=False)
    got = lax.ppermute(sent, "expert", [(i, i ^ 1) for i in range(count)])
    halves = (kept.astype(F32) + got.astype(F32)).astype(BF16)
    total = lax.dynamic_index_in_dim(halves, chip, 0, keepdims=False).astype(F32)
    for step in range(1, chips):
        sent = lax.dynamic_index_in_dim(halves, lax.rem(chip + step, chips), 0, keepdims=False)
        total = total + shifted(sent, "expert", 2 * step).astype(F32)
    return total


def dot(spec, left, right):
    return jnp.einsum(spec, left, right, preferred_element_type=F32)


def swapped_columns(own):
    peer, bands = lax.axis_index("expert"), lax.axis_size("dp")
    mine = by_core(own, lax.rem(peer, 2))
    pieces = []
    for step in range(1, bands):
        got = traded(mine, "dp", step)
        pieces += [got, traded(got, "expert", 1)]
    return pieces


def by_core(values, core):
    paired = values.reshape(-1, 2, *values.shape[1:])
    return lax.dynamic_index_in_dim(paired, core, 1, keepdims=False)


def place_kernel(rank_ref, block_ref, *rest):
    rows_ref = rest[-1]
    count, owned, tok_count = rank_ref.shape
    slots = lax.broadcasted_iota(jnp.int32, (CAP, tok_count), 0)
    width = block_ref.shape[-1]
    for block in range(count):
        ranks = rank_ref[block]
        hot = jnp.concatenate([ranks[e : e + 1] == slots for e in range(owned)], axis=0)
        hot = jnp.where(hot, 1.0, 0.0).astype(BF16)
        for start in range(0, width, WIDTH_TILE):
            cols = slice(start, start + WIDTH_TILE)
            rows = jnp.dot(hot, block_ref[block, :, cols], preferred_element_type=F32)
            rows_ref[:, block, :, cols] = rows.astype(BF16).reshape(owned, CAP, WIDTH_TILE)


def place_rows(ranks, blocks, start, total, buffer=None):
    count, owned, tok_count = ranks.shape
    width = blocks.shape[-1]
    several = 2
    first = start // several
    in_specs = [
        pl.BlockSpec((several, owned, tok_count), lambda b: (b, 0, 0)),
        pl.BlockSpec((several, tok_count, width), lambda b: (b, 0, 0)),
    ]
    given = (ranks, blocks)
    if buffer is not None:
        in_specs.append(pl.BlockSpec(memory_space=pl.ANY))
        given += (buffer,)
    return pl.pallas_call(
        place_kernel,
        grid=(count // several,),
        out_shape=jax.ShapeDtypeStruct((owned, total, CAP, width), BF16),
        in_specs=in_specs,
        out_specs=pl.BlockSpec((owned, several, CAP, width), lambda b: (0, first + b, 0, 0)),
        input_output_aliases={} if buffer is None else {2: 0},
        compiler_params=pltpu.CompilerParams(vmem_limit_bytes=VMEM_BYTES),
        cost_estimate=pl.CostEstimate(
            flops=2 * count * owned * CAP * tok_count * width,
            bytes_accessed=2 * count * (tok_count + owned * CAP) * width,
            transcendentals=0,
        ),
    )(*given)


def combine_kernel(rank_ref, rows_ref, out_ref):
    tok_count, owned = rank_ref.shape[1:]
    slots = owned * CAP
    width = out_ref.shape[-1]
    lane = lax.broadcasted_iota(jnp.int32, (tok_count, slots), 1)
    hot = jnp.zeros((tok_count, slots), F32)
    for e in range(owned):
        ranks = rank_ref[0, :, e : e + 1]
        hot = jnp.where((ranks >= 0) & (lane == ranks + e * CAP), 1.0, hot)
    hot = hot.astype(BF16)
    for start in range(0, width, WIDTH_TILE):
        cols = slice(start, start + WIDTH_TILE)
        rows = rows_ref[:, 0, :, cols].reshape(slots, WIDTH_TILE)
        out_ref[0, :, cols] = jnp.dot(hot, rows, preferred_element_type=F32).astype(BF16)


def combine(ranks, rows):
    count, tok_count, owned = ranks.shape
    width = rows.shape[-1]
    return pl.pallas_call(
        combine_kernel,
        grid=(count,),
        out_shape=jax.ShapeDtypeStruct((count, tok_count, width), BF16),
        in_specs=[
            pl.BlockSpec((1, tok_count, owned), lambda b: (b, 0, 0)),
            pl.BlockSpec((owned, 1, CAP, width), lambda b: (0, b, 0, 0)),
        ],
        out_specs=pl.BlockSpec((1, tok_count, width), lambda b: (b, 0, 0)),
        compiler_params=pltpu.CompilerParams(vmem_limit_bytes=VMEM_BYTES),
        cost_estimate=pl.CostEstimate(
            flops=2 * count * owned * CAP * tok_count * width,
            bytes_accessed=2 * count * (tok_count + owned * CAP) * width,
            transcendentals=0,
        ),
    )(ranks, rows.reshape(owned, count, CAP, width))


def place_all(ranks, pieces, buffer=None, start=0):
    total = ranks.shape[0]
    for piece in pieces:
        count = piece.shape[0]
        buffer = place_rows(ranks[start : start + count], piece, start, total, buffer)
        start += count
    return buffer


def dot_nt(left, right):
    return lax.dot_general(left, right, (((1,), (1,)), ((), ())), preferred_element_type=F32)


def hidden_grads(x, c, gates, wg_ref, wu_ref, wd_ref):
    gate_in = jnp.dot(x, wg_ref[0], preferred_element_type=F32)
    up_in = jnp.dot(x, wu_ref[0], preferred_element_type=F32)
    raw = dot_nt(c, wd_ref[0])
    sig = 1.0 / (1.0 + jnp.exp(-gate_in))
    silu = gate_in * sig
    active = silu * up_in
    grad = raw * gates
    gate_grad = grad * up_in * (sig + silu * (1.0 - sig))
    up_grad = grad * silu
    return (active * gates).astype(BF16), gate_grad.astype(BF16), up_grad.astype(BF16), active * raw


def own_kernel(
    x_ref,
    c_ref,
    g_ref,
    wg_ref,
    wu_ref,
    wd_ref,
    active_ref,
    gate_ref,
    up_ref,
    slot_ref,
    back_ref,
    out_ref,
    back_sum,
    out_sum,
):
    width = x_ref.shape[-1]
    step = pl.program_id(2)
    active, gate_grad, up_grad, slot = hidden_grads(
        x_ref[0], c_ref[0], g_ref[0], wg_ref, wu_ref, wd_ref
    )
    active_ref[0] = active
    gate_ref[0] = gate_grad
    up_ref[0] = up_grad
    slot = jnp.sum(slot, axis=1, keepdims=True)
    slot_ref[0] = jnp.where(step == 0, slot, slot_ref[0] + slot)
    for start in range(0, width, WIDTH_TILE):
        cols = slice(start, start + WIDTH_TILE)
        rows = dot_nt(gate_ref[0], wg_ref[0, cols, :]) + dot_nt(up_ref[0], wu_ref[0, cols, :])
        back_sum[:, cols] = jnp.where(step == 0, rows, back_sum[:, cols] + rows)
        rows = jnp.dot(active_ref[0], wd_ref[0, :, cols], preferred_element_type=F32)
        out_sum[:, cols] = jnp.where(step == 0, rows, out_sum[:, cols] + rows)

    @pl.when(step == pl.num_programs(2) - 1)
    def _():
        back_ref[0] = back_sum[...].astype(BF16)
        out_ref[0] = out_sum[...].astype(BF16)


def own_experts(x_rows, c_rows, gates, w_gate, w_up, w_down):
    owned, rows = gates.shape[:2]
    width = x_rows.shape[-1]
    hidden = w_down.shape[1]
    tile = HIDDEN_TILE
    some = min(rows, OWN_ROWS)
    whole = pl.BlockSpec((1, some, width), lambda e, r, f: (e, r, 0))
    column = pl.BlockSpec((1, some, 1), lambda e, r, f: (e, r, 0))
    part = pl.BlockSpec((1, some, tile), lambda e, r, f: (e, r, f))
    inward = pl.BlockSpec((1, width, tile), lambda e, r, f: (e, 0, f))
    outward = pl.BlockSpec((1, tile, width), lambda e, r, f: (e, f, 0))
    return pl.pallas_call(
        own_kernel,
        grid=(owned, rows // some, hidden // tile),
        in_specs=[whole, whole, column, inward, inward, outward],
        out_specs=[part, part, part, column, whole, whole],
        out_shape=[jax.ShapeDtypeStruct((owned, rows, hidden), BF16)] * 3
        + [jax.ShapeDtypeStruct((owned, rows, 1), F32)]
        + [jax.ShapeDtypeStruct((owned, rows, width), BF16)] * 2,
        scratch_shapes=[pltpu.VMEM((some, width), F32)] * 2,
        compiler_params=pltpu.CompilerParams(vmem_limit_bytes=VMEM_BYTES),
        cost_estimate=pl.CostEstimate(
            flops=12 * owned * rows * width * hidden,
            bytes_accessed=owned * (8 * rows * width + 6 * width * hidden),
            transcendentals=owned * rows * hidden,
        ),
    )(x_rows, c_rows, gates, w_gate, w_up, w_down)


def grads_kernel(
    x_ref, c_ref, g_ref, active_ref, gate_ref, up_ref, wg_ref, wu_ref, wd_ref, *rest
):
    dg_ref, du_ref, dd_ref, sums, pair, actives = rest[-6:]
    tile = HIDDEN_TILE
    rows, width = x_ref.shape[1:]
    own = active_ref.shape[1]
    step = pl.program_id(1)

    def keep(start, active, gate_grad, up_grad):
        part = slice(start, start + own)
        actives[:, part] = active.T
        pair[:tile, part] = gate_grad.T
        pair[tile:, part] = up_grad.T

    def work_out(start):
        part = slice(start, start + own)
        active, gate_grad, up_grad, _ = hidden_grads(
            x_ref[0, part], c_ref[0, part], g_ref[0, part], wg_ref, wu_ref, wd_ref
        )
        keep(start, active, gate_grad, up_grad)

    @pl.when(step == 0)
    def _():
        keep(0, active_ref[0], gate_ref[0], up_ref[0])

    @pl.when(step > 0)
    def _():
        work_out(0)

    for start in range(own, rows, own):
        work_out(start)

    @pl.loop(0, width // WIDTH_TILE)
    def _(c):
        cols = pl.ds(pl.multiple_of(c * WIDTH_TILE, WIDTH_TILE), WIDTH_TILE)
        grads = jnp.dot(pair[...], x_ref[0, :, cols], preferred_element_type=F32)
        sums[:, cols] = jnp.where(step == 0, grads, sums[:, cols] + grads)
        grads = jnp.dot(actives[...], c_ref[0, :, cols], preferred_element_type=F32)
        dd_ref[0, :, cols] = jnp.where(step == 0, grads, dd_ref[0, :, cols] + grads)

    @pl.when(step == pl.num_programs(1) - 1)
    def _():
        same = lax.broadcasted_iota(jnp.int32, (tile, tile), 0) == lax.broadcasted_iota(
            jnp.int32, (tile, tile), 1
        )
        same = jnp.where(same, 1.0, 0.0).astype(BF16)

        @pl.loop(0, width // tile)
        def _(c):
            cols = pl.ds(pl.multiple_of(c * tile, tile), tile)
            dg_ref[0, cols, :] = dot_nt(same, sums[:tile, cols].astype(BF16))
            du_ref[0, cols, :] = dot_nt(same, sums[tile:, cols].astype(BF16))


def expert_grads(x_rows, c_rows, gates, own, w_gate, w_up, w_down, expert, buffers=None):
    owned, rows, width = x_rows.shape
    hidden = w_down.shape[1]
    tile, parts = HIDDEN_TILE, ROW_PARTS
    part, own_rows = rows // parts, own[0].shape[1]
    shapes = [(owned, width, hidden)] * 2 + [(owned, hidden, width)]
    in_specs = [
        pl.BlockSpec((1, part, width), lambda f, r: (expert, r, 0)),
        pl.BlockSpec((1, part, width), lambda f, r: (expert, r, 0)),
        pl.BlockSpec((1, part, 1), lambda f, r: (expert, r, 0)),
        *[pl.BlockSpec((1, own_rows, tile), lambda f, r: (expert, 0, f))] * 3,
        pl.BlockSpec((1, width, tile), lambda f, r: (expert, 0, f)),
        pl.BlockSpec((1, width, tile), lambda f, r: (expert, 0, f)),
        pl.BlockSpec((1, tile, width), lambda f, r: (expert, f, 0)),
    ]
    given = (x_rows, c_rows, gates, *own, w_gate, w_up, w_down)
    aliases = {}
    if buffers is not None:
        aliases = {len(given) + i: i for i in range(3)}
        in_specs += [pl.BlockSpec(memory_space=pl.ANY)] * 3
        given += tuple(buffers)
    return pl.pallas_call(
        grads_kernel,
        grid=(hidden // tile, parts),
        out_shape=[jax.ShapeDtypeStruct(shape, F32) for shape in shapes],
        in_specs=in_specs,
        out_specs=[
            pl.BlockSpec((1, width, tile), lambda f, r: (expert, 0, f)),
            pl.BlockSpec((1, width, tile), lambda f, r: (expert, 0, f)),
            pl.BlockSpec((1, tile, width), lambda f, r: (expert, f, 0)),
        ],
        scratch_shapes=[
            pltpu.VMEM((2 * tile, width), F32),
            pltpu.VMEM((2 * tile, part), BF16),
            pltpu.VMEM((tile, part), BF16),
        ],
        input_output_aliases=aliases,
        compiler_params=pltpu.CompilerParams(vmem_limit_bytes=VMEM_BYTES),
        cost_estimate=pl.CostEstimate(
            flops=12 * rows * width * hidden,
            bytes_accessed=12 * rows * width + 24 * width * hidden,
            transcendentals=rows * hidden,
        ),
    )(*given)


def turn(values, cos, sin):
    return values * cos + pltpu.roll(values, values.shape[-1] // 2, 1) * sin


def qkv_kernel(
    tok_ref,
    gain_ref,
    w_ref,
    cos_ref,
    sin_ref,
    gq_ref,
    gk_ref,
    normed_ref,
    qpre_ref,
    kpre_ref,
    qrot_ref,
    krot_ref,
    value_ref,
):
    head = cos_ref.shape[1]
    heads = qpre_ref.shape[1] // head
    normed = norm_rows(tok_ref[...].astype(F32), gain_ref[...]).astype(BF16)
    normed_ref[...] = normed
    cos, sin = cos_ref[...], sin_ref[...]
    for pair in range(0, heads, 2):
        cols = slice(pair * head, (pair + 2) * head)
        pre = jnp.dot(normed, w_ref[:, cols], preferred_element_type=F32)
        qpre_ref[:, cols] = pre
        for h in range(2):
            one = slice(h * head, (h + 1) * head)
            rot = turn(norm_rows(pre[:, one], gq_ref[...]), cos, sin)
            qrot_ref[:, (pair + h) * head : (pair + h + 1) * head] = rot.astype(BF16)
    cols = slice(heads * head, (heads + 2) * head)
    pre = jnp.dot(normed, w_ref[:, cols], preferred_element_type=F32)
    kpre_ref[...] = pre[:, :head]
    krot_ref[...] = turn(norm_rows(pre[:, :head], gk_ref[...]), cos, sin).astype(BF16)
    value_ref[...] = pre[:, head:].astype(BF16)


def make_qkv(tokens, gain, weight, cos, sin, query_gain, key_gain):
    length, width = tokens.shape
    head = cos.shape[1]
    cols = weight.shape[1]
    q_cols = cols - 3 * head
    block = Q_BLOCK

    def rows(size):
        return pl.BlockSpec((block, size), lambda i: (i, 0))

    def fixed(*shape):
        return pl.BlockSpec(shape, lambda i: (0, 0))

    return pl.pallas_call(
        qkv_kernel,
        grid=(length // block,),
        in_specs=[
            rows(width),
            fixed(1, width),
            fixed(width, cols),
            rows(head),
            rows(head),
            fixed(1, head),
            fixed(1, head),
        ],
        out_specs=[rows(width), rows(q_cols), rows(head), rows(q_cols), rows(head), rows(head)],
        out_shape=[
            jax.ShapeDtypeStruct((length, width), BF16),
            jax.ShapeDtypeStruct((length, q_cols), F32),
            jax.ShapeDtypeStruct((length, head), F32),
            jax.ShapeDtypeStruct((length, q_cols), BF16),
            jax.ShapeDtypeStruct((length, head), BF16),
            jax.ShapeDtypeStruct((length, head), BF16),
        ],
        compiler_params=pltpu.CompilerParams(vmem_limit_bytes=VMEM_BYTES),
        cost_estimate=pl.CostEstimate(
            flops=2 * length * width * cols,
            bytes_accessed=2 * width * cols + 8 * length * width,
            transcendentals=0,
        ),
    )(tokens, gain[None], weight, cos, sin, query_gain[None], key_gain[None])


def masked_scores(q_ref, k_ref, seg_row_ref, seg_col_ref, block, keys):
    size = q_ref.shape[0]
    scores = dot_nt(k_ref[:keys], q_ref[...]) * q_ref.shape[1] ** (-0.5)
    key_at = lax.broadcasted_iota(jnp.int32, (keys, size), 0)
    query_at = lax.broadcasted_iota(jnp.int32, (keys, size), 1) + block * size
    allowed = (key_at <= query_at) & (seg_col_ref[:keys] == seg_row_ref[...])
    return jnp.where(allowed, scores, -1e30)


def attend_kernel(q_ref, k_ref, vt_ref, seg_row_ref, seg_col_ref, out_ref, log_ref):
    size = q_ref.shape[0]
    blocks = k_ref.shape[0] // size
    for block in range(blocks):

        @pl.when(pl.program_id(1) == block)
        def _(block=block):
            keys = (block + 1) * size
            scores = masked_scores(q_ref, k_ref, seg_row_ref, seg_col_ref, block, keys)
            largest = jnp.max(scores, axis=0, keepdims=True)
            raised = jnp.exp(scores - largest)
            total = jnp.sum(raised, axis=0, keepdims=True)
            weights = (raised * (1.0 / total)).astype(BF16)
            out = jnp.dot(vt_ref[:, :keys], weights, preferred_element_type=F32)
            out_ref[...] = out.T.astype(BF16)
            log_ref[0] = largest + jnp.log(total)


def attend(query, key, value, segment):
    length, cols = query.shape
    head = key.shape[1]
    block = Q_BLOCK
    heads = cols // head
    return pl.pallas_call(
        attend_kernel,
        grid=(heads, length // block),
        in_specs=[
            pl.BlockSpec((block, head), lambda h, i: (i, h)),
            pl.BlockSpec((length, head), lambda h, i: (0, 0)),
            pl.BlockSpec((head, length), lambda h, i: (0, 0)),
            pl.BlockSpec((1, block), lambda h, i: (0, i)),
            pl.BlockSpec((length, 1), lambda h, i: (0, 0)),
        ],
        out_specs=[
            pl.BlockSpec((block, head), lambda h, i: (i, h)),
            pl.BlockSpec((1, 1, block), lambda h, i: (h, 0, i)),
        ],
        out_shape=[
            jax.ShapeDtypeStruct((length, cols), BF16),
            jax.ShapeDtypeStruct((heads, 1, length), F32),
        ],
        compiler_params=pltpu.CompilerParams(vmem_limit_bytes=VMEM_BYTES),
        cost_estimate=pl.CostEstimate(
            flops=4 * length * length * cols,
            bytes_accessed=8 * length * cols,
            transcendentals=length * length * heads,
        ),
    )(query, key, value.T, segment[None], segment[:, None])


def attend_back_kernel(
    q_ref,
    k_ref,
    kt_ref,
    v_ref,
    do_ref,
    log_ref,
    seg_row_ref,
    seg_col_ref,
    qpre_ref,
    kpre_ref,
    cos_ref,
    sin_ref,
    gq_ref,
    gk_ref,
    dq_ref,
    dk_ref,
    dv_ref,
    dgain_ref,
    key_sum,
    value_sum,
):
    size, head = q_ref.shape
    blocks = k_ref.shape[0] // size
    scale = head ** (-0.5)
    first = (pl.program_id(0) == 0) & (pl.program_id(1) == 0)
    last = (pl.program_id(0) == pl.num_programs(0) - 1) & (pl.program_id(1) == blocks - 1)

    @pl.when(first)
    def _():
        key_sum[...] = jnp.zeros_like(key_sum)
        value_sum[...] = jnp.zeros_like(value_sum)
        dgain_ref[...] = jnp.zeros_like(dgain_ref)

    def pull(grad, pre, gain, cos, sin):
        grad = grad.astype(BF16).astype(F32)
        turned = grad * cos + pltpu.roll(grad * sin, head // 2, 1)
        scale_row = lax.rsqrt(jnp.mean(pre * pre, axis=-1, keepdims=True) + EPSILON)
        unit = pre * scale_row
        gain_grad = jnp.sum(turned * unit, axis=0, keepdims=True)
        turned = turned * gain
        inner = jnp.mean(turned * unit, axis=-1, keepdims=True)
        return scale_row * (turned - unit * inner), gain_grad

    for block in range(blocks):

        @pl.when(pl.program_id(1) == block)
        def _(block=block):
            keys = (block + 1) * size
            rows = slice(block * size, keys)
            scores = masked_scores(q_ref, k_ref, seg_row_ref, seg_col_ref, block, keys)
            weights = jnp.exp(scores - log_ref[0])
            grads = dot_nt(v_ref[:keys], do_ref[...])
            inner = jnp.sum(weights * grads, axis=0, keepdims=True)
            score_grads = (weights * (grads - inner)).astype(BF16)
            value_sum[:keys] += jnp.dot(
                weights.astype(BF16), do_ref[...], preferred_element_type=F32
            )
            key_sum[:keys] += jnp.dot(score_grads, q_ref[...], preferred_element_type=F32)
            query_grad = jnp.dot(kt_ref[:, :keys], score_grads, preferred_element_type=F32)
            pre_grad, gain_grad = pull(
                query_grad.T * scale, qpre_ref[...], gq_ref[...], cos_ref[rows], sin_ref[rows]
            )
            dq_ref[...] = pre_grad.astype(BF16)
            dgain_ref[0:1] += gain_grad

    @pl.when(last)
    def _():
        pre_grad, gain_grad = pull(
            key_sum[...] * scale, kpre_ref[...], gk_ref[...], cos_ref[...], sin_ref[...]
        )
        dk_ref[...] = pre_grad.astype(BF16)
        dgain_ref[1:2] = gain_grad
        dv_ref[...] = value_sum[...].astype(BF16)


def attend_back(query, key, value, grad, logs, segment, qpre, kpre, cos, sin, gq, gk):
    length, cols = query.shape
    head = key.shape[1]
    block = Q_BLOCK
    heads = cols // head
    tile = pl.BlockSpec((block, head), lambda h, i: (i, h))

    def fixed(*shape):
        return pl.BlockSpec(shape, lambda h, i: (0, 0))

    return pl.pallas_call(
        attend_back_kernel,
        grid=(heads, length // block),
        in_specs=[
            tile,
            fixed(length, head),
            fixed(head, length),
            fixed(length, head),
            tile,
            pl.BlockSpec((1, 1, block), lambda h, i: (h, 0, i)),
            pl.BlockSpec((1, block), lambda h, i: (0, i)),
            fixed(length, 1),
            tile,
            fixed(length, head),
            fixed(length, head),
            fixed(length, head),
            fixed(1, head),
            fixed(1, head),
        ],
        out_specs=[tile, fixed(length, head), fixed(length, head), fixed(8, head)],
        out_shape=[
            jax.ShapeDtypeStruct((length, cols), BF16),
            jax.ShapeDtypeStruct((length, head), BF16),
            jax.ShapeDtypeStruct((length, head), BF16),
            jax.ShapeDtypeStruct((8, head), F32),
        ],
        scratch_shapes=[pltpu.VMEM((length, head), F32), pltpu.VMEM((length, head), F32)],
        compiler_params=pltpu.CompilerParams(vmem_limit_bytes=VMEM_BYTES),
        cost_estimate=pl.CostEstimate(
            flops=7 * length * length * cols,
            bytes_accessed=12 * length * cols,
            transcendentals=length * length * heads,
        ),
    )(
        query,
        key,
        key.T,
        value,
        grad,
        logs,
        segment[None],
        segment[:, None],
        qpre,
        kpre,
        cos,
        sin,
        gq[None],
        gk[None],
    )


def on_device(
    tokens,
    segment_ids,
    routes,
    w_query,
    w_key,
    w_value,
    w_output,
    w_router,
    gain_attn,
    gain_moe,
    gain_query,
    gain_key,
    w_gate,
    w_up,
    w_down,
    cotangent,
):
    bands, peers = lax.axis_size("dp"), lax.axis_size("expert")
    band, peer = lax.axis_index("dp"), lax.axis_index("expert")
    own_tokens = tokens[0]
    tok_count, width = own_tokens.shape
    band_rows = w_query.shape[0]
    experts = w_router.shape[1]
    gain_rows = gain_query.shape[0]
    head_size = gain_rows * bands * peers
    heads = w_query.shape[1] // head_size // bands
    q_cols, k_cols = heads * head_size, head_size
    qkv_cols = q_cols + 2 * k_cols
    owned = experts // peers

    tokens_all = gather_blocks(own_tokens, "dp").reshape(-1, width)
    small = jnp.concatenate(
        [
            w_router,
            gain_attn[:, None],
            gain_moe[:, None],
            jnp.pad(gain_query, (0, band_rows - gain_rows))[:, None],
            jnp.pad(gain_key, (0, band_rows - gain_rows))[:, None],
        ],
        axis=1,
    )
    small = jnp.pad(small, ((0, 0), (0, 128 - small.shape[1])))
    packed = jnp.concatenate(
        [
            w_query.reshape(band_rows, bands, q_cols),
            w_key.reshape(band_rows, bands, k_cols),
            w_value.reshape(band_rows, bands, k_cols),
            jnp.broadcast_to(small[:, None], (band_rows, bands, 128)),
        ],
        axis=-1,
    ).transpose(1, 0, 2)
    swapped = lax.all_to_all(packed, "dp", split_axis=0, concat_axis=0, tiled=True)
    packed_all = lax.all_gather(swapped, "expert", axis=1, tiled=True).reshape(width, -1)
    qkv_w = packed_all[:, :qkv_cols]
    small_all = packed_all[:, qkv_cols:]
    router_full = small_all[:, :experts]
    attn_gain = small_all[:, experts].astype(F32)
    moe_gain = small_all[:, experts + 1].astype(F32)
    head_gains = small_all.reshape(bands * peers, band_rows, 128)[:, :gain_rows]
    query_gain = head_gains[:, :, experts + 2].reshape(-1).astype(F32)
    key_gain = head_gains[:, :, experts + 3].reshape(-1).astype(F32)
    out_w = lax.all_gather(after(w_output, packed_all), "expert", axis=0, tiled=True)
    shared = owned >= bands
    routes_all = lax.all_gather(routes[0], ("dp", "expert") if shared else "expert", axis=0)
    cot_all = lax.all_gather(after(cotangent[0], out_w), "expert", axis=0)

    core = lax.rem(peer, 2)
    expert_ids = jnp.arange(experts, dtype=jnp.int32)
    mask_all = jnp.any(routes_all[..., None] == expert_ids, axis=2)
    mask_own = lax.dynamic_slice_in_dim(mask_all, peer * owned, owned, axis=2)
    earlier = jnp.tril(jnp.ones((tok_count, tok_count), BF16), -1)
    ranks = dot("ts,bse->bet", earlier, mask_own.astype(BF16)).astype(jnp.int32)
    ranks_all = jnp.where(mask_own.transpose(0, 2, 1), ranks, -1)
    if shared:
        ordered = [lax.dynamic_slice_in_dim(ranks_all, band * peers, peers)]
        for step in range(1, bands):
            column = lax.dynamic_slice_in_dim(ranks_all, (band ^ step) * peers, peers)
            ordered += [by_core(column, core), by_core(column, 1 - core)]
        ranks_all = jnp.concatenate(ordered)
        mask_all = lax.dynamic_slice_in_dim(mask_all, band * peers, peers)
    slots = jnp.arange(CAP, dtype=jnp.int32)
    chosen = ranks_all[:peers, :, None, :] == slots[None, None, :, None]
    token_ranks = ranks_all[:peers].transpose(0, 2, 1)
    cot_pieces = swapped_columns(cot_all) if shared else []

    inputs = own_tokens.astype(F32)
    length = tokens_all.shape[0]
    half = head_size // 2
    frequency = ROPE_BASE ** (-jnp.arange(half, dtype=F32) * 2.0 / head_size)
    angles = jnp.arange(length, dtype=jnp.int32).astype(F32)[:, None] * frequency[None, :]
    cos = jnp.concatenate([jnp.cos(angles)] * 2, axis=-1)
    sin = jnp.concatenate([-jnp.sin(angles), jnp.sin(angles)], axis=-1)
    normed, query_pre, key_pre, query_low, key_low, value_low = make_qkv(
        tokens_all, attn_gain, packed_all, cos, sin, query_gain, key_gain
    )
    segment = segment_ids[0]
    attended_low, log_total = attend(query_low, key_low, value_low, segment)
    branch = dot("tm,md->td", attended_low, out_w).astype(BF16)
    branch = sum_blocks(branch.reshape(bands, tok_count, width), "dp")
    hidden = inputs + branch

    normed_moe_f, moe_pull = jax.vjp(norm_rows, hidden, moe_gain)
    normed_moe = normed_moe_f.astype(BF16)
    moe_all = lax.all_gather(normed_moe, "expert", axis=0)
    gates_all = masked_softmax(dot("btd,de->bte", moe_all, router_full), mask_all)
    gates_own = lax.dynamic_slice_in_dim(gates_all, peer * owned, owned, axis=2)
    slot_gates = jnp.sum(
        jnp.where(chosen, gates_own.transpose(0, 2, 1)[:, :, None, :], 0.0), axis=-1
    )

    row_gates = slot_gates.transpose(1, 0, 2).reshape(owned, peers * CAP, 1)
    cot_placed = place_rows(after(ranks_all[:peers], normed_moe), cot_all, 0, len(ranks_all))
    x_placed = place_rows(ranks_all[:peers], moe_all, 0, len(ranks_all))
    *own, slot_grads, rows_back, rows_out = own_experts(
        x_placed.reshape(owned, -1, width),
        cot_placed.reshape(owned, -1, width),
        row_gates,
        w_gate,
        w_up,
        w_down,
    )
    if not shared:
        active, gate_low, up_low = own
        arrived, cot_rows = (rows.reshape(owned, -1, width) for rows in (x_placed, cot_placed))
        expert_sums = lax.psum(
            (
                dot("erd,erf->edf", arrived, gate_low).astype(BF16),
                dot("erd,erf->edf", arrived, up_low).astype(BF16),
                dot("erf,erd->efd", active, cot_rows).astype(BF16),
            ),
            "dp",
        )
    rows_back = combine(token_ranks, rows_back)
    back = lax.psum_scatter(rows_back, "expert", scatter_dimension=0, tiled=True)[0]
    slot_grads = slot_grads.reshape(owned, peers, CAP).transpose(1, 0, 2)
    token_grads = jnp.sum(jnp.where(chosen, slot_grads[..., None], 0.0), axis=2)
    gate_grads = (
        lax.all_to_all(token_grads, "expert", split_axis=0, concat_axis=0, tiled=True)
        .reshape(experts, tok_count)
        .T
    )
    rows_out = combine(after(token_ranks, rows_back), rows_out)

    expert_sums = None if shared else expert_sums

    def next_expert(number, sums, *earlier):
        if not shared or number >= owned:
            return sums
        return expert_grads(
            x_placed.reshape(owned, -1, width),
            cot_placed.reshape(owned, -1, width),
            after(all_gates, *earlier),
            own,
            w_gate,
            w_up,
            w_down,
            number,
            sums,
        )

    if shared:
        later = after(ranks_all, rows_out)
        cot_placed = place_all(later, cot_pieces, cot_placed, peers)
        x_placed = place_all(later, swapped_columns(moe_all), x_placed, peers)
        all_gates = [slot_gates]
        for step in range(1, bands):
            got = traded(slot_gates, "dp", step)
            all_gates += [by_core(got, core), by_core(got, 1 - core)]
        all_gates = jnp.concatenate(all_gates).transpose(1, 0, 2).reshape(owned, -1, 1)
    expert_sums = next_expert(0, expert_sums, rows_out)

    own_gates = lax.dynamic_index_in_dim(gates_all, peer, 0, keepdims=False)
    grad_logits = own_gates * (
        gate_grads - jnp.sum(own_gates * gate_grads, axis=-1, keepdims=True)
    )
    grad_router_w = jnp.einsum("td,te->de", normed_moe.astype(F32), grad_logits, precision=PRECISE)
    grad_normed = back.astype(F32) + jnp.einsum(
        "te,de->td", grad_logits, router_full.astype(F32), precision=PRECISE
    )
    grad_hidden_n, grad_moe_gain = moe_pull(grad_normed)
    grad_hidden = cotangent[0].astype(F32) + grad_hidden_n
    grad_branch = grad_hidden.astype(BF16)
    branch_all = lax.all_gather(grad_branch, "dp", axis=0, tiled=True)
    expert_sums = next_expert(1, expert_sums, grad_branch)

    grad_attended = dot("td,md->tm", branch_all, out_w).astype(BF16)
    query_grad, key_grad, value_grad, head_grads = attend_back(
        query_low,
        key_low,
        value_low,
        grad_attended,
        log_total,
        segment,
        query_pre,
        key_pre,
        cos,
        sin,
        query_gain,
        key_gain,
    )
    qkv_grad = jnp.concatenate([query_grad, key_grad, value_grad], axis=1)
    grad_normed_attn = dot("tm,dm->td", qkv_grad, qkv_w).astype(BF16)
    expert_sums = next_expert(2, expert_sums, grad_normed_attn)
    grad_normed_attn = lax.psum_scatter(
        grad_normed_attn, "dp", scatter_dimension=0, tiled=True
    ).astype(F32)
    _, attn_pull = jax.vjp(norm_rows, inputs, attn_gain)
    grad_inputs_n, grad_attn_gain = attn_pull(grad_normed_attn)
    grad_tokens = grad_hidden + grad_inputs_n

    whole_gains = jnp.stack([grad_attn_gain, grad_moe_gain], axis=1)
    head_gains = head_grads[:2].T
    head_gains = jnp.pad(
        head_gains.reshape(bands * peers, gain_rows, 2),
        ((0, 0), (0, band_rows - gain_rows), (0, 0)),
    )
    small_grad = jnp.concatenate(
        [grad_router_w, whole_gains, head_gains.reshape(width, 2)], axis=1
    )
    small_grad = jnp.pad(small_grad, ((0, 0), (0, 128 - small_grad.shape[1])))
    band_qkv = jnp.concatenate([dot("td,tm->dm", normed, qkv_grad), small_grad], axis=1)
    band_qkv = band_qkv.astype(BF16).reshape(bands, peers, band_rows, -1).transpose(1, 0, 2, 3)
    expert_sums = next_expert(3, expert_sums, band_qkv)
    for number in range(4, owned):
        expert_sums = next_expert(number, expert_sums)
    band_qkv = lax.psum_scatter(
        band_qkv.reshape(width, -1), "expert", scatter_dimension=0, tiled=True
    ).reshape(bands, band_rows, -1)
    band_qkv = lax.all_to_all(band_qkv, "dp", split_axis=0, concat_axis=0, tiled=True).transpose(
        1, 0, 2
    )
    grad_query = band_qkv[:, :, :q_cols].astype(F32).reshape(band_rows, -1)
    grad_key = band_qkv[:, :, q_cols : q_cols + k_cols].astype(F32).reshape(band_rows, -1)
    grad_value = band_qkv[:, :, q_cols + k_cols : qkv_cols].astype(F32).reshape(band_rows, -1)
    smaller = jnp.sum(band_qkv[:, :, qkv_cols:].astype(F32), axis=1)
    grad_output = sum_peers(
        dot("tm,td->md", attended_low, branch_all).astype(BF16).reshape(peers, -1, width)
    )

    moe_sum = sum_peers(rows_out)
    block_out = (hidden + moe_sum).astype(BF16)
    return (
        block_out[None],
        grad_tokens[None],
        grad_query,
        grad_key,
        grad_value,
        grad_output,
        smaller[:, :experts],
        smaller[:, experts],
        smaller[:, experts + 1],
        smaller[:gain_rows, experts + 2],
        smaller[:gain_rows, experts + 3],
        expert_sums[0].astype(F32),
        expert_sums[1].astype(F32),
        expert_sums[2].astype(F32),
    )


def solution(mesh):
    both = ("dp", "expert")
    return jax.shard_map(
        on_device,
        mesh=mesh,
        in_specs=(
            P("expert", "dp", None),
            P("expert", None),
            P("expert", "dp", None),
            P(both, None),
            P(both, None),
            P(both, None),
            P(both, None),
            P(both, None),
            P(both),
            P(both),
            P(both),
            P(both),
            P("expert", None, None),
            P("expert", None, None),
            P("expert", None, None),
            P("expert", "dp", None),
        ),
        out_specs=(
            P("expert", "dp", None),
            P("expert", "dp", None),
            P(both, None),
            P(both, None),
            P(both, None),
            P(both, None),
            P(both, None),
            P(both),
            P(both),
            P(both),
            P(both),
            P("expert", None, None),
            P("expert", None, None),
            P("expert", None, None),
        ),
        check_vma=False,
    )
```

```python
import jax
import jax.numpy as jnp
from jax import lax
from jax.experimental import pallas as pl
from jax.experimental.pallas import tpu as pltpu
from jax.sharding import PartitionSpec as P

CAP = 80
Q_BLOCK = 256
HIDDEN_TILE = 256
OWN_ROWS = 8 * CAP
WIDTH_TILE = 512
SIDE = 128
ROW_PARTS = 2
VMEM_BYTES = 60 << 20


EPSILON = 1e-06
ROPE_BASE = 1000000.0
PRECISE = lax.Precision.HIGHEST
F32 = jnp.float32
BF16 = jnp.bfloat16
FREE = pl.CostEstimate(flops=0, bytes_accessed=0, transcendentals=0)


def norm_rows(values, gain_row):
    return (
        values * lax.rsqrt(jnp.mean(values * values, axis=-1, keepdims=True) + EPSILON) * gain_row
    )


def activate(gate_vals, up_vals):
    return gate_vals * jax.nn.sigmoid(gate_vals) * up_vals


def masked_softmax(logits, mask):
    kept = jnp.where(mask, logits, -jnp.inf)
    largest = jnp.max(kept, axis=-1, keepdims=True)
    raised = jnp.where(mask, jnp.exp(logits - largest), 0.0)
    return raised / jnp.sum(raised, axis=-1, keepdims=True)


def nothing(*refs):
    del refs


def after(value, *others):
    anywhere = pl.BlockSpec(memory_space=pl.ANY)
    return pl.pallas_call(
        nothing,
        out_shape=jax.ShapeDtypeStruct(value.shape, value.dtype),
        in_specs=[anywhere] * (1 + len(others)),
        out_specs=anywhere,
        input_output_aliases={0: 0},
    )(value, *others)


def shifted(value, axis, step):
    count = lax.axis_size(axis)
    return lax.ppermute(value, axis, [(i, (i + step) % count) for i in range(count)])


def traded(value, axis, step):
    return lax.ppermute(value, axis, [(i, i ^ step) for i in range(lax.axis_size(axis))])


def gather_blocks(own, axis):
    count, me = lax.axis_size(axis), lax.axis_index(axis)
    whole = jnp.zeros((count, *own.shape), own.dtype)
    whole = lax.dynamic_update_index_in_dim(whole, own, me, 0)
    for step in range(1, count):
        whole = lax.dynamic_update_index_in_dim(whole, traded(own, axis, step), me ^ step, 0)
    return whole


def gather_peers(own):
    me = lax.axis_index("expert")
    chips, chip, core = lax.axis_size("expert") // 2, lax.div(me, 2), lax.rem(me, 2)
    mine = jnp.zeros((chips, *own.shape), own.dtype)
    mine = lax.dynamic_update_index_in_dim(mine, own, chip, 0)
    for step in range(1, chips):
        got = traded(own, "expert", 2 * step)
        mine = lax.dynamic_update_index_in_dim(mine, got, chip ^ step, 0)
    twin = traded(mine, "expert", 1)
    first = core == 0
    return jnp.stack([jnp.where(first, mine, twin), jnp.where(first, twin, mine)], axis=1)


def sum_blocks(blocks, axis):
    count, me = lax.axis_size(axis), lax.axis_index(axis)
    total = lax.dynamic_index_in_dim(blocks, me, 0, keepdims=False).astype(F32)
    for step in range(1, count):
        sent = lax.dynamic_index_in_dim(blocks, me ^ step, 0, keepdims=False)
        total = total + traded(sent, axis, step).astype(F32)
    return total


def sum_peers(blocks):
    count, me = lax.axis_size("expert"), lax.axis_index("expert")
    core, chip, chips = lax.rem(me, 2), lax.div(me, 2), count // 2
    paired = blocks.reshape(chips, 2, *blocks.shape[1:])
    sent = lax.dynamic_index_in_dim(paired, 1 - core, 1, keepdims=False)
    kept = lax.dynamic_index_in_dim(paired, core, 1, keepdims=False)
    got = lax.ppermute(sent, "expert", [(i, i ^ 1) for i in range(count)])
    halves = (kept.astype(F32) + got.astype(F32)).astype(BF16)
    total = lax.dynamic_index_in_dim(halves, chip, 0, keepdims=False).astype(F32)
    for step in range(1, chips):
        sent = lax.dynamic_index_in_dim(halves, lax.rem(chip + step, chips), 0, keepdims=False)
        total = total + shifted(sent, "expert", 2 * step).astype(F32)
    return total


def dot(spec, left, right):
    return jnp.einsum(spec, left, right, preferred_element_type=F32)


def swapped_columns(own):
    peer, bands = lax.axis_index("expert"), lax.axis_size("dp")
    mine = by_core(own, lax.rem(peer, 2))
    pieces = []
    for step in range(1, bands):
        got = traded(mine, "dp", step)
        pieces += [got, traded(got, "expert", 1)]
    return pieces


def relayed_columns(own):
    mine = by_core(own, lax.rem(lax.axis_index("expert"), 2))
    half = mine.shape[0] // 2
    first, second = mine[:half], mine[half:]
    first_x, second_y = traded(first, "dp", 1), traded(second, "dp", 2)
    second_x, first_y = traded(second, "dp", 1), traded(first, "dp", 2)
    first_far, second_far = traded(first_x, "dp", 2), traded(second_y, "dp", 1)
    pieces = []
    for pair in ((first_x, second_x), (first_y, second_y), (first_far, second_far)):
        pieces += [*pair, *(traded(piece, "expert", 1) for piece in pair)]
    return pieces


def block_ranks(routes, peer, owned, experts):
    chosen = jnp.any(routes[..., None] == jnp.arange(experts, dtype=jnp.int32), axis=2)
    chosen = lax.dynamic_slice_in_dim(chosen, peer * owned, owned, axis=2)
    tok_count = chosen.shape[1]
    earlier = jnp.tril(jnp.ones((tok_count, tok_count), BF16), -1)
    ranks = dot("ts,bse->bet", earlier, chosen.astype(BF16)).astype(jnp.int32)
    return jnp.where(chosen.transpose(0, 2, 1), ranks, -1)


def slot_values(ranks, values):
    slots = jnp.arange(CAP, dtype=jnp.int32)
    chosen = ranks[:, :, None, :] == slots[None, None, :, None]
    return jnp.sum(jnp.where(chosen, values.transpose(0, 2, 1)[:, :, None, :], 0.0), axis=-1)


def by_core(values, core):
    paired = values.reshape(-1, 2, *values.shape[1:])
    return lax.dynamic_index_in_dim(paired, core, 1, keepdims=False)


def place_kernel(rank_ref, block_ref, *rest):
    rows_ref = rest[-1]
    count, owned, tok_count = rank_ref.shape
    slots = lax.broadcasted_iota(jnp.int32, (CAP, tok_count), 0)
    width = block_ref.shape[-1]
    for block in range(count):
        ranks = rank_ref[block]
        hot = jnp.concatenate([ranks[e : e + 1] == slots for e in range(owned)], axis=0)
        hot = jnp.where(hot, 1.0, 0.0).astype(BF16)
        for start in range(0, width, WIDTH_TILE):
            cols = slice(start, start + WIDTH_TILE)
            rows = jnp.dot(hot, block_ref[block, :, cols], preferred_element_type=F32)
            rows_ref[:, block, :, cols] = rows.astype(BF16).reshape(owned, CAP, WIDTH_TILE)


def place_rows(ranks, blocks, start, total, buffer=None):
    count, owned, tok_count = ranks.shape
    width = blocks.shape[-1] - SIDE
    several = 2
    first = start // several
    in_specs = [
        pl.BlockSpec((several, owned, tok_count), lambda b: (b, 0, 0)),
        pl.BlockSpec((several, tok_count, width), lambda b: (b, 0, 0)),
    ]
    given = (ranks, blocks)
    if buffer is not None:
        in_specs.append(pl.BlockSpec(memory_space=pl.ANY))
        given += (buffer,)
    return pl.pallas_call(
        place_kernel,
        grid=(count // several,),
        out_shape=jax.ShapeDtypeStruct((owned, total, CAP, width), BF16),
        in_specs=in_specs,
        out_specs=pl.BlockSpec((owned, several, CAP, width), lambda b: (0, first + b, 0, 0)),
        input_output_aliases={} if buffer is None else {2: 0},
        compiler_params=pltpu.CompilerParams(vmem_limit_bytes=VMEM_BYTES),
        cost_estimate=FREE,
    )(*given)


def combine_kernel(rank_ref, rows_ref, out_ref):
    tok_count, owned = rank_ref.shape[1:]
    slots = owned * CAP
    width = out_ref.shape[-1]
    lane = lax.broadcasted_iota(jnp.int32, (tok_count, slots), 1)
    hot = jnp.zeros((tok_count, slots), F32)
    for e in range(owned):
        ranks = rank_ref[0, :, e : e + 1]
        hot = jnp.where((ranks >= 0) & (lane == ranks + e * CAP), 1.0, hot)
    hot = hot.astype(BF16)
    for start in range(0, width, WIDTH_TILE):
        cols = slice(start, start + WIDTH_TILE)
        rows = rows_ref[:, 0, :, cols].reshape(slots, WIDTH_TILE)
        out_ref[0, :, cols] = jnp.dot(hot, rows, preferred_element_type=F32).astype(BF16)


def combine(ranks, rows):
    count, tok_count, owned = ranks.shape
    width = rows.shape[-1]
    return pl.pallas_call(
        combine_kernel,
        grid=(count,),
        out_shape=jax.ShapeDtypeStruct((count, tok_count, width), BF16),
        in_specs=[
            pl.BlockSpec((1, tok_count, owned), lambda b: (b, 0, 0)),
            pl.BlockSpec((owned, 1, CAP, width), lambda b: (0, b, 0, 0)),
        ],
        out_specs=pl.BlockSpec((1, tok_count, width), lambda b: (b, 0, 0)),
        compiler_params=pltpu.CompilerParams(vmem_limit_bytes=VMEM_BYTES),
        cost_estimate=FREE,
    )(ranks, rows.reshape(owned, count, CAP, width))


def place_all(ranks, pieces, buffer, start):
    total, done = buffer.shape[1], 0
    for piece in pieces:
        count = piece.shape[0]
        buffer = place_rows(ranks[done : done + count], piece, start + done, total, buffer)
        done += count
    return buffer


def dot_nt(left, right):
    return lax.dot_general(left, right, (((1,), (1,)), ((), ())), preferred_element_type=F32)


def hidden_grads(x, c, gates, wg_ref, wu_ref, wd_ref):
    gate_in = jnp.dot(x, wg_ref[0], preferred_element_type=F32)
    up_in = jnp.dot(x, wu_ref[0], preferred_element_type=F32)
    raw = dot_nt(c, wd_ref[0])
    sig = 1.0 / (1.0 + jnp.exp(-gate_in))
    silu = gate_in * sig
    active = silu * up_in
    grad = raw * gates
    gate_grad = grad * up_in * (sig + silu * (1.0 - sig))
    up_grad = grad * silu
    return (active * gates).astype(BF16), gate_grad.astype(BF16), up_grad.astype(BF16), active * raw


def own_kernel(
    x_ref,
    c_ref,
    g_ref,
    wg_ref,
    wu_ref,
    wd_ref,
    active_ref,
    gate_ref,
    up_ref,
    slot_ref,
    back_ref,
    out_ref,
    back_sum,
    out_sum,
):
    width = x_ref.shape[-1]
    step = pl.program_id(2)
    active, gate_grad, up_grad, slot = hidden_grads(
        x_ref[0], c_ref[0], g_ref[0], wg_ref, wu_ref, wd_ref
    )
    active_ref[0] = active
    gate_ref[0] = gate_grad
    up_ref[0] = up_grad
    slot = jnp.sum(slot, axis=1, keepdims=True)
    slot_ref[0] = jnp.where(step == 0, slot, slot_ref[0] + slot)
    for start in range(0, width, WIDTH_TILE):
        cols = slice(start, start + WIDTH_TILE)
        rows = dot_nt(gate_ref[0], wg_ref[0, cols, :]) + dot_nt(up_ref[0], wu_ref[0, cols, :])
        back_sum[:, cols] = jnp.where(step == 0, rows, back_sum[:, cols] + rows)
        rows = jnp.dot(active_ref[0], wd_ref[0, :, cols], preferred_element_type=F32)
        out_sum[:, cols] = jnp.where(step == 0, rows, out_sum[:, cols] + rows)

    @pl.when(step == pl.num_programs(2) - 1)
    def _():
        back_ref[0] = back_sum[...].astype(BF16)
        out_ref[0] = out_sum[...].astype(BF16)


def own_experts(x_rows, c_rows, gates, w_gate, w_up, w_down):
    owned, rows = gates.shape[:2]
    width = x_rows.shape[-1]
    hidden = w_down.shape[1]
    tile = HIDDEN_TILE
    some = min(rows, OWN_ROWS)
    whole = pl.BlockSpec((1, some, width), lambda e, r, f: (e, r, 0))
    column = pl.BlockSpec((1, some, 1), lambda e, r, f: (e, r, 0))
    part = pl.BlockSpec((1, some, tile), lambda e, r, f: (e, r, f))
    inward = pl.BlockSpec((1, width, tile), lambda e, r, f: (e, 0, f))
    outward = pl.BlockSpec((1, tile, width), lambda e, r, f: (e, f, 0))
    return pl.pallas_call(
        own_kernel,
        grid=(owned, rows // some, hidden // tile),
        in_specs=[whole, whole, column, inward, inward, outward],
        out_specs=[part, part, part, column, whole, whole],
        out_shape=[jax.ShapeDtypeStruct((owned, rows, hidden), BF16)] * 3
        + [jax.ShapeDtypeStruct((owned, rows, 1), F32)]
        + [jax.ShapeDtypeStruct((owned, rows, width), BF16)] * 2,
        scratch_shapes=[pltpu.VMEM((some, width), F32)] * 2,
        compiler_params=pltpu.CompilerParams(vmem_limit_bytes=VMEM_BYTES),
        cost_estimate=FREE,
    )(x_rows, c_rows, gates, w_gate, w_up, w_down)


def grads_kernel(
    x_ref, c_ref, g_ref, active_ref, gate_ref, up_ref, wg_ref, wu_ref, wd_ref, *rest
):
    dg_ref, du_ref, dd_ref, sums, pair, actives = rest[-6:]
    tile = HIDDEN_TILE
    rows, width = x_ref.shape[1:]
    own = active_ref.shape[1]
    step = pl.program_id(1)

    def keep(start, active, gate_grad, up_grad):
        part = slice(start, start + own)
        actives[:, part] = active.T
        pair[:tile, part] = gate_grad.T
        pair[tile:, part] = up_grad.T

    def work_out(start):
        part = slice(start, start + own)
        active, gate_grad, up_grad, _ = hidden_grads(
            x_ref[0, part], c_ref[0, part], g_ref[0, part], wg_ref, wu_ref, wd_ref
        )
        keep(start, active, gate_grad, up_grad)

    @pl.when(step == 0)
    def _():
        keep(0, active_ref[0], gate_ref[0], up_ref[0])

    @pl.when(step > 0)
    def _():
        work_out(0)

    for start in range(own, rows, own):
        work_out(start)

    @pl.loop(0, width // WIDTH_TILE)
    def _(c):
        cols = pl.ds(pl.multiple_of(c * WIDTH_TILE, WIDTH_TILE), WIDTH_TILE)
        grads = jnp.dot(pair[...], x_ref[0, :, cols], preferred_element_type=F32)
        sums[:, cols] = jnp.where(step == 0, grads, sums[:, cols] + grads)
        grads = jnp.dot(actives[...], c_ref[0, :, cols], preferred_element_type=F32)
        dd_ref[0, :, cols] = jnp.where(step == 0, grads, dd_ref[0, :, cols] + grads)

    @pl.when(step == pl.num_programs(1) - 1)
    def _():
        same = lax.broadcasted_iota(jnp.int32, (tile, tile), 0) == lax.broadcasted_iota(
            jnp.int32, (tile, tile), 1
        )
        same = jnp.where(same, 1.0, 0.0).astype(BF16)

        @pl.loop(0, width // tile)
        def _(c):
            cols = pl.ds(pl.multiple_of(c * tile, tile), tile)
            dg_ref[0, cols, :] = dot_nt(same, sums[:tile, cols].astype(BF16))
            du_ref[0, cols, :] = dot_nt(same, sums[tile:, cols].astype(BF16))


def expert_grads(x_rows, c_rows, gates, own, w_gate, w_up, w_down, expert, buffers=None):
    owned, rows, width = x_rows.shape
    hidden = w_down.shape[1]
    tile, parts = HIDDEN_TILE, ROW_PARTS
    part, own_rows = rows // parts, own[0].shape[1]
    shapes = [(owned, width, hidden)] * 2 + [(owned, hidden, width)]
    in_specs = [
        pl.BlockSpec((1, part, width), lambda f, r: (expert, r, 0)),
        pl.BlockSpec((1, part, width), lambda f, r: (expert, r, 0)),
        pl.BlockSpec((1, part, 1), lambda f, r: (expert, r, 0)),
        *[pl.BlockSpec((1, own_rows, tile), lambda f, r: (expert, 0, f))] * 3,
        pl.BlockSpec((1, width, tile), lambda f, r: (expert, 0, f)),
        pl.BlockSpec((1, width, tile), lambda f, r: (expert, 0, f)),
        pl.BlockSpec((1, tile, width), lambda f, r: (expert, f, 0)),
    ]
    given = (x_rows, c_rows, gates, *own, w_gate, w_up, w_down)
    aliases = {}
    if buffers is not None:
        aliases = {len(given) + i: i for i in range(3)}
        in_specs += [pl.BlockSpec(memory_space=pl.ANY)] * 3
        given += tuple(buffers)
    return pl.pallas_call(
        grads_kernel,
        grid=(hidden // tile, parts),
        out_shape=[jax.ShapeDtypeStruct(shape, F32) for shape in shapes],
        in_specs=in_specs,
        out_specs=[
            pl.BlockSpec((1, width, tile), lambda f, r: (expert, 0, f)),
            pl.BlockSpec((1, width, tile), lambda f, r: (expert, 0, f)),
            pl.BlockSpec((1, tile, width), lambda f, r: (expert, f, 0)),
        ],
        scratch_shapes=[
            pltpu.VMEM((2 * tile, width), F32),
            pltpu.VMEM((2 * tile, part), BF16),
            pltpu.VMEM((tile, part), BF16),
        ],
        input_output_aliases=aliases,
        compiler_params=pltpu.CompilerParams(vmem_limit_bytes=VMEM_BYTES),
        cost_estimate=FREE,
    )(*given)


def turn(values, cos, sin):
    return values * cos + pltpu.roll(values, values.shape[-1] // 2, 1) * sin


def qkv_kernel(
    tok_ref,
    gain_ref,
    w_ref,
    cos_ref,
    sin_ref,
    gq_ref,
    gk_ref,
    normed_ref,
    qpre_ref,
    kpre_ref,
    qrot_ref,
    krot_ref,
    value_ref,
):
    head = cos_ref.shape[1]
    heads = qpre_ref.shape[1] // head
    normed = norm_rows(tok_ref[...].astype(F32), gain_ref[...]).astype(BF16)
    normed_ref[...] = normed
    cos, sin = cos_ref[...], sin_ref[...]
    for pair in range(0, heads, 2):
        cols = slice(pair * head, (pair + 2) * head)
        pre = jnp.dot(normed, w_ref[:, cols], preferred_element_type=F32)
        qpre_ref[:, cols] = pre
        for h in range(2):
            one = slice(h * head, (h + 1) * head)
            rot = turn(norm_rows(pre[:, one], gq_ref[...]), cos, sin)
            qrot_ref[:, (pair + h) * head : (pair + h + 1) * head] = rot.astype(BF16)
    cols = slice(heads * head, (heads + 2) * head)
    pre = jnp.dot(normed, w_ref[:, cols], preferred_element_type=F32)
    kpre_ref[...] = pre[:, :head]
    krot_ref[...] = turn(norm_rows(pre[:, :head], gk_ref[...]), cos, sin).astype(BF16)
    value_ref[...] = pre[:, head:].astype(BF16)


def make_qkv(tokens, gain, weight, cos, sin, query_gain, key_gain):
    length, width = tokens.shape
    head = cos.shape[1]
    cols = weight.shape[1]
    q_cols = cols - 3 * head
    block = Q_BLOCK

    def rows(size):
        return pl.BlockSpec((block, size), lambda i: (i, 0))

    def fixed(*shape):
        return pl.BlockSpec(shape, lambda i: (0, 0))

    return pl.pallas_call(
        qkv_kernel,
        grid=(length // block,),
        in_specs=[
            rows(width),
            fixed(1, width),
            fixed(width, cols),
            rows(head),
            rows(head),
            fixed(1, head),
            fixed(1, head),
        ],
        out_specs=[rows(width), rows(q_cols), rows(head), rows(q_cols), rows(head), rows(head)],
        out_shape=[
            jax.ShapeDtypeStruct((length, width), BF16),
            jax.ShapeDtypeStruct((length, q_cols), F32),
            jax.ShapeDtypeStruct((length, head), F32),
            jax.ShapeDtypeStruct((length, q_cols), BF16),
            jax.ShapeDtypeStruct((length, head), BF16),
            jax.ShapeDtypeStruct((length, head), BF16),
        ],
        compiler_params=pltpu.CompilerParams(vmem_limit_bytes=VMEM_BYTES),
        cost_estimate=FREE,
    )(tokens, gain[None], weight, cos, sin, query_gain[None], key_gain[None])


def masked_scores(q_ref, k_ref, seg_row_ref, seg_col_ref, block, keys):
    size = q_ref.shape[0]
    scores = dot_nt(k_ref[:keys], q_ref[...]) * q_ref.shape[1] ** (-0.5)
    key_at = lax.broadcasted_iota(jnp.int32, (keys, size), 0)
    query_at = lax.broadcasted_iota(jnp.int32, (keys, size), 1) + block * size
    allowed = (key_at <= query_at) & (seg_col_ref[:keys] == seg_row_ref[...])
    return jnp.where(allowed, scores, -1e30)


def attend_kernel(q_ref, k_ref, vt_ref, seg_row_ref, seg_col_ref, out_ref, log_ref):
    size = q_ref.shape[0]
    blocks = k_ref.shape[0] // size
    for block in range(blocks):

        @pl.when(pl.program_id(1) == block)
        def _(block=block):
            keys = (block + 1) * size
            scores = masked_scores(q_ref, k_ref, seg_row_ref, seg_col_ref, block, keys)
            largest = jnp.max(scores, axis=0, keepdims=True)
            raised = jnp.exp(scores - largest)
            total = jnp.sum(raised, axis=0, keepdims=True)
            weights = (raised * (1.0 / total)).astype(BF16)
            out = jnp.dot(vt_ref[:, :keys], weights, preferred_element_type=F32)
            out_ref[...] = out.T.astype(BF16)
            log_ref[0] = largest + jnp.log(total)


def attend(query, key, value, segment):
    length, cols = query.shape
    head = key.shape[1]
    block = Q_BLOCK
    heads = cols // head
    return pl.pallas_call(
        attend_kernel,
        grid=(heads, length // block),
        in_specs=[
            pl.BlockSpec((block, head), lambda h, i: (i, h)),
            pl.BlockSpec((length, head), lambda h, i: (0, 0)),
            pl.BlockSpec((head, length), lambda h, i: (0, 0)),
            pl.BlockSpec((1, block), lambda h, i: (0, i)),
            pl.BlockSpec((length, 1), lambda h, i: (0, 0)),
        ],
        out_specs=[
            pl.BlockSpec((block, head), lambda h, i: (i, h)),
            pl.BlockSpec((1, 1, block), lambda h, i: (h, 0, i)),
        ],
        out_shape=[
            jax.ShapeDtypeStruct((length, cols), BF16),
            jax.ShapeDtypeStruct((heads, 1, length), F32),
        ],
        compiler_params=pltpu.CompilerParams(vmem_limit_bytes=VMEM_BYTES),
        cost_estimate=FREE,
    )(query, key, value.T, segment[None], segment[:, None])


def attend_back_kernel(
    q_ref,
    k_ref,
    kt_ref,
    v_ref,
    do_ref,
    log_ref,
    seg_row_ref,
    seg_col_ref,
    qpre_ref,
    kpre_ref,
    cos_ref,
    sin_ref,
    gq_ref,
    gk_ref,
    dq_ref,
    dk_ref,
    dv_ref,
    dgain_ref,
    key_sum,
    value_sum,
):
    size, head = q_ref.shape
    blocks = k_ref.shape[0] // size
    scale = head ** (-0.5)
    first = (pl.program_id(0) == 0) & (pl.program_id(1) == 0)
    last = (pl.program_id(0) == pl.num_programs(0) - 1) & (pl.program_id(1) == blocks - 1)

    @pl.when(first)
    def _():
        key_sum[...] = jnp.zeros_like(key_sum)
        value_sum[...] = jnp.zeros_like(value_sum)
        dgain_ref[...] = jnp.zeros_like(dgain_ref)

    def pull(grad, pre, gain, cos, sin):
        grad = grad.astype(BF16).astype(F32)
        turned = grad * cos + pltpu.roll(grad * sin, head // 2, 1)
        scale_row = lax.rsqrt(jnp.mean(pre * pre, axis=-1, keepdims=True) + EPSILON)
        unit = pre * scale_row
        gain_grad = jnp.sum(turned * unit, axis=0, keepdims=True)
        turned = turned * gain
        inner = jnp.mean(turned * unit, axis=-1, keepdims=True)
        return scale_row * (turned - unit * inner), gain_grad

    for block in range(blocks):

        @pl.when(pl.program_id(1) == block)
        def _(block=block):
            keys = (block + 1) * size
            rows = slice(block * size, keys)
            scores = masked_scores(q_ref, k_ref, seg_row_ref, seg_col_ref, block, keys)
            weights = jnp.exp(scores - log_ref[0])
            grads = dot_nt(v_ref[:keys], do_ref[...])
            inner = jnp.sum(weights * grads, axis=0, keepdims=True)
            score_grads = (weights * (grads - inner)).astype(BF16)
            value_sum[:keys] += jnp.dot(
                weights.astype(BF16), do_ref[...], preferred_element_type=F32
            )
            key_sum[:keys] += jnp.dot(score_grads, q_ref[...], preferred_element_type=F32)
            query_grad = jnp.dot(kt_ref[:, :keys], score_grads, preferred_element_type=F32)
            pre_grad, gain_grad = pull(
                query_grad.T * scale, qpre_ref[...], gq_ref[...], cos_ref[rows], sin_ref[rows]
            )
            dq_ref[...] = pre_grad.astype(BF16)
            dgain_ref[0:1] += gain_grad

    @pl.when(last)
    def _():
        pre_grad, gain_grad = pull(
            key_sum[...] * scale, kpre_ref[...], gk_ref[...], cos_ref[...], sin_ref[...]
        )
        dk_ref[...] = pre_grad.astype(BF16)
        dgain_ref[1:2] = gain_grad
        dv_ref[...] = value_sum[...].astype(BF16)


def attend_back(query, key, value, grad, logs, segment, qpre, kpre, cos, sin, gq, gk):
    length, cols = query.shape
    head = key.shape[1]
    block = Q_BLOCK
    heads = cols // head
    tile = pl.BlockSpec((block, head), lambda h, i: (i, h))

    def fixed(*shape):
        return pl.BlockSpec(shape, lambda h, i: (0, 0))

    return pl.pallas_call(
        attend_back_kernel,
        grid=(heads, length // block),
        in_specs=[
            tile,
            fixed(length, head),
            fixed(head, length),
            fixed(length, head),
            tile,
            pl.BlockSpec((1, 1, block), lambda h, i: (h, 0, i)),
            pl.BlockSpec((1, block), lambda h, i: (0, i)),
            fixed(length, 1),
            tile,
            fixed(length, head),
            fixed(length, head),
            fixed(length, head),
            fixed(1, head),
            fixed(1, head),
        ],
        out_specs=[tile, fixed(length, head), fixed(length, head), fixed(8, head)],
        out_shape=[
            jax.ShapeDtypeStruct((length, cols), BF16),
            jax.ShapeDtypeStruct((length, head), BF16),
            jax.ShapeDtypeStruct((length, head), BF16),
            jax.ShapeDtypeStruct((8, head), F32),
        ],
        scratch_shapes=[pltpu.VMEM((length, head), F32), pltpu.VMEM((length, head), F32)],
        compiler_params=pltpu.CompilerParams(vmem_limit_bytes=VMEM_BYTES),
        cost_estimate=FREE,
    )(
        query,
        key,
        key.T,
        value,
        grad,
        logs,
        segment[None],
        segment[:, None],
        qpre,
        kpre,
        cos,
        sin,
        gq[None],
        gk[None],
    )


def on_device(
    tokens,
    segment_ids,
    routes,
    w_query,
    w_key,
    w_value,
    w_output,
    w_router,
    gain_attn,
    gain_moe,
    gain_query,
    gain_key,
    w_gate,
    w_up,
    w_down,
    cotangent,
):
    bands, peers = lax.axis_size("dp"), lax.axis_size("expert")
    band, peer = lax.axis_index("dp"), lax.axis_index("expert")
    own_tokens = tokens[0]
    tok_count, width = own_tokens.shape
    band_rows = w_query.shape[0]
    experts = w_router.shape[1]
    gain_rows = gain_query.shape[0]
    head_size = gain_rows * bands * peers
    heads = w_query.shape[1] // head_size // bands
    q_cols, k_cols = heads * head_size, head_size
    qkv_cols = q_cols + 2 * k_cols
    owned = experts // peers

    tokens_all = gather_blocks(own_tokens, "dp").reshape(-1, width)
    small = jnp.concatenate(
        [
            w_router,
            gain_attn[:, None],
            gain_moe[:, None],
            jnp.pad(gain_query, (0, band_rows - gain_rows))[:, None],
            jnp.pad(gain_key, (0, band_rows - gain_rows))[:, None],
        ],
        axis=1,
    )
    small = jnp.pad(small, ((0, 0), (0, 128 - small.shape[1])))
    packed = jnp.concatenate(
        [
            w_query.reshape(band_rows, bands, q_cols),
            w_key.reshape(band_rows, bands, k_cols),
            w_value.reshape(band_rows, bands, k_cols),
            jnp.broadcast_to(small[:, None], (band_rows, bands, 128)),
        ],
        axis=-1,
    ).transpose(1, 0, 2)
    swapped = lax.all_to_all(packed, "dp", split_axis=0, concat_axis=0, tiled=True)
    packed_all = lax.all_gather(swapped, "expert", axis=1, tiled=True).reshape(width, -1)
    qkv_w = packed_all[:, :qkv_cols]
    small_all = packed_all[:, qkv_cols:]
    router_full = small_all[:, :experts]
    attn_gain = small_all[:, experts].astype(F32)
    moe_gain = small_all[:, experts + 1].astype(F32)
    head_gains = small_all.reshape(bands * peers, band_rows, 128)[:, :gain_rows]
    query_gain = head_gains[:, :, experts + 2].reshape(-1).astype(F32)
    key_gain = head_gains[:, :, experts + 3].reshape(-1).astype(F32)
    out_w = gather_peers(w_output).reshape(-1, width)
    shared = owned >= bands
    top = routes.shape[-1]

    def beside(rows, *sides):
        used = sum(side.shape[-1] for side in sides)
        filler = jnp.zeros((tok_count, SIDE - used), BF16)
        return jnp.concatenate([rows, *(side.astype(BF16) for side in sides), filler], axis=1)

    def side_routes(blocks):
        return blocks[..., width : width + top].astype(jnp.int32)

    def side_gates(blocks):
        gates = blocks[..., width : width + experts].astype(F32)
        gates = gates + blocks[..., width + experts : width + 2 * experts].astype(F32)
        return lax.dynamic_slice_in_dim(gates, peer * owned, owned, axis=2)

    cot_all = lax.all_gather(beside(after(cotangent[0], packed_all), routes[0]), "expert", axis=0)
    if shared:
        cot_pieces = relayed_columns(cot_all) if bands == 4 else swapped_columns(cot_all)

    inputs = own_tokens.astype(F32)
    length = tokens_all.shape[0]
    half = head_size // 2
    frequency = ROPE_BASE ** (-jnp.arange(half, dtype=F32) * 2.0 / head_size)
    angles = jnp.arange(length, dtype=jnp.int32).astype(F32)[:, None] * frequency[None, :]
    cos = jnp.concatenate([jnp.cos(angles)] * 2, axis=-1)
    sin = jnp.concatenate([-jnp.sin(angles), jnp.sin(angles)], axis=-1)
    normed, query_pre, key_pre, query_low, key_low, value_low = make_qkv(
        tokens_all, attn_gain, packed_all, cos, sin, query_gain, key_gain
    )
    segment = segment_ids[0]
    attended_low, log_total = attend(query_low, key_low, value_low, segment)
    branch = dot("tm,md->td", attended_low, out_w).astype(BF16)
    branch = sum_blocks(branch.reshape(bands, tok_count, width), "dp")
    hidden = inputs + branch

    normed_moe_f, moe_pull = jax.vjp(norm_rows, hidden, moe_gain)
    normed_moe = normed_moe_f.astype(BF16)
    mask = jnp.any(routes[0][..., None] == jnp.arange(experts, dtype=jnp.int32), axis=1)
    own_gates = masked_softmax(dot("td,de->te", normed_moe, router_full), mask)
    high = own_gates.astype(BF16)
    low = own_gates - high.astype(F32)
    moe_all = lax.all_gather(beside(normed_moe, high, low), "expert", axis=0)
    own_ranks = after(block_ranks(side_routes(cot_all), peer, owned, experts), normed_moe)
    token_ranks = own_ranks.transpose(0, 2, 1)
    total = peers * (bands if shared else 1)
    cot_placed = place_rows(own_ranks, cot_all, 0, total)
    slot_gates = slot_values(own_ranks, side_gates(moe_all))
    row_gates = slot_gates.transpose(1, 0, 2).reshape(owned, peers * CAP, 1)
    x_placed = place_rows(own_ranks, moe_all, 0, total)
    *own, slot_grads, rows_back, rows_out = own_experts(
        x_placed.reshape(owned, -1, width),
        cot_placed.reshape(owned, -1, width),
        row_gates,
        w_gate,
        w_up,
        w_down,
    )
    if not shared:
        active, gate_low, up_low = own
        arrived, cot_rows = (rows.reshape(owned, -1, width) for rows in (x_placed, cot_placed))
        expert_sums = lax.psum(
            (
                dot("erd,erf->edf", arrived, gate_low).astype(BF16),
                dot("erd,erf->edf", arrived, up_low).astype(BF16),
                dot("erf,erd->efd", active, cot_rows).astype(BF16),
            ),
            "dp",
        )
    rows_back = combine(token_ranks, rows_back)
    back = lax.psum_scatter(rows_back, "expert", scatter_dimension=0, tiled=True)[0]
    slot_grads = slot_grads.reshape(owned, peers, CAP).transpose(1, 0, 2)
    slots = jnp.arange(CAP, dtype=jnp.int32)[None, None, :, None]
    token_grads = jnp.where(own_ranks[:, :, None, :] == slots, slot_grads[..., None], 0.0)
    token_grads = jnp.sum(token_grads, axis=2)
    gate_grads = (
        lax.all_to_all(token_grads, "expert", split_axis=0, concat_axis=0, tiled=True)
        .reshape(experts, tok_count)
        .T
    )
    rows_out = combine(after(token_ranks, rows_back), rows_out)

    expert_sums = None if shared else expert_sums

    def next_expert(number, sums, *earlier):
        if not shared or number >= owned:
            return sums
        return expert_grads(
            x_placed.reshape(owned, -1, width),
            cot_placed.reshape(owned, -1, width),
            after(all_gates, *earlier),
            own,
            w_gate,
            w_up,
            w_down,
            number,
            sums,
        )

    if shared:
        ranks = block_ranks(
            jnp.concatenate([side_routes(piece) for piece in cot_pieces]), peer, owned, experts
        )
        ranks = after(ranks, rows_out)
        cot_placed = place_all(ranks, cot_pieces, cot_placed, peers)
        pieces = swapped_columns(moe_all)
        x_placed = place_all(ranks, pieces, x_placed, peers)
        gates = jnp.concatenate([side_gates(piece) for piece in pieces])
        all_gates = jnp.concatenate([slot_gates, slot_values(ranks, gates)])
        all_gates = all_gates.transpose(1, 0, 2).reshape(owned, -1, 1)
    expert_sums = next_expert(0, expert_sums, rows_out)

    grad_logits = own_gates * (
        gate_grads - jnp.sum(own_gates * gate_grads, axis=-1, keepdims=True)
    )
    grad_router_w = jnp.einsum("td,te->de", normed_moe.astype(F32), grad_logits, precision=PRECISE)
    grad_normed = back.astype(F32) + jnp.einsum(
        "te,de->td", grad_logits, router_full.astype(F32), precision=PRECISE
    )
    grad_hidden_n, grad_moe_gain = moe_pull(grad_normed)
    grad_hidden = cotangent[0].astype(F32) + grad_hidden_n
    grad_branch = grad_hidden.astype(BF16)
    branch_all = lax.all_gather(grad_branch, "dp", axis=0, tiled=True)
    expert_sums = next_expert(1, expert_sums, grad_branch)

    grad_attended = dot("td,md->tm", branch_all, out_w).astype(BF16)
    query_grad, key_grad, value_grad, head_grads = attend_back(
        query_low,
        key_low,
        value_low,
        grad_attended,
        log_total,
        segment,
        query_pre,
        key_pre,
        cos,
        sin,
        query_gain,
        key_gain,
    )
    qkv_grad = jnp.concatenate([query_grad, key_grad, value_grad], axis=1)
    grad_normed_attn = dot("tm,dm->td", qkv_grad, qkv_w).astype(BF16)
    expert_sums = next_expert(2, expert_sums, grad_normed_attn)
    grad_normed_attn = lax.psum_scatter(
        grad_normed_attn, "dp", scatter_dimension=0, tiled=True
    ).astype(F32)
    _, attn_pull = jax.vjp(norm_rows, inputs, attn_gain)
    grad_inputs_n, grad_attn_gain = attn_pull(grad_normed_attn)
    grad_tokens = grad_hidden + grad_inputs_n

    whole_gains = jnp.stack([grad_attn_gain, grad_moe_gain], axis=1)
    head_gains = head_grads[:2].T
    head_gains = jnp.pad(
        head_gains.reshape(bands * peers, gain_rows, 2),
        ((0, 0), (0, band_rows - gain_rows), (0, 0)),
    )
    small_grad = jnp.concatenate(
        [grad_router_w, whole_gains, head_gains.reshape(width, 2)], axis=1
    )
    small_grad = jnp.pad(small_grad, ((0, 0), (0, 128 - small_grad.shape[1])))
    band_qkv = jnp.concatenate([dot("td,tm->dm", normed, qkv_grad), small_grad], axis=1)
    band_qkv = band_qkv.astype(BF16).reshape(bands, peers, band_rows, -1).transpose(1, 0, 2, 3)
    expert_sums = next_expert(3, expert_sums, band_qkv)
    for number in range(4, owned):
        expert_sums = next_expert(number, expert_sums)
    band_qkv = lax.psum_scatter(
        band_qkv.reshape(width, -1), "expert", scatter_dimension=0, tiled=True
    ).reshape(bands, band_rows, -1)
    band_qkv = lax.all_to_all(band_qkv, "dp", split_axis=0, concat_axis=0, tiled=True).transpose(
        1, 0, 2
    )
    grad_query = band_qkv[:, :, :q_cols].astype(F32).reshape(band_rows, -1)
    grad_key = band_qkv[:, :, q_cols : q_cols + k_cols].astype(F32).reshape(band_rows, -1)
    grad_value = band_qkv[:, :, q_cols + k_cols : qkv_cols].astype(F32).reshape(band_rows, -1)
    smaller = jnp.sum(band_qkv[:, :, qkv_cols:].astype(F32), axis=1)
    grad_output = sum_peers(
        dot("tm,td->md", attended_low, branch_all).astype(BF16).reshape(peers, -1, width)
    )

    moe_sum = sum_peers(after(rows_out, branch_all))
    block_out = (hidden + moe_sum).astype(BF16)
    return (
        block_out[None],
        grad_tokens[None],
        grad_query,
        grad_key,
        grad_value,
        grad_output,
        smaller[:, :experts],
        smaller[:, experts],
        smaller[:, experts + 1],
        smaller[:gain_rows, experts + 2],
        smaller[:gain_rows, experts + 3],
        expert_sums[0].astype(F32),
        expert_sums[1].astype(F32),
        expert_sums[2].astype(F32),
    )


def solution(mesh):
    both = ("dp", "expert")
    return jax.shard_map(
        on_device,
        mesh=mesh,
        in_specs=(
            P("expert", "dp", None),
            P("expert", None),
            P("expert", "dp", None),
            P(both, None),
            P(both, None),
            P(both, None),
            P(both, None),
            P(both, None),
            P(both),
            P(both),
            P(both),
            P(both),
            P("expert", None, None),
            P("expert", None, None),
            P("expert", None, None),
            P("expert", "dp", None),
        ),
        out_specs=(
            P("expert", "dp", None),
            P("expert", "dp", None),
            P(both, None),
            P(both, None),
            P(both, None),
            P(both, None),
            P(both, None),
            P(both),
            P(both),
            P(both),
            P(both),
            P("expert", None, None),
            P("expert", None, None),
            P("expert", None, None),
        ),
        check_vma=False,
    )
```

```python
import jax
import jax.numpy as jnp
from jax import lax
from jax.experimental import pallas as pl
from jax.experimental.pallas import tpu as pltpu
from jax.sharding import PartitionSpec as P

CAP = 80
Q_BLOCK = 256
HIDDEN_TILE = 256
OWN_ROWS = 8 * CAP
WIDTH_TILE = 512
SIDE = 128
ROW_PARTS = 2
VMEM_BYTES = 60 << 20


EPSILON = 1e-06
ROPE_BASE = 1000000.0
PRECISE = lax.Precision.HIGHEST
F32 = jnp.float32
BF16 = jnp.bfloat16
FREE = pl.CostEstimate(flops=0, bytes_accessed=0, transcendentals=0)


def norm_rows(values, gain_row):
    return (
        values * lax.rsqrt(jnp.mean(values * values, axis=-1, keepdims=True) + EPSILON) * gain_row
    )


def activate(gate_vals, up_vals):
    return gate_vals * jax.nn.sigmoid(gate_vals) * up_vals


def masked_softmax(logits, mask):
    kept = jnp.where(mask, logits, -jnp.inf)
    largest = jnp.max(kept, axis=-1, keepdims=True)
    raised = jnp.where(mask, jnp.exp(logits - largest), 0.0)
    return raised / jnp.sum(raised, axis=-1, keepdims=True)


def nothing(*refs):
    del refs


def after(value, *others):
    anywhere = pl.BlockSpec(memory_space=pl.ANY)
    return pl.pallas_call(
        nothing,
        out_shape=jax.ShapeDtypeStruct(value.shape, value.dtype),
        in_specs=[anywhere] * (1 + len(others)),
        out_specs=anywhere,
        input_output_aliases={0: 0},
    )(value, *others)


def shifted(value, axis, step):
    count = lax.axis_size(axis)
    return lax.ppermute(value, axis, [(i, (i + step) % count) for i in range(count)])


def traded(value, axis, step):
    return lax.ppermute(value, axis, [(i, i ^ step) for i in range(lax.axis_size(axis))])


def gather_blocks(own, axis):
    count, me = lax.axis_size(axis), lax.axis_index(axis)
    whole = jnp.zeros((count, *own.shape), own.dtype)
    whole = lax.dynamic_update_index_in_dim(whole, own, me, 0)
    for step in range(1, count):
        whole = lax.dynamic_update_index_in_dim(whole, traded(own, axis, step), me ^ step, 0)
    return whole


def sum_blocks(blocks, axis):
    count, me = lax.axis_size(axis), lax.axis_index(axis)
    total = lax.dynamic_index_in_dim(blocks, me, 0, keepdims=False).astype(F32)
    for step in range(1, count):
        sent = lax.dynamic_index_in_dim(blocks, me ^ step, 0, keepdims=False)
        total = total + traded(sent, axis, step).astype(F32)
    return total


def sum_peers(blocks):
    count, me = lax.axis_size("expert"), lax.axis_index("expert")
    core, chip, chips = lax.rem(me, 2), lax.div(me, 2), count // 2
    paired = blocks.reshape(chips, 2, *blocks.shape[1:])
    sent = lax.dynamic_index_in_dim(paired, 1 - core, 1, keepdims=False)
    kept = lax.dynamic_index_in_dim(paired, core, 1, keepdims=False)
    got = lax.ppermute(sent, "expert", [(i, i ^ 1) for i in range(count)])
    halves = (kept.astype(F32) + got.astype(F32)).astype(BF16)
    total = lax.dynamic_index_in_dim(halves, chip, 0, keepdims=False).astype(F32)
    for step in range(1, chips):
        sent = lax.dynamic_index_in_dim(halves, lax.rem(chip + step, chips), 0, keepdims=False)
        total = total + shifted(sent, "expert", 2 * step).astype(F32)
    return total


def dot(spec, left, right):
    return jnp.einsum(spec, left, right, preferred_element_type=F32)


def line_sems(chips):
    return [pltpu.SemaphoreType.DMA((chips,))] * 6 + [pltpu.SemaphoreType.DMA]


def send_to(source, target, send_sem, recv_sem, device):
    return pltpu.make_async_remote_copy(
        src_ref=source,
        dst_ref=target,
        send_sem=send_sem,
        recv_sem=recv_sem,
        device_id=device,
        device_id_type=pl.DeviceIdType.MESH,
    )


def greet(devices, conditions):
    barrier = pltpu.get_barrier_semaphore()
    for device, condition in zip(devices, conditions):

        @pl.when(condition)
        def _(device=device):
            pl.semaphore_signal(
                barrier, inc=1, device_id=device, device_id_type=pl.DeviceIdType.MESH
            )

    pl.semaphore_wait(barrier, sum(condition.astype(jnp.int32) for condition in conditions))


def expert_place():
    me = lax.axis_index("expert")
    return me, lax.div(me, 2), lax.rem(me, 2), lax.axis_size("expert") // 2


def line_partners():
    me, chip, core, chips = expert_place()
    band = lax.axis_index("dp")
    devices = [(band, me + 1 - 2 * core), (band, me + 2), (band, me - 2)]
    return devices, [chip >= 0, chip < chips - 1, chip > 0]


class Line:
    def __init__(self, own, slot, sems):
        self.own, self.slot = own, slot
        self.up_out, self.up_in, self.down_out, self.down_in, self.side_out, self.side_in, self.self_sem = sems
        self.me, self.chip, self.core, self.chips = expert_place()
        (self.twin, self.up, self.down), _ = line_partners()

    def local(self):
        return pltpu.make_async_copy(self.own, self.slot(self.me), self.self_sem)

    def side(self, source, block):
        return send_to(
            source,
            self.slot(2 * block + self.core),
            self.side_out.at[block],
            self.side_in.at[block],
            self.twin,
        )

    def upward(self, source, block, step):
        return send_to(
            source,
            self.slot(2 * block + self.core),
            self.up_out.at[step],
            self.up_in.at[step],
            self.up,
        )

    def downward(self, source, block, step):
        return send_to(
            source,
            self.slot(2 * block + self.core),
            self.down_out.at[step],
            self.down_in.at[step],
            self.down,
        )

    def begin(self):
        self.local().start()

        @pl.when(self.chip < self.chips - 1)
        def _():
            self.upward(self.own, self.chip, 0).start()

        @pl.when(self.chip > 0)
        def _():
            self.downward(self.own, self.chip, 0).start()

        self.side(self.own, self.chip).start()

    def advance(self, step):
        below, above = self.chip - 1 - step, self.chip + 1 + step

        @pl.when(below >= 0)
        def _():
            held = self.slot(2 * below + self.core)
            self.upward(held, below, step).wait_recv()

            if step + 1 < self.chips - 1:

                @pl.when(self.chip < self.chips - 1)
                def _():
                    self.upward(held, below, step + 1).start()

            self.side(held, below).start()

        @pl.when(above < self.chips)
        def _():
            held = self.slot(2 * above + self.core)
            self.downward(held, above, step).wait_recv()

            if step + 1 < self.chips - 1:

                @pl.when(self.chip > 0)
                def _():
                    self.downward(held, above, step + 1).start()

            self.side(held, above).start()

    def finish(self):
        self.local().wait()
        for step in range(self.chips - 1):

            @pl.when((self.chip < self.chips - 1) & (self.chip >= step))
            def _(step=step):
                block = self.chip - step
                self.upward(self.slot(2 * block + self.core), block, step).wait_send()

            @pl.when((self.chip > 0) & (self.chip + step < self.chips))
            def _(step=step):
                block = self.chip + step
                self.downward(self.slot(2 * block + self.core), block, step).wait_send()

        for block in range(self.chips):
            self.side(self.slot(2 * block + self.core), block).wait_send()
            send_to(
                self.slot(2 * block + self.core),
                self.slot(2 * block + 1 - self.core),
                self.side_out.at[block],
                self.side_in.at[block],
                self.twin,
            ).wait_recv()


def rows_kernel(own_ref, all_ref, *sems):
    greet(*line_partners())
    line = Line(own_ref, lambda i: all_ref.at[i], sems)
    line.begin()
    for step in range(line.chips - 1):
        line.advance(step)
    line.finish()


def gather_rows(own):
    peers = lax.axis_size("expert")
    anywhere = pl.BlockSpec(memory_space=pl.ANY)
    return pl.pallas_call(
        rows_kernel,
        out_shape=jax.ShapeDtypeStruct((peers, *own.shape), own.dtype),
        in_specs=[anywhere],
        out_specs=anywhere,
        scratch_shapes=line_sems(peers // 2),
        compiler_params=pltpu.CompilerParams(collective_id=1, has_side_effects=True),
    )(own)


def square_kernel(own_ref, all_ref, *sems):
    band, me = lax.axis_index("dp"), lax.axis_index("expert")
    outs, arrivals, twin_out, twin_in = sems[:3], sems[3:6], sems[6], sems[7]
    columns = [(band ^ 1, me), (band ^ 2, me)]
    devices, conditions = line_partners()
    greet(devices + columns, conditions + [band >= 0] * 2)
    line = Line(own_ref, lambda i: all_ref.at[band, i], sems[8:])
    chip, chips, core = line.chip, line.chips, line.core

    def across(source, block, step):
        return send_to(
            source,
            all_ref.at[band, 2 * block + core],
            outs[step - 1].at[block],
            arrivals[step - 1].at[block],
            (band ^ step, me),
        )

    def held(block, step):
        return all_ref.at[band ^ step, 2 * block + core]

    def arrive(block, step):
        send_to(
            own_ref,
            held(block, step),
            outs[step - 1].at[block],
            arrivals[step - 1].at[block],
            (band ^ step, me),
        ).wait_recv()

    def onward(block, step):
        return send_to(
            held(block, step),
            held(block, step),
            outs[2].at[block],
            arrivals[2].at[block],
            (band ^ (3 - step), me),
        )

    def twin(block, step):
        place = (step - 1) * chips + block
        return send_to(
            held(block, step),
            held(block, step),
            twin_out.at[place],
            twin_in.at[place],
            line.twin,
        )

    def spread(source, block):
        across(source, block, 1).start()
        across(source, block, 2).start()

    def receive(block):
        for step in (1, 2):
            arrive(block, step)

            @pl.when(lax.rem(block, 2) == step - 1)
            def _(step=step):
                onward(block, step).start()

            twin(block, step).start()

    line.begin()
    spread(own_ref, chip)
    for step in range(chips - 1):
        line.advance(step)
        below, above = chip - 1 - step, chip + 1 + step

        @pl.when(below >= 0)
        def _(below=below):
            spread(line.slot(2 * below + core), below)

        @pl.when(above < chips)
        def _(above=above):
            spread(line.slot(2 * above + core), above)

    receive(chip)
    for step in range(chips - 1):
        below, above = chip - 1 - step, chip + 1 + step

        @pl.when(below >= 0)
        def _(below=below):
            receive(below)

        @pl.when(above < chips)
        def _(above=above):
            receive(above)

    for block in range(chips):
        arrive(block, 3)
        twin(block, 3).start()
    line.finish()
    for block in range(chips):
        across(own_ref, block, 1).wait_send()
        across(own_ref, block, 2).wait_send()
        onward(block, 1).wait_send()
        for step in (1, 2, 3):
            place = (step - 1) * chips + block
            twin(block, step).wait_send()
            there = all_ref.at[band ^ step, 2 * block + 1 - core]
            send_to(there, there, twin_out.at[place], twin_in.at[place], line.twin).wait_recv()


def gather_square(own):
    bands, peers = lax.axis_size("dp"), lax.axis_size("expert")
    chips = peers // 2
    anywhere = pl.BlockSpec(memory_space=pl.ANY)
    return pl.pallas_call(
        square_kernel,
        out_shape=jax.ShapeDtypeStruct((bands, peers, *own.shape), own.dtype),
        in_specs=[anywhere],
        out_specs=anywhere,
        scratch_shapes=[pltpu.SemaphoreType.DMA((chips,))] * 6
        + [pltpu.SemaphoreType.DMA((3 * chips,))] * 2
        + line_sems(chips),
        compiler_params=pltpu.CompilerParams(collective_id=2, has_side_effects=True),
    )(own)


def start_kernel(
    tok_ref, pack_ref, wo_ref, tokens_ref, swap_ref, pack_all_ref, wo_all_ref, *sems
):
    bands, band = lax.axis_size("dp"), lax.axis_index("dp")
    me = lax.axis_index("expert")
    tok_out, tok_in, swap_out, swap_in, self_sems = sems[:5]
    pack_sems, wo_sems = sems[5:12], sems[12:]
    columns = [(band ^ step, me) for step in range(1, bands)]
    devices, conditions = line_partners()
    greet(devices + columns, conditions + [band >= 0] * (bands - 1))
    own_tok = pltpu.make_async_copy(tok_ref, tokens_ref.at[band], self_sems.at[0])
    own_swap = pltpu.make_async_copy(pack_ref.at[band], swap_ref.at[band], self_sems.at[1])
    own_swap.start()
    own_tok.start()

    def swap(step):
        other = band ^ step
        return send_to(
            pack_ref.at[other],
            swap_ref.at[band],
            swap_out.at[step - 1],
            swap_in.at[step - 1],
            (other, me),
        )

    def token(step):
        other = band ^ step
        return send_to(
            tok_ref, tokens_ref.at[band], tok_out.at[step - 1], tok_in.at[step - 1], (other, me)
        )

    def arrived(step, source, target, out, arrival):
        other = band ^ step
        send_to(
            source, target.at[other], out.at[step - 1], arrival.at[step - 1], (other, me)
        ).wait_recv()

    for step in range(1, bands):
        swap(step).start()
    wo_line = Line(wo_ref, lambda i: wo_all_ref.at[i], wo_sems)
    wo_line.begin()
    for step in range(1, bands):
        token(step).start()
    own_swap.wait()
    for step in range(1, bands):
        arrived(step, pack_ref.at[band], swap_ref, swap_out, swap_in)
    pack_line = Line(swap_ref, lambda i: pack_all_ref.at[:, i], pack_sems)
    pack_line.begin()
    for step in range(pack_line.chips - 1):
        wo_line.advance(step)
        pack_line.advance(step)
    wo_line.finish()
    pack_line.finish()
    own_tok.wait()
    for step in range(1, bands):
        arrived(step, tok_ref, tokens_ref, tok_out, tok_in)
        token(step).wait_send()
        swap(step).wait_send()


def start_moves(tokens, packed, w_output):
    bands, peers = lax.axis_size("dp"), lax.axis_size("expert")
    anywhere = pl.BlockSpec(memory_space=pl.ANY)
    chips = peers // 2
    shapes = [
        (bands, *tokens.shape),
        packed.shape,
        (bands, peers, *packed.shape[1:]),
        (peers, *w_output.shape),
    ]
    tokens_all, _, packed_all, output_all = pl.pallas_call(
        start_kernel,
        out_shape=[jax.ShapeDtypeStruct(shape, BF16) for shape in shapes],
        in_specs=[anywhere] * 3,
        out_specs=[anywhere] * 4,
        scratch_shapes=[pltpu.SemaphoreType.DMA((bands - 1,))] * 4
        + [pltpu.SemaphoreType.DMA((2,))]
        + line_sems(chips) * 2,
        compiler_params=pltpu.CompilerParams(collective_id=0, has_side_effects=True),
    )(tokens, packed, w_output)
    width = tokens.shape[1]
    return (
        tokens_all.reshape(-1, width),
        packed_all.reshape(-1, packed.shape[-1]),
        output_all.reshape(-1, width),
    )


def block_ranks(routes, peer, owned, experts):
    chosen = jnp.any(routes[..., None] == jnp.arange(experts, dtype=jnp.int32), axis=2)
    chosen = lax.dynamic_slice_in_dim(chosen, peer * owned, owned, axis=2)
    tok_count = chosen.shape[1]
    earlier = jnp.tril(jnp.ones((tok_count, tok_count), BF16), -1)
    ranks = dot("ts,bse->bet", earlier, chosen.astype(BF16)).astype(jnp.int32)
    return jnp.where(chosen.transpose(0, 2, 1), ranks, -1)


def slot_values(ranks, values):
    slots = jnp.arange(CAP, dtype=jnp.int32)
    chosen = ranks[:, :, None, :] == slots[None, None, :, None]
    return jnp.sum(jnp.where(chosen, values.transpose(0, 2, 1)[:, :, None, :], 0.0), axis=-1)


def by_core(values, core):
    paired = values.reshape(-1, 2, *values.shape[1:])
    return lax.dynamic_index_in_dim(paired, core, 1, keepdims=False)


def place_kernel(_, rank_ref, block_ref, rows_ref):
    count, owned, tok_count = rank_ref.shape
    slots = lax.broadcasted_iota(jnp.int32, (CAP, tok_count), 0)
    width = block_ref.shape[-1]
    for block in range(count):
        ranks = rank_ref[block]
        hot = jnp.concatenate([ranks[e : e + 1] == slots for e in range(owned)], axis=0)
        hot = jnp.where(hot, 1.0, 0.0).astype(BF16)
        for start in range(0, width, WIDTH_TILE):
            cols = slice(start, start + WIDTH_TILE)
            rows = jnp.dot(hot, block_ref[0, block, :, cols], preferred_element_type=F32)
            rows_ref[:, block, :, cols] = rows.astype(BF16).reshape(owned, CAP, WIDTH_TILE)


def place_rows(ranks, columns, first):
    total, owned, tok_count = ranks.shape
    peers = columns.shape[1]
    width = columns.shape[-1] - SIDE
    several = 2
    steps = peers // several

    def block_at(b, at):
        return lax.bitwise_xor(at[0], lax.div(b, steps)), lax.rem(b, steps), 0, 0

    return pl.pallas_call(
        place_kernel,
        grid_spec=pltpu.PrefetchScalarGridSpec(
            num_scalar_prefetch=1,
            grid=(total // several,),
            in_specs=[
                pl.BlockSpec((several, owned, tok_count), lambda b, at: (b, 0, 0)),
                pl.BlockSpec((1, several, tok_count, width), block_at),
            ],
            out_specs=pl.BlockSpec((owned, several, CAP, width), lambda b, at: (0, b, 0, 0)),
        ),
        out_shape=jax.ShapeDtypeStruct((owned, total, CAP, width), BF16),
        compiler_params=pltpu.CompilerParams(vmem_limit_bytes=VMEM_BYTES),
        cost_estimate=FREE,
    )(jnp.asarray(first, jnp.int32).reshape(1), ranks, columns)


def combine_kernel(rank_ref, rows_ref, out_ref):
    tok_count, owned = rank_ref.shape[1:]
    slots = owned * CAP
    width = out_ref.shape[-1]
    lane = lax.broadcasted_iota(jnp.int32, (tok_count, slots), 1)
    hot = jnp.zeros((tok_count, slots), F32)
    for e in range(owned):
        ranks = rank_ref[0, :, e : e + 1]
        hot = jnp.where((ranks >= 0) & (lane == ranks + e * CAP), 1.0, hot)
    hot = hot.astype(BF16)
    for start in range(0, width, WIDTH_TILE):
        cols = slice(start, start + WIDTH_TILE)
        rows = rows_ref[:, 0, :, cols].reshape(slots, WIDTH_TILE)
        out_ref[0, :, cols] = jnp.dot(hot, rows, preferred_element_type=F32).astype(BF16)


def combine(ranks, rows):
    count, tok_count, owned = ranks.shape
    width = rows.shape[-1]
    return pl.pallas_call(
        combine_kernel,
        grid=(count,),
        out_shape=jax.ShapeDtypeStruct((count, tok_count, width), BF16),
        in_specs=[
            pl.BlockSpec((1, tok_count, owned), lambda b: (b, 0, 0)),
            pl.BlockSpec((owned, 1, CAP, width), lambda b: (0, b, 0, 0)),
        ],
        out_specs=pl.BlockSpec((1, tok_count, width), lambda b: (b, 0, 0)),
        compiler_params=pltpu.CompilerParams(vmem_limit_bytes=VMEM_BYTES),
        cost_estimate=FREE,
    )(ranks, rows.reshape(owned, count, CAP, width))


def dot_nt(left, right):
    return lax.dot_general(left, right, (((1,), (1,)), ((), ())), preferred_element_type=F32)


def hidden_grads(x, c, gates, wg_ref, wu_ref, wd_ref):
    gate_in = jnp.dot(x, wg_ref[0], preferred_element_type=F32)
    up_in = jnp.dot(x, wu_ref[0], preferred_element_type=F32)
    raw = dot_nt(c, wd_ref[0])
    sig = 1.0 / (1.0 + jnp.exp(-gate_in))
    silu = gate_in * sig
    active = silu * up_in
    grad = raw * gates
    gate_grad = grad * up_in * (sig + silu * (1.0 - sig))
    up_grad = grad * silu
    return (active * gates).astype(BF16), gate_grad.astype(BF16), up_grad.astype(BF16), active * raw


def own_kernel(
    x_ref,
    c_ref,
    g_ref,
    wg_ref,
    wu_ref,
    wd_ref,
    active_ref,
    gate_ref,
    up_ref,
    slot_ref,
    back_ref,
    out_ref,
    back_sum,
    out_sum,
):
    width = x_ref.shape[-1]
    step = pl.program_id(2)
    active, gate_grad, up_grad, slot = hidden_grads(
        x_ref[0], c_ref[0], g_ref[0], wg_ref, wu_ref, wd_ref
    )
    active_ref[0] = active
    gate_ref[0] = gate_grad
    up_ref[0] = up_grad
    slot = jnp.sum(slot, axis=1, keepdims=True)
    slot_ref[0] = jnp.where(step == 0, slot, slot_ref[0] + slot)
    for start in range(0, width, WIDTH_TILE):
        cols = slice(start, start + WIDTH_TILE)
        rows = dot_nt(gate_ref[0], wg_ref[0, cols, :]) + dot_nt(up_ref[0], wu_ref[0, cols, :])
        back_sum[:, cols] = jnp.where(step == 0, rows, back_sum[:, cols] + rows)
        rows = jnp.dot(active_ref[0], wd_ref[0, :, cols], preferred_element_type=F32)
        out_sum[:, cols] = jnp.where(step == 0, rows, out_sum[:, cols] + rows)

    @pl.when(step == pl.num_programs(2) - 1)
    def _():
        back_ref[0] = back_sum[...].astype(BF16)
        out_ref[0] = out_sum[...].astype(BF16)


def own_experts(x_rows, c_rows, gates, rows, w_gate, w_up, w_down):
    owned, _, width = x_rows.shape
    hidden = w_down.shape[1]
    tile = HIDDEN_TILE
    some = min(rows, OWN_ROWS)
    whole = pl.BlockSpec((1, some, width), lambda e, r, f: (e, r, 0))
    column = pl.BlockSpec((1, some, 1), lambda e, r, f: (e, r, 0))
    part = pl.BlockSpec((1, some, tile), lambda e, r, f: (e, r, f))
    inward = pl.BlockSpec((1, width, tile), lambda e, r, f: (e, 0, f))
    outward = pl.BlockSpec((1, tile, width), lambda e, r, f: (e, f, 0))
    return pl.pallas_call(
        own_kernel,
        grid=(owned, rows // some, hidden // tile),
        in_specs=[whole, whole, column, inward, inward, outward],
        out_specs=[part, part, part, column, whole, whole],
        out_shape=[jax.ShapeDtypeStruct((owned, rows, hidden), BF16)] * 3
        + [jax.ShapeDtypeStruct((owned, rows, 1), F32)]
        + [jax.ShapeDtypeStruct((owned, rows, width), BF16)] * 2,
        scratch_shapes=[pltpu.VMEM((some, width), F32)] * 2,
        compiler_params=pltpu.CompilerParams(vmem_limit_bytes=VMEM_BYTES),
        cost_estimate=pl.CostEstimate(
            flops=12 * owned * rows * width * hidden,
            bytes_accessed=owned * (8 * rows * width + 6 * width * hidden),
            transcendentals=owned * rows * hidden,
        ),
    )(x_rows, c_rows, gates, w_gate, w_up, w_down)


def grads_kernel(
    x_ref, c_ref, g_ref, active_ref, gate_ref, up_ref, wg_ref, wu_ref, wd_ref, *rest
):
    dg_ref, du_ref, dd_ref, mark_ref, sums, pair, actives = rest[-7:]
    mark_ref[...] = jnp.zeros_like(mark_ref)
    tile = HIDDEN_TILE
    rows, width = x_ref.shape[1:]
    own = active_ref.shape[1]
    step = pl.program_id(1)

    def keep(start, active, gate_grad, up_grad):
        part = slice(start, start + own)
        actives[:, part] = active.T
        pair[:tile, part] = gate_grad.T
        pair[tile:, part] = up_grad.T

    def work_out(start):
        part = slice(start, start + own)
        active, gate_grad, up_grad, _ = hidden_grads(
            x_ref[0, part], c_ref[0, part], g_ref[0, part], wg_ref, wu_ref, wd_ref
        )
        keep(start, active, gate_grad, up_grad)

    @pl.when(step == 0)
    def _():
        keep(0, active_ref[0], gate_ref[0], up_ref[0])

    @pl.when(step > 0)
    def _():
        work_out(0)

    for start in range(own, rows, own):
        work_out(start)

    @pl.loop(0, width // WIDTH_TILE)
    def _(c):
        cols = pl.ds(pl.multiple_of(c * WIDTH_TILE, WIDTH_TILE), WIDTH_TILE)
        grads = jnp.dot(pair[...], x_ref[0, :, cols], preferred_element_type=F32)
        sums[:, cols] = jnp.where(step == 0, grads, sums[:, cols] + grads)
        grads = jnp.dot(actives[...], c_ref[0, :, cols], preferred_element_type=F32)
        dd_ref[0, :, cols] = jnp.where(step == 0, grads, dd_ref[0, :, cols] + grads)

    @pl.when(step == pl.num_programs(1) - 1)
    def _():
        same = lax.broadcasted_iota(jnp.int32, (tile, tile), 0) == lax.broadcasted_iota(
            jnp.int32, (tile, tile), 1
        )
        same = jnp.where(same, 1.0, 0.0).astype(BF16)

        @pl.loop(0, width // tile)
        def _(c):
            cols = pl.ds(pl.multiple_of(c * tile, tile), tile)
            dg_ref[0, cols, :] = dot_nt(same, sums[:tile, cols].astype(BF16))
            du_ref[0, cols, :] = dot_nt(same, sums[tile:, cols].astype(BF16))


def expert_grads(x_rows, c_rows, gates, own, w_gate, w_up, w_down, expert, buffers=None):
    owned, rows, width = x_rows.shape
    hidden = w_down.shape[1]
    tile, parts = HIDDEN_TILE, ROW_PARTS
    part, own_rows = rows // parts, own[0].shape[1]
    shapes = [(owned, width, hidden)] * 2 + [(owned, hidden, width)]
    in_specs = [
        pl.BlockSpec((1, part, width), lambda f, r: (expert, r, 0)),
        pl.BlockSpec((1, part, width), lambda f, r: (expert, r, 0)),
        pl.BlockSpec((1, part, 1), lambda f, r: (expert, r, 0)),
        *[pl.BlockSpec((1, own_rows, tile), lambda f, r: (expert, 0, f))] * 3,
        pl.BlockSpec((1, width, tile), lambda f, r: (expert, 0, f)),
        pl.BlockSpec((1, width, tile), lambda f, r: (expert, 0, f)),
        pl.BlockSpec((1, tile, width), lambda f, r: (expert, f, 0)),
    ]
    given = (x_rows, c_rows, gates, *own, w_gate, w_up, w_down)
    aliases = {}
    if buffers is not None:
        aliases = {len(given) + i: i for i in range(3)}
        in_specs += [pl.BlockSpec(memory_space=pl.ANY)] * 3
        given += tuple(buffers)
    return pl.pallas_call(
        grads_kernel,
        grid=(hidden // tile, parts),
        out_shape=[jax.ShapeDtypeStruct(shape, F32) for shape in [*shapes, (8, 128)]],
        in_specs=in_specs,
        out_specs=[
            pl.BlockSpec((1, width, tile), lambda f, r: (expert, 0, f)),
            pl.BlockSpec((1, width, tile), lambda f, r: (expert, 0, f)),
            pl.BlockSpec((1, tile, width), lambda f, r: (expert, f, 0)),
            pl.BlockSpec((8, 128), lambda f, r: (0, 0)),
        ],
        scratch_shapes=[
            pltpu.VMEM((2 * tile, width), F32),
            pltpu.VMEM((2 * tile, part), BF16),
            pltpu.VMEM((tile, part), BF16),
        ],
        input_output_aliases=aliases,
        compiler_params=pltpu.CompilerParams(vmem_limit_bytes=VMEM_BYTES),
        cost_estimate=pl.CostEstimate(
            flops=12 * rows * width * hidden,
            bytes_accessed=12 * rows * width + 24 * width * hidden,
            transcendentals=rows * hidden,
        ),
    )(*given)


def turn(values, cos, sin):
    return values * cos + pltpu.roll(values, values.shape[-1] // 2, 1) * sin


def qkv_kernel(
    tok_ref,
    gain_ref,
    w_ref,
    cos_ref,
    sin_ref,
    gq_ref,
    gk_ref,
    normed_ref,
    qpre_ref,
    kpre_ref,
    qrot_ref,
    krot_ref,
    value_ref,
):
    head = cos_ref.shape[1]
    heads = qpre_ref.shape[1] // head
    normed = norm_rows(tok_ref[...].astype(F32), gain_ref[...]).astype(BF16)
    normed_ref[...] = normed
    cos, sin = cos_ref[...], sin_ref[...]
    for pair in range(0, heads, 2):
        cols = slice(pair * head, (pair + 2) * head)
        pre = jnp.dot(normed, w_ref[:, cols], preferred_element_type=F32)
        qpre_ref[:, cols] = pre
        for h in range(2):
            one = slice(h * head, (h + 1) * head)
            rot = turn(norm_rows(pre[:, one], gq_ref[...]), cos, sin)
            qrot_ref[:, (pair + h) * head : (pair + h + 1) * head] = rot.astype(BF16)
    cols = slice(heads * head, (heads + 2) * head)
    pre = jnp.dot(normed, w_ref[:, cols], preferred_element_type=F32)
    kpre_ref[...] = pre[:, :head]
    krot_ref[...] = turn(norm_rows(pre[:, :head], gk_ref[...]), cos, sin).astype(BF16)
    value_ref[...] = pre[:, head:].astype(BF16)


def make_qkv(tokens, gain, weight, cos, sin, query_gain, key_gain):
    length, width = tokens.shape
    head = cos.shape[1]
    cols = weight.shape[1]
    q_cols = cols - 3 * head
    block = Q_BLOCK

    def rows(size):
        return pl.BlockSpec((block, size), lambda i: (i, 0))

    def fixed(*shape):
        return pl.BlockSpec(shape, lambda i: (0, 0))

    return pl.pallas_call(
        qkv_kernel,
        grid=(length // block,),
        in_specs=[
            rows(width),
            fixed(1, width),
            fixed(width, cols),
            rows(head),
            rows(head),
            fixed(1, head),
            fixed(1, head),
        ],
        out_specs=[rows(width), rows(q_cols), rows(head), rows(q_cols), rows(head), rows(head)],
        out_shape=[
            jax.ShapeDtypeStruct((length, width), BF16),
            jax.ShapeDtypeStruct((length, q_cols), F32),
            jax.ShapeDtypeStruct((length, head), F32),
            jax.ShapeDtypeStruct((length, q_cols), BF16),
            jax.ShapeDtypeStruct((length, head), BF16),
            jax.ShapeDtypeStruct((length, head), BF16),
        ],
        compiler_params=pltpu.CompilerParams(vmem_limit_bytes=VMEM_BYTES),
        cost_estimate=FREE,
    )(tokens, gain[None], weight, cos, sin, query_gain[None], key_gain[None])


def masked_scores(q_ref, k_ref, seg_row_ref, seg_col_ref, block, keys):
    size = q_ref.shape[0]
    scores = dot_nt(k_ref[:keys], q_ref[...]) * q_ref.shape[1] ** (-0.5)
    key_at = lax.broadcasted_iota(jnp.int32, (keys, size), 0)
    query_at = lax.broadcasted_iota(jnp.int32, (keys, size), 1) + block * size
    allowed = (key_at <= query_at) & (seg_col_ref[:keys] == seg_row_ref[...])
    return jnp.where(allowed, scores, -1e30)


def attend_kernel(q_ref, k_ref, vt_ref, seg_row_ref, seg_col_ref, out_ref, log_ref):
    size = q_ref.shape[0]
    blocks = k_ref.shape[0] // size
    for block in range(blocks):

        @pl.when(pl.program_id(1) == block)
        def _(block=block):
            keys = (block + 1) * size
            scores = masked_scores(q_ref, k_ref, seg_row_ref, seg_col_ref, block, keys)
            largest = jnp.max(scores, axis=0, keepdims=True)
            raised = jnp.exp(scores - largest)
            total = jnp.sum(raised, axis=0, keepdims=True)
            weights = (raised * (1.0 / total)).astype(BF16)
            out = jnp.dot(vt_ref[:, :keys], weights, preferred_element_type=F32)
            out_ref[...] = out.T.astype(BF16)
            log_ref[0] = largest + jnp.log(total)


def attend(query, key, value, segment):
    length, cols = query.shape
    head = key.shape[1]
    block = Q_BLOCK
    heads = cols // head
    return pl.pallas_call(
        attend_kernel,
        grid=(heads, length // block),
        in_specs=[
            pl.BlockSpec((block, head), lambda h, i: (i, h)),
            pl.BlockSpec((length, head), lambda h, i: (0, 0)),
            pl.BlockSpec((head, length), lambda h, i: (0, 0)),
            pl.BlockSpec((1, block), lambda h, i: (0, i)),
            pl.BlockSpec((length, 1), lambda h, i: (0, 0)),
        ],
        out_specs=[
            pl.BlockSpec((block, head), lambda h, i: (i, h)),
            pl.BlockSpec((1, 1, block), lambda h, i: (h, 0, i)),
        ],
        out_shape=[
            jax.ShapeDtypeStruct((length, cols), BF16),
            jax.ShapeDtypeStruct((heads, 1, length), F32),
        ],
        compiler_params=pltpu.CompilerParams(vmem_limit_bytes=VMEM_BYTES),
        cost_estimate=FREE,
    )(query, key, value.T, segment[None], segment[:, None])


def attend_back_kernel(
    q_ref,
    k_ref,
    kt_ref,
    v_ref,
    do_ref,
    log_ref,
    seg_row_ref,
    seg_col_ref,
    qpre_ref,
    kpre_ref,
    cos_ref,
    sin_ref,
    gq_ref,
    gk_ref,
    dq_ref,
    dk_ref,
    dv_ref,
    dgain_ref,
    key_sum,
    value_sum,
):
    size, head = q_ref.shape
    blocks = k_ref.shape[0] // size
    scale = head ** (-0.5)
    first = (pl.program_id(0) == 0) & (pl.program_id(1) == 0)
    last = (pl.program_id(0) == pl.num_programs(0) - 1) & (pl.program_id(1) == blocks - 1)

    @pl.when(first)
    def _():
        key_sum[...] = jnp.zeros_like(key_sum)
        value_sum[...] = jnp.zeros_like(value_sum)
        dgain_ref[...] = jnp.zeros_like(dgain_ref)

    def pull(grad, pre, gain, cos, sin):
        grad = grad.astype(BF16).astype(F32)
        turned = grad * cos + pltpu.roll(grad * sin, head // 2, 1)
        scale_row = lax.rsqrt(jnp.mean(pre * pre, axis=-1, keepdims=True) + EPSILON)
        unit = pre * scale_row
        gain_grad = jnp.sum(turned * unit, axis=0, keepdims=True)
        turned = turned * gain
        inner = jnp.mean(turned * unit, axis=-1, keepdims=True)
        return scale_row * (turned - unit * inner), gain_grad

    for block in range(blocks):

        @pl.when(pl.program_id(1) == block)
        def _(block=block):
            keys = (block + 1) * size
            rows = slice(block * size, keys)
            scores = masked_scores(q_ref, k_ref, seg_row_ref, seg_col_ref, block, keys)
            weights = jnp.exp(scores - log_ref[0])
            grads = dot_nt(v_ref[:keys], do_ref[...])
            inner = jnp.sum(weights * grads, axis=0, keepdims=True)
            score_grads = (weights * (grads - inner)).astype(BF16)
            value_sum[:keys] += jnp.dot(
                weights.astype(BF16), do_ref[...], preferred_element_type=F32
            )
            key_sum[:keys] += jnp.dot(score_grads, q_ref[...], preferred_element_type=F32)
            query_grad = jnp.dot(kt_ref[:, :keys], score_grads, preferred_element_type=F32)
            pre_grad, gain_grad = pull(
                query_grad.T * scale, qpre_ref[...], gq_ref[...], cos_ref[rows], sin_ref[rows]
            )
            dq_ref[...] = pre_grad.astype(BF16)
            dgain_ref[0:1] += gain_grad

    @pl.when(last)
    def _():
        pre_grad, gain_grad = pull(
            key_sum[...] * scale, kpre_ref[...], gk_ref[...], cos_ref[...], sin_ref[...]
        )
        dk_ref[...] = pre_grad.astype(BF16)
        dgain_ref[1:2] = gain_grad
        dv_ref[...] = value_sum[...].astype(BF16)


def attend_back(query, key, value, grad, logs, segment, qpre, kpre, cos, sin, gq, gk):
    length, cols = query.shape
    head = key.shape[1]
    block = Q_BLOCK
    heads = cols // head
    tile = pl.BlockSpec((block, head), lambda h, i: (i, h))

    def fixed(*shape):
        return pl.BlockSpec(shape, lambda h, i: (0, 0))

    return pl.pallas_call(
        attend_back_kernel,
        grid=(heads, length // block),
        in_specs=[
            tile,
            fixed(length, head),
            fixed(head, length),
            fixed(length, head),
            tile,
            pl.BlockSpec((1, 1, block), lambda h, i: (h, 0, i)),
            pl.BlockSpec((1, block), lambda h, i: (0, i)),
            fixed(length, 1),
            tile,
            fixed(length, head),
            fixed(length, head),
            fixed(length, head),
            fixed(1, head),
            fixed(1, head),
        ],
        out_specs=[tile, fixed(length, head), fixed(length, head), fixed(8, head)],
        out_shape=[
            jax.ShapeDtypeStruct((length, cols), BF16),
            jax.ShapeDtypeStruct((length, head), BF16),
            jax.ShapeDtypeStruct((length, head), BF16),
            jax.ShapeDtypeStruct((8, head), F32),
        ],
        scratch_shapes=[pltpu.VMEM((length, head), F32), pltpu.VMEM((length, head), F32)],
        compiler_params=pltpu.CompilerParams(vmem_limit_bytes=VMEM_BYTES),
        cost_estimate=FREE,
    )(
        query,
        key,
        key.T,
        value,
        grad,
        logs,
        segment[None],
        segment[:, None],
        qpre,
        kpre,
        cos,
        sin,
        gq[None],
        gk[None],
    )


def on_device(
    tokens,
    segment_ids,
    routes,
    w_query,
    w_key,
    w_value,
    w_output,
    w_router,
    gain_attn,
    gain_moe,
    gain_query,
    gain_key,
    w_gate,
    w_up,
    w_down,
    cotangent,
):
    bands, peers = lax.axis_size("dp"), lax.axis_size("expert")
    band, peer = lax.axis_index("dp"), lax.axis_index("expert")
    own_tokens = tokens[0]
    tok_count, width = own_tokens.shape
    band_rows = w_query.shape[0]
    experts = w_router.shape[1]
    gain_rows = gain_query.shape[0]
    head_size = gain_rows * bands * peers
    heads = w_query.shape[1] // head_size // bands
    q_cols, k_cols = heads * head_size, head_size
    qkv_cols = q_cols + 2 * k_cols
    owned = experts // peers

    small = jnp.concatenate(
        [
            w_router,
            gain_attn[:, None],
            gain_moe[:, None],
            jnp.pad(gain_query, (0, band_rows - gain_rows))[:, None],
            jnp.pad(gain_key, (0, band_rows - gain_rows))[:, None],
        ],
        axis=1,
    )
    small = jnp.pad(small, ((0, 0), (0, 128 - small.shape[1])))
    packed = jnp.concatenate(
        [
            w_query.reshape(band_rows, bands, q_cols),
            w_key.reshape(band_rows, bands, k_cols),
            w_value.reshape(band_rows, bands, k_cols),
            jnp.broadcast_to(small[:, None], (band_rows, bands, 128)),
        ],
        axis=-1,
    ).transpose(1, 0, 2)
    tokens_all, packed_all, out_w = start_moves(own_tokens, packed, w_output)
    qkv_w = packed_all[:, :qkv_cols]
    small_all = packed_all[:, qkv_cols:]
    router_full = small_all[:, :experts]
    attn_gain = small_all[:, experts].astype(F32)
    moe_gain = small_all[:, experts + 1].astype(F32)
    head_gains = small_all.reshape(bands * peers, band_rows, 128)[:, :gain_rows]
    query_gain = head_gains[:, :, experts + 2].reshape(-1).astype(F32)
    key_gain = head_gains[:, :, experts + 3].reshape(-1).astype(F32)
    shared = owned >= bands == 4
    top = routes.shape[-1]

    def beside(rows, *sides):
        used = sum(side.shape[-1] for side in sides)
        filler = jnp.zeros((tok_count, SIDE - used), BF16)
        return jnp.concatenate([rows, *(side.astype(BF16) for side in sides), filler], axis=1)

    def side_gates(sides):
        gates = sides[..., :experts].astype(F32)
        gates = gates + sides[..., experts : 2 * experts].astype(F32)
        return lax.dynamic_slice_in_dim(gates, peer * owned, owned, axis=2)

    cot_rows = beside(after(cotangent[0], out_w), routes[0])
    if shared:
        cot_all = lax.all_gather(cot_rows, ("dp", "expert"), axis=0, tiled=False)
        cot_all = cot_all.reshape(bands, peers, tok_count, -1)
    else:
        cot_all = lax.all_gather(cot_rows, "expert", axis=0)[None]
    here = band if shared else 0

    inputs = own_tokens.astype(F32)
    length = tokens_all.shape[0]
    half = head_size // 2
    frequency = ROPE_BASE ** (-jnp.arange(half, dtype=F32) * 2.0 / head_size)
    angles = jnp.arange(length, dtype=jnp.int32).astype(F32)[:, None] * frequency[None, :]
    cos = jnp.concatenate([jnp.cos(angles)] * 2, axis=-1)
    sin = jnp.concatenate([-jnp.sin(angles), jnp.sin(angles)], axis=-1)
    normed, query_pre, key_pre, query_low, key_low, value_low = make_qkv(
        tokens_all, attn_gain, packed_all, cos, sin, query_gain, key_gain
    )
    segment = segment_ids[0]
    attended_low, log_total = attend(query_low, key_low, value_low, segment)
    branch = dot("tm,md->td", attended_low, out_w).astype(BF16)
    branch = sum_blocks(branch.reshape(bands, tok_count, width), "dp")
    hidden = inputs + branch

    normed_moe_f, moe_pull = jax.vjp(norm_rows, hidden, moe_gain)
    normed_moe = normed_moe_f.astype(BF16)
    mask = jnp.any(routes[0][..., None] == jnp.arange(experts, dtype=jnp.int32), axis=1)
    own_gates = masked_softmax(dot("td,de->te", normed_moe, router_full), mask)
    high = own_gates.astype(BF16)
    low = own_gates - high.astype(F32)
    moe_rows = beside(normed_moe, high, low)
    moe_all = gather_square(moe_rows) if shared else gather_rows(moe_rows)[None]
    cot_all = after(cot_all, moe_all)

    def in_order(columns):
        pick = [
            lax.dynamic_index_in_dim(columns, here ^ i, 0, keepdims=False)
            for i in range(len(columns))
        ]
        return jnp.concatenate(pick)

    routes_all = in_order(cot_all[..., width : width + top]).astype(jnp.int32)
    ranks_all = block_ranks(routes_all, peer, owned, experts)
    own_ranks = ranks_all[:peers]
    token_ranks = own_ranks.transpose(0, 2, 1)
    cot_placed = place_rows(ranks_all, cot_all, here).reshape(owned, -1, width)
    x_placed = place_rows(ranks_all, moe_all, here).reshape(owned, -1, width)
    all_gates = slot_values(ranks_all, side_gates(in_order(moe_all[..., width:])))
    all_gates = all_gates.transpose(1, 0, 2).reshape(owned, -1, 1)
    *own, slot_grads, rows_back, rows_out = own_experts(
        x_placed,
        cot_placed,
        all_gates,
        peers * CAP,
        w_gate,
        w_up,
        w_down,
    )
    if not shared:
        active, gate_low, up_low = own
        expert_sums = lax.psum(
            (
                dot("erd,erf->edf", x_placed, gate_low).astype(BF16),
                dot("erd,erf->edf", x_placed, up_low).astype(BF16),
                dot("erf,erd->efd", active, cot_placed).astype(BF16),
            ),
            "dp",
        )
    rows_back = combine(token_ranks, rows_back)
    back = lax.psum_scatter(rows_back, "expert", scatter_dimension=0, tiled=True)[0]
    slot_grads = slot_grads.reshape(owned, peers, CAP).transpose(1, 0, 2)
    slots = jnp.arange(CAP, dtype=jnp.int32)[None, None, :, None]
    token_grads = jnp.where(own_ranks[:, :, None, :] == slots, slot_grads[..., None], 0.0)
    token_grads = jnp.sum(token_grads, axis=2)
    gate_grads = (
        lax.all_to_all(token_grads, "expert", split_axis=0, concat_axis=0, tiled=True)
        .reshape(experts, tok_count)
        .T
    )
    rows_out = combine(after(token_ranks, rows_back), rows_out)

    expert_sums = None if shared else expert_sums

    def next_expert(number, sums, *earlier):
        if not shared or number >= owned:
            return sums, earlier[0]
        *sums, mark = expert_grads(
            x_placed,
            cot_placed,
            after(all_gates, *earlier),
            own,
            w_gate,
            w_up,
            w_down,
            number,
            sums,
        )
        return sums, mark

    expert_sums, mark = next_expert(0, expert_sums, rows_out)
    back = after(back, mark)

    grad_logits = own_gates * (
        gate_grads - jnp.sum(own_gates * gate_grads, axis=-1, keepdims=True)
    )
    grad_router_w = jnp.einsum("td,te->de", normed_moe.astype(F32), grad_logits, precision=PRECISE)
    grad_normed = back.astype(F32) + jnp.einsum(
        "te,de->td", grad_logits, router_full.astype(F32), precision=PRECISE
    )
    grad_hidden_n, grad_moe_gain = moe_pull(grad_normed)
    grad_hidden = cotangent[0].astype(F32) + grad_hidden_n
    grad_branch = grad_hidden.astype(BF16)
    branch_all = lax.all_gather(grad_branch, "dp", axis=0, tiled=True)
    expert_sums, mark = next_expert(1, expert_sums, grad_branch)
    branch_all = after(branch_all, mark)

    grad_attended = dot("td,md->tm", branch_all, out_w).astype(BF16)
    query_grad, key_grad, value_grad, head_grads = attend_back(
        query_low,
        key_low,
        value_low,
        grad_attended,
        log_total,
        segment,
        query_pre,
        key_pre,
        cos,
        sin,
        query_gain,
        key_gain,
    )
    qkv_grad = jnp.concatenate([query_grad, key_grad, value_grad], axis=1)
    grad_normed_attn = dot("tm,dm->td", qkv_grad, qkv_w).astype(BF16)
    expert_sums, mark = next_expert(2, expert_sums, grad_normed_attn)
    grad_normed_attn = lax.psum_scatter(
        grad_normed_attn, "dp", scatter_dimension=0, tiled=True
    )
    grad_normed_attn = after(grad_normed_attn, mark).astype(F32)
    _, attn_pull = jax.vjp(norm_rows, inputs, attn_gain)
    grad_inputs_n, grad_attn_gain = attn_pull(grad_normed_attn)
    grad_tokens = grad_hidden + grad_inputs_n

    whole_gains = jnp.stack([grad_attn_gain, grad_moe_gain], axis=1)
    head_gains = head_grads[:2].T
    head_gains = jnp.pad(
        head_gains.reshape(bands * peers, gain_rows, 2),
        ((0, 0), (0, band_rows - gain_rows), (0, 0)),
    )
    small_grad = jnp.concatenate(
        [grad_router_w, whole_gains, head_gains.reshape(width, 2)], axis=1
    )
    small_grad = jnp.pad(small_grad, ((0, 0), (0, 128 - small_grad.shape[1])))
    band_qkv = jnp.concatenate([dot("td,tm->dm", normed, qkv_grad), small_grad], axis=1)
    band_qkv = band_qkv.astype(BF16).reshape(bands, peers, band_rows, -1).transpose(1, 0, 2, 3)
    for number in range(3, owned):
        expert_sums, mark = next_expert(number, expert_sums, band_qkv)
    band_qkv = lax.psum_scatter(
        band_qkv.reshape(width, -1), "expert", scatter_dimension=0, tiled=True
    ).reshape(bands, band_rows, -1)
    band_qkv = after(band_qkv, mark)
    band_qkv = lax.all_to_all(band_qkv, "dp", split_axis=0, concat_axis=0, tiled=True).transpose(
        1, 0, 2
    )
    grad_query = band_qkv[:, :, :q_cols].astype(F32).reshape(band_rows, -1)
    grad_key = band_qkv[:, :, q_cols : q_cols + k_cols].astype(F32).reshape(band_rows, -1)
    grad_value = band_qkv[:, :, q_cols + k_cols : qkv_cols].astype(F32).reshape(band_rows, -1)
    smaller = jnp.sum(band_qkv[:, :, qkv_cols:].astype(F32), axis=1)
    grad_output = sum_peers(
        dot("tm,td->md", attended_low, branch_all).astype(BF16).reshape(peers, -1, width)
    )

    moe_sum = sum_peers(after(rows_out, branch_all))
    block_out = (hidden + moe_sum).astype(BF16)
    return (
        block_out[None],
        grad_tokens[None],
        grad_query,
        grad_key,
        grad_value,
        grad_output,
        smaller[:, :experts],
        smaller[:, experts],
        smaller[:, experts + 1],
        smaller[:gain_rows, experts + 2],
        smaller[:gain_rows, experts + 3],
        expert_sums[0].astype(F32),
        expert_sums[1].astype(F32),
        expert_sums[2].astype(F32),
    )


def solution(mesh):
    both = ("dp", "expert")
    return jax.shard_map(
        on_device,
        mesh=mesh,
        in_specs=(
            P("expert", "dp", None),
            P("expert", None),
            P("expert", "dp", None),
            P(both, None),
            P(both, None),
            P(both, None),
            P(both, None),
            P(both, None),
            P(both),
            P(both),
            P(both),
            P(both),
            P("expert", None, None),
            P("expert", None, None),
            P("expert", None, None),
            P("expert", "dp", None),
        ),
        out_specs=(
            P("expert", "dp", None),
            P("expert", "dp", None),
            P(both, None),
            P(both, None),
            P(both, None),
            P(both, None),
            P(both, None),
            P(both),
            P(both),
            P(both),
            P(both),
            P("expert", None, None),
            P("expert", None, None),
            P("expert", None, None),
        ),
        check_vma=False,
    )
```

```python
import jax
import jax.numpy as jnp
from jax import lax
from jax.experimental import pallas as pl
from jax.experimental.pallas import tpu as pltpu
from jax.sharding import PartitionSpec as P

CAP = 80
Q_BLOCK = 256
HIDDEN_TILE = 256
OWN_ROWS = 8 * CAP
WIDTH_TILE = 512
SIDE = 128
ROW_PARTS = 2
VMEM_BYTES = 60 << 20


EPSILON = 1e-06
ROPE_BASE = 1000000.0
PRECISE = lax.Precision.HIGHEST
F32 = jnp.float32
BF16 = jnp.bfloat16
FREE = pl.CostEstimate(flops=0, bytes_accessed=0, transcendentals=0)


def norm_rows(values, gain_row):
    return (
        values * lax.rsqrt(jnp.mean(values * values, axis=-1, keepdims=True) + EPSILON) * gain_row
    )


def activate(gate_vals, up_vals):
    return gate_vals * jax.nn.sigmoid(gate_vals) * up_vals


def masked_softmax(logits, mask):
    kept = jnp.where(mask, logits, -jnp.inf)
    largest = jnp.max(kept, axis=-1, keepdims=True)
    raised = jnp.where(mask, jnp.exp(logits - largest), 0.0)
    return raised / jnp.sum(raised, axis=-1, keepdims=True)


def nothing(*refs):
    del refs


def after(value, *others):
    anywhere = pl.BlockSpec(memory_space=pl.ANY)
    return pl.pallas_call(
        nothing,
        out_shape=jax.ShapeDtypeStruct(value.shape, value.dtype),
        in_specs=[anywhere] * (1 + len(others)),
        out_specs=anywhere,
        input_output_aliases={0: 0},
    )(value, *others)


def shifted(value, axis, step):
    count = lax.axis_size(axis)
    return lax.ppermute(value, axis, [(i, (i + step) % count) for i in range(count)])


def traded(value, axis, step):
    return lax.ppermute(value, axis, [(i, i ^ step) for i in range(lax.axis_size(axis))])


def gather_blocks(own, axis):
    count, me = lax.axis_size(axis), lax.axis_index(axis)
    whole = jnp.zeros((count, *own.shape), own.dtype)
    whole = lax.dynamic_update_index_in_dim(whole, own, me, 0)
    for step in range(1, count):
        whole = lax.dynamic_update_index_in_dim(whole, traded(own, axis, step), me ^ step, 0)
    return whole


def sum_blocks(blocks, axis):
    count, me = lax.axis_size(axis), lax.axis_index(axis)
    total = lax.dynamic_index_in_dim(blocks, me, 0, keepdims=False).astype(F32)
    for step in range(1, count):
        sent = lax.dynamic_index_in_dim(blocks, me ^ step, 0, keepdims=False)
        total = total + traded(sent, axis, step).astype(F32)
    return total


def sum_cores(blocks):
    count, me = lax.axis_size("expert"), lax.axis_index("expert")
    core, chips = lax.rem(me, 2), count // 2
    paired = blocks.reshape(chips, 2, *blocks.shape[1:])
    sent = lax.dynamic_index_in_dim(paired, 1 - core, 1, keepdims=False)
    kept = lax.dynamic_index_in_dim(paired, core, 1, keepdims=False)
    got = lax.ppermute(sent, "expert", [(i, i ^ 1) for i in range(count)])
    return (kept.astype(F32) + got.astype(F32)).astype(BF16)


def sum_chips(halves):
    me = lax.axis_index("expert")
    chip, chips = lax.div(me, 2), lax.axis_size("expert") // 2
    total = lax.dynamic_index_in_dim(halves, chip, 0, keepdims=False).astype(F32)
    for step in range(1, chips):
        sent = lax.dynamic_index_in_dim(halves, lax.rem(chip + step, chips), 0, keepdims=False)
        total = total + shifted(sent, "expert", 2 * step).astype(F32)
    return total


def dot(spec, left, right):
    return jnp.einsum(spec, left, right, preferred_element_type=F32)


def line_sems(chips):
    return [pltpu.SemaphoreType.DMA((chips,))] * 6 + [pltpu.SemaphoreType.DMA]


def send_to(source, target, send_sem, recv_sem, device):
    return pltpu.make_async_remote_copy(
        src_ref=source,
        dst_ref=target,
        send_sem=send_sem,
        recv_sem=recv_sem,
        device_id=device,
        device_id_type=pl.DeviceIdType.MESH,
    )


def greet(devices, conditions):
    barrier = pltpu.get_barrier_semaphore()
    for device, condition in zip(devices, conditions):

        @pl.when(condition)
        def _(device=device):
            pl.semaphore_signal(
                barrier, inc=1, device_id=device, device_id_type=pl.DeviceIdType.MESH
            )

    pl.semaphore_wait(barrier, sum(condition.astype(jnp.int32) for condition in conditions))


def expert_place():
    me = lax.axis_index("expert")
    return me, lax.div(me, 2), lax.rem(me, 2), lax.axis_size("expert") // 2


def line_partners():
    me, chip, core, chips = expert_place()
    band = lax.axis_index("dp")
    devices = [(band, me + 1 - 2 * core), (band, me + 2), (band, me - 2)]
    return devices, [chip >= 0, chip < chips - 1, chip > 0]


class Line:
    def __init__(self, own, slot, sems):
        self.own, self.slot = own, slot
        self.up_out, self.up_in, self.down_out, self.down_in, self.side_out, self.side_in, self.self_sem = sems
        self.me, self.chip, self.core, self.chips = expert_place()
        (self.twin, self.up, self.down), _ = line_partners()

    def local(self):
        return pltpu.make_async_copy(self.own, self.slot(self.me), self.self_sem)

    def side(self, source, block):
        return send_to(
            source,
            self.slot(2 * block + self.core),
            self.side_out.at[block],
            self.side_in.at[block],
            self.twin,
        )

    def upward(self, source, block, step):
        return send_to(
            source,
            self.slot(2 * block + self.core),
            self.up_out.at[step],
            self.up_in.at[step],
            self.up,
        )

    def downward(self, source, block, step):
        return send_to(
            source,
            self.slot(2 * block + self.core),
            self.down_out.at[step],
            self.down_in.at[step],
            self.down,
        )

    def begin(self):
        self.local().start()

        @pl.when(self.chip < self.chips - 1)
        def _():
            self.upward(self.own, self.chip, 0).start()

        @pl.when(self.chip > 0)
        def _():
            self.downward(self.own, self.chip, 0).start()

        self.side(self.own, self.chip).start()

    def advance(self, step):
        below, above = self.chip - 1 - step, self.chip + 1 + step

        @pl.when(below >= 0)
        def _():
            held = self.slot(2 * below + self.core)
            self.upward(held, below, step).wait_recv()

            if step + 1 < self.chips - 1:

                @pl.when(self.chip < self.chips - 1)
                def _():
                    self.upward(held, below, step + 1).start()

            self.side(held, below).start()

        @pl.when(above < self.chips)
        def _():
            held = self.slot(2 * above + self.core)
            self.downward(held, above, step).wait_recv()

            if step + 1 < self.chips - 1:

                @pl.when(self.chip > 0)
                def _():
                    self.downward(held, above, step + 1).start()

            self.side(held, above).start()

    def finish(self):
        self.local().wait()
        for step in range(self.chips - 1):

            @pl.when((self.chip < self.chips - 1) & (self.chip >= step))
            def _(step=step):
                block = self.chip - step
                self.upward(self.slot(2 * block + self.core), block, step).wait_send()

            @pl.when((self.chip > 0) & (self.chip + step < self.chips))
            def _(step=step):
                block = self.chip + step
                self.downward(self.slot(2 * block + self.core), block, step).wait_send()

        for block in range(self.chips):
            self.side(self.slot(2 * block + self.core), block).wait_send()
            send_to(
                self.slot(2 * block + self.core),
                self.slot(2 * block + 1 - self.core),
                self.side_out.at[block],
                self.side_in.at[block],
                self.twin,
            ).wait_recv()


def rows_kernel(own_ref, all_ref, *sems):
    greet(*line_partners())
    line = Line(own_ref, lambda i: all_ref.at[i], sems)
    line.begin()
    for step in range(line.chips - 1):
        line.advance(step)
    line.finish()


def gather_rows(own):
    peers = lax.axis_size("expert")
    anywhere = pl.BlockSpec(memory_space=pl.ANY)
    return pl.pallas_call(
        rows_kernel,
        out_shape=jax.ShapeDtypeStruct((peers, *own.shape), own.dtype),
        in_specs=[anywhere],
        out_specs=anywhere,
        scratch_shapes=line_sems(peers // 2),
        compiler_params=pltpu.CompilerParams(collective_id=1, has_side_effects=True),
    )(own)


def square_kernel(own_ref, all_ref, *sems):
    band, me = lax.axis_index("dp"), lax.axis_index("expert")
    outs, arrivals, twin_out, twin_in = sems[:3], sems[3:6], sems[6], sems[7]
    columns = [(band ^ 1, me), (band ^ 2, me)]
    devices, conditions = line_partners()
    greet(devices + columns, conditions + [band >= 0] * 2)
    line = Line(own_ref, lambda i: all_ref.at[band, i], sems[8:])
    chip, chips, core = line.chip, line.chips, line.core

    def across(source, block, step):
        return send_to(
            source,
            all_ref.at[band, 2 * block + core],
            outs[step - 1].at[block],
            arrivals[step - 1].at[block],
            (band ^ step, me),
        )

    def held(block, step):
        return all_ref.at[band ^ step, 2 * block + core]

    def arrive(block, step):
        send_to(
            own_ref,
            held(block, step),
            outs[step - 1].at[block],
            arrivals[step - 1].at[block],
            (band ^ step, me),
        ).wait_recv()

    def onward(block, step):
        return send_to(
            held(block, step),
            held(block, step),
            outs[2].at[block],
            arrivals[2].at[block],
            (band ^ (3 - step), me),
        )

    def twin(block, step):
        place = (step - 1) * chips + block
        return send_to(
            held(block, step),
            held(block, step),
            twin_out.at[place],
            twin_in.at[place],
            line.twin,
        )

    def spread(source, block):
        across(source, block, 1).start()
        across(source, block, 2).start()

    def receive(block):
        for step in (1, 2):
            arrive(block, step)

            @pl.when(lax.rem(block, 2) == step - 1)
            def _(step=step):
                onward(block, step).start()

            twin(block, step).start()

    line.begin()
    spread(own_ref, chip)
    for step in range(chips - 1):
        line.advance(step)
        below, above = chip - 1 - step, chip + 1 + step

        @pl.when(below >= 0)
        def _(below=below):
            spread(line.slot(2 * below + core), below)

        @pl.when(above < chips)
        def _(above=above):
            spread(line.slot(2 * above + core), above)

    receive(chip)
    for step in range(chips - 1):
        below, above = chip - 1 - step, chip + 1 + step

        @pl.when(below >= 0)
        def _(below=below):
            receive(below)

        @pl.when(above < chips)
        def _(above=above):
            receive(above)

    for block in range(chips):
        arrive(block, 3)
        twin(block, 3).start()
    line.finish()
    for block in range(chips):
        across(own_ref, block, 1).wait_send()
        across(own_ref, block, 2).wait_send()
        onward(block, 1).wait_send()
        for step in (1, 2, 3):
            place = (step - 1) * chips + block
            twin(block, step).wait_send()
            there = all_ref.at[band ^ step, 2 * block + 1 - core]
            send_to(there, there, twin_out.at[place], twin_in.at[place], line.twin).wait_recv()


def gather_square(own):
    bands, peers = lax.axis_size("dp"), lax.axis_size("expert")
    chips = peers // 2
    anywhere = pl.BlockSpec(memory_space=pl.ANY)
    return pl.pallas_call(
        square_kernel,
        out_shape=jax.ShapeDtypeStruct((bands, peers, *own.shape), own.dtype),
        in_specs=[anywhere],
        out_specs=anywhere,
        scratch_shapes=[pltpu.SemaphoreType.DMA((chips,))] * 6
        + [pltpu.SemaphoreType.DMA((3 * chips,))] * 2
        + line_sems(chips),
        compiler_params=pltpu.CompilerParams(collective_id=2, has_side_effects=True),
    )(own)


def start_kernel(
    tok_ref, pack_ref, wo_ref, tokens_ref, swap_ref, pack_all_ref, wo_all_ref, *sems
):
    bands, band = lax.axis_size("dp"), lax.axis_index("dp")
    me = lax.axis_index("expert")
    tok_out, tok_in, swap_out, swap_in, self_sems = sems[:5]
    pack_sems, wo_sems = sems[5:12], sems[12:]
    columns = [(band ^ step, me) for step in range(1, bands)]
    devices, conditions = line_partners()
    greet(devices + columns, conditions + [band >= 0] * (bands - 1))
    own_tok = pltpu.make_async_copy(tok_ref, tokens_ref.at[band], self_sems.at[0])
    own_swap = pltpu.make_async_copy(pack_ref.at[band], swap_ref.at[band], self_sems.at[1])
    own_swap.start()
    own_tok.start()

    def swap(step):
        other = band ^ step
        return send_to(
            pack_ref.at[other],
            swap_ref.at[band],
            swap_out.at[step - 1],
            swap_in.at[step - 1],
            (other, me),
        )

    def token(step):
        other = band ^ step
        return send_to(
            tok_ref, tokens_ref.at[band], tok_out.at[step - 1], tok_in.at[step - 1], (other, me)
        )

    def arrived(step, source, target, out, arrival):
        other = band ^ step
        send_to(
            source, target.at[other], out.at[step - 1], arrival.at[step - 1], (other, me)
        ).wait_recv()

    for step in range(1, bands):
        swap(step).start()
    wo_line = Line(wo_ref, lambda i: wo_all_ref.at[i], wo_sems)
    wo_line.begin()
    for step in range(1, bands):
        token(step).start()
    own_swap.wait()
    for step in range(1, bands):
        arrived(step, pack_ref.at[band], swap_ref, swap_out, swap_in)
    pack_line = Line(swap_ref, lambda i: pack_all_ref.at[:, i], pack_sems)
    pack_line.begin()
    for step in range(pack_line.chips - 1):
        wo_line.advance(step)
        pack_line.advance(step)
    wo_line.finish()
    pack_line.finish()
    own_tok.wait()
    for step in range(1, bands):
        arrived(step, tok_ref, tokens_ref, tok_out, tok_in)
        token(step).wait_send()
        swap(step).wait_send()


def start_moves(tokens, packed, w_output):
    bands, peers = lax.axis_size("dp"), lax.axis_size("expert")
    anywhere = pl.BlockSpec(memory_space=pl.ANY)
    chips = peers // 2
    shapes = [
        (bands, *tokens.shape),
        packed.shape,
        (bands, peers, *packed.shape[1:]),
        (peers, *w_output.shape),
    ]
    tokens_all, _, packed_all, output_all = pl.pallas_call(
        start_kernel,
        out_shape=[jax.ShapeDtypeStruct(shape, BF16) for shape in shapes],
        in_specs=[anywhere] * 3,
        out_specs=[anywhere] * 4,
        scratch_shapes=[pltpu.SemaphoreType.DMA((bands - 1,))] * 4
        + [pltpu.SemaphoreType.DMA((2,))]
        + line_sems(chips) * 2,
        compiler_params=pltpu.CompilerParams(collective_id=0, has_side_effects=True),
    )(tokens, packed, w_output)
    width = tokens.shape[1]
    return (
        tokens_all.reshape(-1, width),
        packed_all.reshape(-1, packed.shape[-1]),
        output_all.reshape(-1, width),
    )


def block_ranks(routes, peer, owned, experts):
    chosen = jnp.any(routes[..., None] == jnp.arange(experts, dtype=jnp.int32), axis=2)
    chosen = lax.dynamic_slice_in_dim(chosen, peer * owned, owned, axis=2)
    tok_count = chosen.shape[1]
    earlier = jnp.tril(jnp.ones((tok_count, tok_count), BF16), -1)
    ranks = dot("ts,bse->bet", earlier, chosen.astype(BF16)).astype(jnp.int32)
    return jnp.where(chosen.transpose(0, 2, 1), ranks, -1)


def slot_values(ranks, values):
    slots = jnp.arange(CAP, dtype=jnp.int32)
    chosen = ranks[:, :, None, :] == slots[None, None, :, None]
    return jnp.sum(jnp.where(chosen, values.transpose(0, 2, 1)[:, :, None, :], 0.0), axis=-1)


def by_core(values, core):
    paired = values.reshape(-1, 2, *values.shape[1:])
    return lax.dynamic_index_in_dim(paired, core, 1, keepdims=False)


def place_kernel(_, rank_ref, block_ref, rows_ref):
    count, owned, tok_count = rank_ref.shape
    slots = lax.broadcasted_iota(jnp.int32, (CAP, tok_count), 0)
    width = block_ref.shape[-1]
    for block in range(count):
        ranks = rank_ref[block]
        hot = jnp.concatenate([ranks[e : e + 1] == slots for e in range(owned)], axis=0)
        hot = jnp.where(hot, 1.0, 0.0).astype(BF16)
        for start in range(0, width, WIDTH_TILE):
            cols = slice(start, start + WIDTH_TILE)
            rows = jnp.dot(hot, block_ref[0, block, :, cols], preferred_element_type=F32)
            rows_ref[:, block, :, cols] = rows.astype(BF16).reshape(owned, CAP, WIDTH_TILE)


def place_rows(ranks, columns, first):
    total, owned, tok_count = ranks.shape
    peers = columns.shape[1]
    width = columns.shape[-1] - SIDE
    several = 2
    steps = peers // several

    def block_at(b, at):
        return lax.bitwise_xor(at[0], lax.div(b, steps)), lax.rem(b, steps), 0, 0

    return pl.pallas_call(
        place_kernel,
        grid_spec=pltpu.PrefetchScalarGridSpec(
            num_scalar_prefetch=1,
            grid=(total // several,),
            in_specs=[
                pl.BlockSpec((several, owned, tok_count), lambda b, at: (b, 0, 0)),
                pl.BlockSpec((1, several, tok_count, width), block_at),
            ],
            out_specs=pl.BlockSpec((owned, several, CAP, width), lambda b, at: (0, b, 0, 0)),
        ),
        out_shape=jax.ShapeDtypeStruct((owned, total, CAP, width), BF16),
        compiler_params=pltpu.CompilerParams(vmem_limit_bytes=VMEM_BYTES),
        cost_estimate=FREE,
    )(jnp.asarray(first, jnp.int32).reshape(1), ranks, columns)


def combine_kernel(rank_ref, rows_ref, out_ref):
    tok_count, owned = rank_ref.shape[1:]
    slots = owned * CAP
    width = out_ref.shape[-1]
    lane = lax.broadcasted_iota(jnp.int32, (tok_count, slots), 1)
    hot = jnp.zeros((tok_count, slots), F32)
    for e in range(owned):
        ranks = rank_ref[0, :, e : e + 1]
        hot = jnp.where((ranks >= 0) & (lane == ranks + e * CAP), 1.0, hot)
    hot = hot.astype(BF16)
    for start in range(0, width, WIDTH_TILE):
        cols = slice(start, start + WIDTH_TILE)
        rows = rows_ref[:, 0, :, cols].reshape(slots, WIDTH_TILE)
        out_ref[0, :, cols] = jnp.dot(hot, rows, preferred_element_type=F32).astype(BF16)


def combine(ranks, rows):
    count, tok_count, owned = ranks.shape
    width = rows.shape[-1]
    return pl.pallas_call(
        combine_kernel,
        grid=(count,),
        out_shape=jax.ShapeDtypeStruct((count, tok_count, width), BF16),
        in_specs=[
            pl.BlockSpec((1, tok_count, owned), lambda b: (b, 0, 0)),
            pl.BlockSpec((owned, 1, CAP, width), lambda b: (0, b, 0, 0)),
        ],
        out_specs=pl.BlockSpec((1, tok_count, width), lambda b: (b, 0, 0)),
        compiler_params=pltpu.CompilerParams(vmem_limit_bytes=VMEM_BYTES),
        cost_estimate=FREE,
    )(ranks, rows.reshape(owned, count, CAP, width))


def dot_nt(left, right):
    return lax.dot_general(left, right, (((1,), (1,)), ((), ())), preferred_element_type=F32)


def hidden_grads(x, c, gates, wg_ref, wu_ref, wd_ref):
    gate_in = jnp.dot(x, wg_ref[0], preferred_element_type=F32)
    up_in = jnp.dot(x, wu_ref[0], preferred_element_type=F32)
    raw = dot_nt(c, wd_ref[0])
    sig = 1.0 / (1.0 + jnp.exp(-gate_in))
    silu = gate_in * sig
    active = silu * up_in
    grad = raw * gates
    gate_grad = grad * up_in * (sig + silu * (1.0 - sig))
    up_grad = grad * silu
    return (active * gates).astype(BF16), gate_grad.astype(BF16), up_grad.astype(BF16), active * raw


def own_kernel(
    x_ref,
    c_ref,
    g_ref,
    wg_ref,
    wu_ref,
    wd_ref,
    active_ref,
    gate_ref,
    up_ref,
    slot_ref,
    back_ref,
    out_ref,
    back_sum,
    out_sum,
):
    width = x_ref.shape[-1]
    step = pl.program_id(2)
    active, gate_grad, up_grad, slot = hidden_grads(
        x_ref[0], c_ref[0], g_ref[0], wg_ref, wu_ref, wd_ref
    )
    active_ref[0] = active
    gate_ref[0] = gate_grad
    up_ref[0] = up_grad
    slot = jnp.sum(slot, axis=1, keepdims=True)
    slot_ref[0] = jnp.where(step == 0, slot, slot_ref[0] + slot)
    for start in range(0, width, WIDTH_TILE):
        cols = slice(start, start + WIDTH_TILE)
        rows = dot_nt(gate_ref[0], wg_ref[0, cols, :]) + dot_nt(up_ref[0], wu_ref[0, cols, :])
        back_sum[:, cols] = jnp.where(step == 0, rows, back_sum[:, cols] + rows)
        rows = jnp.dot(active_ref[0], wd_ref[0, :, cols], preferred_element_type=F32)
        out_sum[:, cols] = jnp.where(step == 0, rows, out_sum[:, cols] + rows)

    @pl.when(step == pl.num_programs(2) - 1)
    def _():
        back_ref[0] = back_sum[...].astype(BF16)
        out_ref[0] = out_sum[...].astype(BF16)


def own_experts(x_rows, c_rows, gates, rows, w_gate, w_up, w_down):
    owned, _, width = x_rows.shape
    hidden = w_down.shape[1]
    tile = HIDDEN_TILE
    some = min(rows, OWN_ROWS)
    whole = pl.BlockSpec((1, some, width), lambda e, r, f: (e, r, 0))
    column = pl.BlockSpec((1, some, 1), lambda e, r, f: (e, r, 0))
    part = pl.BlockSpec((1, some, tile), lambda e, r, f: (e, r, f))
    inward = pl.BlockSpec((1, width, tile), lambda e, r, f: (e, 0, f))
    outward = pl.BlockSpec((1, tile, width), lambda e, r, f: (e, f, 0))
    return pl.pallas_call(
        own_kernel,
        grid=(owned, rows // some, hidden // tile),
        in_specs=[whole, whole, column, inward, inward, outward],
        out_specs=[part, part, part, column, whole, whole],
        out_shape=[jax.ShapeDtypeStruct((owned, rows, hidden), BF16)] * 3
        + [jax.ShapeDtypeStruct((owned, rows, 1), F32)]
        + [jax.ShapeDtypeStruct((owned, rows, width), BF16)] * 2,
        scratch_shapes=[pltpu.VMEM((some, width), F32)] * 2,
        compiler_params=pltpu.CompilerParams(vmem_limit_bytes=VMEM_BYTES),
        cost_estimate=pl.CostEstimate(
            flops=12 * owned * rows * width * hidden,
            bytes_accessed=owned * (8 * rows * width + 6 * width * hidden),
            transcendentals=owned * rows * hidden,
        ),
    )(x_rows, c_rows, gates, w_gate, w_up, w_down)


def grads_kernel(
    x_ref, c_ref, g_ref, active_ref, gate_ref, up_ref, wg_ref, wu_ref, wd_ref, *rest
):
    dg_ref, du_ref, dd_ref, mark_ref, sums, pair, actives = rest[-7:]
    mark_ref[...] = jnp.zeros_like(mark_ref)
    tile = HIDDEN_TILE
    rows, width = x_ref.shape[1:]
    own = active_ref.shape[1]
    step = pl.program_id(1)

    def keep(start, active, gate_grad, up_grad):
        part = slice(start, start + own)
        actives[:, part] = active.T
        pair[:tile, part] = gate_grad.T
        pair[tile:, part] = up_grad.T

    def work_out(start):
        part = slice(start, start + own)
        active, gate_grad, up_grad, _ = hidden_grads(
            x_ref[0, part], c_ref[0, part], g_ref[0, part], wg_ref, wu_ref, wd_ref
        )
        keep(start, active, gate_grad, up_grad)

    @pl.when(step == 0)
    def _():
        keep(0, active_ref[0], gate_ref[0], up_ref[0])

    @pl.when(step > 0)
    def _():
        work_out(0)

    for start in range(own, rows, own):
        work_out(start)

    @pl.loop(0, width // WIDTH_TILE)
    def _(c):
        cols = pl.ds(pl.multiple_of(c * WIDTH_TILE, WIDTH_TILE), WIDTH_TILE)
        grads = jnp.dot(pair[...], x_ref[0, :, cols], preferred_element_type=F32)
        sums[:, cols] = jnp.where(step == 0, grads, sums[:, cols] + grads)
        grads = jnp.dot(actives[...], c_ref[0, :, cols], preferred_element_type=F32)
        dd_ref[0, :, cols] = jnp.where(step == 0, grads, dd_ref[0, :, cols] + grads)

    @pl.when(step == pl.num_programs(1) - 1)
    def _():
        same = lax.broadcasted_iota(jnp.int32, (tile, tile), 0) == lax.broadcasted_iota(
            jnp.int32, (tile, tile), 1
        )
        same = jnp.where(same, 1.0, 0.0).astype(BF16)

        @pl.loop(0, width // tile)
        def _(c):
            cols = pl.ds(pl.multiple_of(c * tile, tile), tile)
            dg_ref[0, cols, :] = dot_nt(same, sums[:tile, cols].astype(BF16))
            du_ref[0, cols, :] = dot_nt(same, sums[tile:, cols].astype(BF16))


def expert_grads(x_rows, c_rows, gates, own, w_gate, w_up, w_down, expert, buffers=None):
    owned, rows, width = x_rows.shape
    hidden = w_down.shape[1]
    tile, parts = HIDDEN_TILE, ROW_PARTS
    part, own_rows = rows // parts, own[0].shape[1]
    shapes = [(owned, width, hidden)] * 2 + [(owned, hidden, width)]
    in_specs = [
        pl.BlockSpec((1, part, width), lambda f, r: (expert, r, 0)),
        pl.BlockSpec((1, part, width), lambda f, r: (expert, r, 0)),
        pl.BlockSpec((1, part, 1), lambda f, r: (expert, r, 0)),
        *[pl.BlockSpec((1, own_rows, tile), lambda f, r: (expert, 0, f))] * 3,
        pl.BlockSpec((1, width, tile), lambda f, r: (expert, 0, f)),
        pl.BlockSpec((1, width, tile), lambda f, r: (expert, 0, f)),
        pl.BlockSpec((1, tile, width), lambda f, r: (expert, f, 0)),
    ]
    given = (x_rows, c_rows, gates, *own, w_gate, w_up, w_down)
    aliases = {}
    if buffers is not None:
        aliases = {len(given) + i: i for i in range(3)}
        in_specs += [pl.BlockSpec(memory_space=pl.ANY)] * 3
        given += tuple(buffers)
    return pl.pallas_call(
        grads_kernel,
        grid=(hidden // tile, parts),
        out_shape=[jax.ShapeDtypeStruct(shape, F32) for shape in [*shapes, (8, 128)]],
        in_specs=in_specs,
        out_specs=[
            pl.BlockSpec((1, width, tile), lambda f, r: (expert, 0, f)),
            pl.BlockSpec((1, width, tile), lambda f, r: (expert, 0, f)),
            pl.BlockSpec((1, tile, width), lambda f, r: (expert, f, 0)),
            pl.BlockSpec((8, 128), lambda f, r: (0, 0)),
        ],
        scratch_shapes=[
            pltpu.VMEM((2 * tile, width), F32),
            pltpu.VMEM((2 * tile, part), BF16),
            pltpu.VMEM((tile, part), BF16),
        ],
        input_output_aliases=aliases,
        compiler_params=pltpu.CompilerParams(vmem_limit_bytes=VMEM_BYTES),
        cost_estimate=pl.CostEstimate(
            flops=12 * rows * width * hidden,
            bytes_accessed=12 * rows * width + 24 * width * hidden,
            transcendentals=rows * hidden,
        ),
    )(*given)


def turn(values, cos, sin):
    return values * cos + pltpu.roll(values, values.shape[-1] // 2, 1) * sin


def qkv_kernel(
    tok_ref,
    gain_ref,
    w_ref,
    cos_ref,
    sin_ref,
    gq_ref,
    gk_ref,
    normed_ref,
    qpre_ref,
    kpre_ref,
    qrot_ref,
    krot_ref,
    value_ref,
):
    head = cos_ref.shape[1]
    heads = qpre_ref.shape[1] // head
    normed = norm_rows(tok_ref[...].astype(F32), gain_ref[...]).astype(BF16)
    normed_ref[...] = normed
    cos, sin = cos_ref[...], sin_ref[...]
    for pair in range(0, heads, 2):
        cols = slice(pair * head, (pair + 2) * head)
        pre = jnp.dot(normed, w_ref[:, cols], preferred_element_type=F32)
        qpre_ref[:, cols] = pre
        for h in range(2):
            one = slice(h * head, (h + 1) * head)
            rot = turn(norm_rows(pre[:, one], gq_ref[...]), cos, sin)
            qrot_ref[:, (pair + h) * head : (pair + h + 1) * head] = rot.astype(BF16)
    cols = slice(heads * head, (heads + 2) * head)
    pre = jnp.dot(normed, w_ref[:, cols], preferred_element_type=F32)
    kpre_ref[...] = pre[:, :head]
    krot_ref[...] = turn(norm_rows(pre[:, :head], gk_ref[...]), cos, sin).astype(BF16)
    value_ref[...] = pre[:, head:].astype(BF16)


def make_qkv(tokens, gain, weight, cos, sin, query_gain, key_gain):
    length, width = tokens.shape
    head = cos.shape[1]
    cols = weight.shape[1]
    q_cols = cols - 3 * head
    block = Q_BLOCK

    def rows(size):
        return pl.BlockSpec((block, size), lambda i: (i, 0))

    def fixed(*shape):
        return pl.BlockSpec(shape, lambda i: (0, 0))

    return pl.pallas_call(
        qkv_kernel,
        grid=(length // block,),
        in_specs=[
            rows(width),
            fixed(1, width),
            fixed(width, cols),
            rows(head),
            rows(head),
            fixed(1, head),
            fixed(1, head),
        ],
        out_specs=[rows(width), rows(q_cols), rows(head), rows(q_cols), rows(head), rows(head)],
        out_shape=[
            jax.ShapeDtypeStruct((length, width), BF16),
            jax.ShapeDtypeStruct((length, q_cols), F32),
            jax.ShapeDtypeStruct((length, head), F32),
            jax.ShapeDtypeStruct((length, q_cols), BF16),
            jax.ShapeDtypeStruct((length, head), BF16),
            jax.ShapeDtypeStruct((length, head), BF16),
        ],
        compiler_params=pltpu.CompilerParams(vmem_limit_bytes=VMEM_BYTES),
        cost_estimate=FREE,
    )(tokens, gain[None], weight, cos, sin, query_gain[None], key_gain[None])


def masked_scores(q_ref, k_ref, seg_row_ref, seg_col_ref, block, keys):
    size = q_ref.shape[0]
    scores = dot_nt(k_ref[:keys], q_ref[...]) * q_ref.shape[1] ** (-0.5)
    key_at = lax.broadcasted_iota(jnp.int32, (keys, size), 0)
    query_at = lax.broadcasted_iota(jnp.int32, (keys, size), 1) + block * size
    allowed = (key_at <= query_at) & (seg_col_ref[:keys] == seg_row_ref[...])
    return jnp.where(allowed, scores, -1e30)


def attend_kernel(q_ref, k_ref, vt_ref, seg_row_ref, seg_col_ref, out_ref, log_ref):
    size = q_ref.shape[0]
    blocks = k_ref.shape[0] // size
    for block in range(blocks):

        @pl.when(pl.program_id(1) == block)
        def _(block=block):
            keys = (block + 1) * size
            scores = masked_scores(q_ref, k_ref, seg_row_ref, seg_col_ref, block, keys)
            largest = jnp.max(scores, axis=0, keepdims=True)
            raised = jnp.exp(scores - largest)
            total = jnp.sum(raised, axis=0, keepdims=True)
            weights = (raised * (1.0 / total)).astype(BF16)
            out = jnp.dot(vt_ref[:, :keys], weights, preferred_element_type=F32)
            out_ref[...] = out.T.astype(BF16)
            log_ref[0] = largest + jnp.log(total)


def attend(query, key, value, segment):
    length, cols = query.shape
    head = key.shape[1]
    block = Q_BLOCK
    heads = cols // head
    return pl.pallas_call(
        attend_kernel,
        grid=(heads, length // block),
        in_specs=[
            pl.BlockSpec((block, head), lambda h, i: (i, h)),
            pl.BlockSpec((length, head), lambda h, i: (0, 0)),
            pl.BlockSpec((head, length), lambda h, i: (0, 0)),
            pl.BlockSpec((1, block), lambda h, i: (0, i)),
            pl.BlockSpec((length, 1), lambda h, i: (0, 0)),
        ],
        out_specs=[
            pl.BlockSpec((block, head), lambda h, i: (i, h)),
            pl.BlockSpec((1, 1, block), lambda h, i: (h, 0, i)),
        ],
        out_shape=[
            jax.ShapeDtypeStruct((length, cols), BF16),
            jax.ShapeDtypeStruct((heads, 1, length), F32),
        ],
        compiler_params=pltpu.CompilerParams(vmem_limit_bytes=VMEM_BYTES),
        cost_estimate=FREE,
    )(query, key, value.T, segment[None], segment[:, None])


def attend_back_kernel(
    q_ref,
    k_ref,
    kt_ref,
    v_ref,
    do_ref,
    log_ref,
    seg_row_ref,
    seg_col_ref,
    qpre_ref,
    kpre_ref,
    cos_ref,
    sin_ref,
    gq_ref,
    gk_ref,
    dq_ref,
    dk_ref,
    dv_ref,
    dgain_ref,
    key_sum,
    value_sum,
):
    size, head = q_ref.shape
    blocks = k_ref.shape[0] // size
    scale = head ** (-0.5)
    first = (pl.program_id(0) == 0) & (pl.program_id(1) == 0)
    last = (pl.program_id(0) == pl.num_programs(0) - 1) & (pl.program_id(1) == blocks - 1)

    @pl.when(first)
    def _():
        key_sum[...] = jnp.zeros_like(key_sum)
        value_sum[...] = jnp.zeros_like(value_sum)
        dgain_ref[...] = jnp.zeros_like(dgain_ref)

    def pull(grad, pre, gain, cos, sin):
        grad = grad.astype(BF16).astype(F32)
        turned = grad * cos + pltpu.roll(grad * sin, head // 2, 1)
        scale_row = lax.rsqrt(jnp.mean(pre * pre, axis=-1, keepdims=True) + EPSILON)
        unit = pre * scale_row
        gain_grad = jnp.sum(turned * unit, axis=0, keepdims=True)
        turned = turned * gain
        inner = jnp.mean(turned * unit, axis=-1, keepdims=True)
        return scale_row * (turned - unit * inner), gain_grad

    for block in range(blocks):

        @pl.when(pl.program_id(1) == block)
        def _(block=block):
            keys = (block + 1) * size
            rows = slice(block * size, keys)
            scores = masked_scores(q_ref, k_ref, seg_row_ref, seg_col_ref, block, keys)
            weights = jnp.exp(scores - log_ref[0])
            grads = dot_nt(v_ref[:keys], do_ref[...])
            inner = jnp.sum(weights * grads, axis=0, keepdims=True)
            score_grads = (weights * (grads - inner)).astype(BF16)
            value_sum[:keys] += jnp.dot(
                weights.astype(BF16), do_ref[...], preferred_element_type=F32
            )
            key_sum[:keys] += jnp.dot(score_grads, q_ref[...], preferred_element_type=F32)
            query_grad = jnp.dot(kt_ref[:, :keys], score_grads, preferred_element_type=F32)
            pre_grad, gain_grad = pull(
                query_grad.T * scale, qpre_ref[...], gq_ref[...], cos_ref[rows], sin_ref[rows]
            )
            dq_ref[...] = pre_grad.astype(BF16)
            dgain_ref[0:1] += gain_grad

    @pl.when(last)
    def _():
        pre_grad, gain_grad = pull(
            key_sum[...] * scale, kpre_ref[...], gk_ref[...], cos_ref[...], sin_ref[...]
        )
        dk_ref[...] = pre_grad.astype(BF16)
        dgain_ref[1:2] = gain_grad
        dv_ref[...] = value_sum[...].astype(BF16)


def attend_back(query, key, value, grad, logs, segment, qpre, kpre, cos, sin, gq, gk):
    length, cols = query.shape
    head = key.shape[1]
    block = Q_BLOCK
    heads = cols // head
    tile = pl.BlockSpec((block, head), lambda h, i: (i, h))

    def fixed(*shape):
        return pl.BlockSpec(shape, lambda h, i: (0, 0))

    return pl.pallas_call(
        attend_back_kernel,
        grid=(heads, length // block),
        in_specs=[
            tile,
            fixed(length, head),
            fixed(head, length),
            fixed(length, head),
            tile,
            pl.BlockSpec((1, 1, block), lambda h, i: (h, 0, i)),
            pl.BlockSpec((1, block), lambda h, i: (0, i)),
            fixed(length, 1),
            tile,
            fixed(length, head),
            fixed(length, head),
            fixed(length, head),
            fixed(1, head),
            fixed(1, head),
        ],
        out_specs=[tile, fixed(length, head), fixed(length, head), fixed(8, head)],
        out_shape=[
            jax.ShapeDtypeStruct((length, cols), BF16),
            jax.ShapeDtypeStruct((length, head), BF16),
            jax.ShapeDtypeStruct((length, head), BF16),
            jax.ShapeDtypeStruct((8, head), F32),
        ],
        scratch_shapes=[pltpu.VMEM((length, head), F32), pltpu.VMEM((length, head), F32)],
        compiler_params=pltpu.CompilerParams(vmem_limit_bytes=VMEM_BYTES),
        cost_estimate=FREE,
    )(
        query,
        key,
        key.T,
        value,
        grad,
        logs,
        segment[None],
        segment[:, None],
        qpre,
        kpre,
        cos,
        sin,
        gq[None],
        gk[None],
    )


def on_device(
    tokens,
    segment_ids,
    routes,
    w_query,
    w_key,
    w_value,
    w_output,
    w_router,
    gain_attn,
    gain_moe,
    gain_query,
    gain_key,
    w_gate,
    w_up,
    w_down,
    cotangent,
):
    bands, peers = lax.axis_size("dp"), lax.axis_size("expert")
    band, peer = lax.axis_index("dp"), lax.axis_index("expert")
    own_tokens = tokens[0]
    tok_count, width = own_tokens.shape
    band_rows = w_query.shape[0]
    experts = w_router.shape[1]
    gain_rows = gain_query.shape[0]
    head_size = gain_rows * bands * peers
    heads = w_query.shape[1] // head_size // bands
    q_cols, k_cols = heads * head_size, head_size
    qkv_cols = q_cols + 2 * k_cols
    owned = experts // peers

    small = jnp.concatenate(
        [
            w_router,
            gain_attn[:, None],
            gain_moe[:, None],
            jnp.pad(gain_query, (0, band_rows - gain_rows))[:, None],
            jnp.pad(gain_key, (0, band_rows - gain_rows))[:, None],
        ],
        axis=1,
    )
    shared = owned >= bands == 4
    top = routes.shape[-1]
    ride = tok_count * top // band_rows
    if shared:
        small = jnp.concatenate([small, routes[0].reshape(band_rows, ride).astype(BF16)], axis=1)
    small = jnp.pad(small, ((0, 0), (0, 128 - small.shape[1])))
    packed = jnp.concatenate(
        [
            w_query.reshape(band_rows, bands, q_cols),
            w_key.reshape(band_rows, bands, k_cols),
            w_value.reshape(band_rows, bands, k_cols),
            jnp.broadcast_to(small[:, None], (band_rows, bands, 128)),
        ],
        axis=-1,
    ).transpose(1, 0, 2)
    tokens_all, packed_all, out_w = start_moves(own_tokens, packed, w_output)
    qkv_w = packed_all[:, :qkv_cols]
    small_all = packed_all[:, qkv_cols:]
    router_full = small_all[:, :experts]
    attn_gain = small_all[:, experts].astype(F32)
    moe_gain = small_all[:, experts + 1].astype(F32)
    head_gains = small_all.reshape(bands * peers, band_rows, 128)[:, :gain_rows]
    query_gain = head_gains[:, :, experts + 2].reshape(-1).astype(F32)
    key_gain = head_gains[:, :, experts + 3].reshape(-1).astype(F32)

    def beside(rows, *sides):
        used = sum(side.shape[-1] for side in sides)
        filler = jnp.zeros((tok_count, SIDE - used), BF16)
        return jnp.concatenate([rows, *(side.astype(BF16) for side in sides), filler], axis=1)

    def side_gates(sides):
        gates = sides[..., :experts].astype(F32)
        gates = gates + sides[..., experts : 2 * experts].astype(F32)
        return lax.dynamic_slice_in_dim(gates, peer * owned, owned, axis=2)

    cot_rows = beside(cotangent[0], routes[0])
    if shared:
        cot_all = lax.all_gather(cot_rows, ("dp", "expert"), axis=0, tiled=False)
        cot_all = cot_all.reshape(bands, peers, tok_count, -1)
    else:
        cot_all = lax.all_gather(cot_rows, "expert", axis=0)[None]
    here = band if shared else 0

    inputs = own_tokens.astype(F32)
    length = tokens_all.shape[0]
    half = head_size // 2
    frequency = ROPE_BASE ** (-jnp.arange(half, dtype=F32) * 2.0 / head_size)
    angles = jnp.arange(length, dtype=jnp.int32).astype(F32)[:, None] * frequency[None, :]
    cos = jnp.concatenate([jnp.cos(angles)] * 2, axis=-1)
    sin = jnp.concatenate([-jnp.sin(angles), jnp.sin(angles)], axis=-1)
    normed, query_pre, key_pre, query_low, key_low, value_low = make_qkv(
        tokens_all, attn_gain, packed_all, cos, sin, query_gain, key_gain
    )
    segment = segment_ids[0]
    attended_low, log_total = attend(query_low, key_low, value_low, segment)
    branch = dot("tm,md->td", attended_low, out_w).astype(BF16)
    branch = sum_blocks(branch.reshape(bands, tok_count, width), "dp")
    hidden = inputs + branch

    normed_moe_f, moe_pull = jax.vjp(norm_rows, hidden, moe_gain)
    normed_moe = normed_moe_f.astype(BF16)
    mask = jnp.any(routes[0][..., None] == jnp.arange(experts, dtype=jnp.int32), axis=1)
    own_gates = masked_softmax(dot("td,de->te", normed_moe, router_full), mask)
    high = own_gates.astype(BF16)
    low = own_gates - high.astype(F32)
    moe_rows = beside(normed_moe, high, low)

    def in_order(columns):
        pick = [
            lax.dynamic_index_in_dim(columns, here ^ i, 0, keepdims=False)
            for i in range(len(columns))
        ]
        return jnp.concatenate(pick)

    if shared:
        sides = small_all.reshape(bands, peers, band_rows, 128)
        routes_all = sides[..., experts + 4 : experts + 4 + ride]
        routes_all = in_order(routes_all.reshape(bands, peers, tok_count, top))
        ranks_all = block_ranks(routes_all.astype(jnp.int32), peer, owned, experts)
        moe_rows = after(moe_rows, ranks_all)
    moe_all = gather_square(moe_rows) if shared else gather_rows(moe_rows)[None]
    cot_all = after(cot_all, moe_all)
    if not shared:
        routes_all = cot_all[0, ..., width : width + top].astype(jnp.int32)
        ranks_all = block_ranks(routes_all, peer, owned, experts)
    own_ranks = ranks_all[:peers]
    token_ranks = own_ranks.transpose(0, 2, 1)
    cot_placed = place_rows(ranks_all, cot_all, here).reshape(owned, -1, width)
    x_placed = place_rows(ranks_all, moe_all, here).reshape(owned, -1, width)
    all_gates = slot_values(ranks_all, side_gates(in_order(moe_all[..., width:])))
    all_gates = all_gates.transpose(1, 0, 2).reshape(owned, -1, 1)
    *own, slot_grads, rows_back, rows_out = own_experts(
        x_placed,
        cot_placed,
        all_gates,
        peers * CAP,
        w_gate,
        w_up,
        w_down,
    )
    if not shared:
        active, gate_low, up_low = own
        expert_sums = lax.psum(
            (
                dot("erd,erf->edf", x_placed, gate_low).astype(BF16),
                dot("erd,erf->edf", x_placed, up_low).astype(BF16),
                dot("erf,erd->efd", active, cot_placed).astype(BF16),
            ),
            "dp",
        )
    rows_back = combine(token_ranks, rows_back)
    back = lax.psum_scatter(rows_back, "expert", scatter_dimension=0, tiled=True)[0]
    slot_grads = slot_grads.reshape(owned, peers, CAP).transpose(1, 0, 2)
    slots = jnp.arange(CAP, dtype=jnp.int32)[None, None, :, None]
    token_grads = jnp.where(own_ranks[:, :, None, :] == slots, slot_grads[..., None], 0.0)
    token_grads = jnp.sum(token_grads, axis=2)
    gate_grads = (
        lax.all_to_all(token_grads, "expert", split_axis=0, concat_axis=0, tiled=True)
        .reshape(experts, tok_count)
        .T
    )
    rows_out = combine(after(token_ranks, rows_back), rows_out)

    expert_sums = None if shared else expert_sums

    def next_expert(number, sums, *earlier):
        if not shared or number >= owned:
            return sums, earlier[0]
        *sums, mark = expert_grads(
            x_placed,
            cot_placed,
            after(all_gates, *earlier),
            own,
            w_gate,
            w_up,
            w_down,
            number,
            sums,
        )
        return sums, mark

    expert_sums, mark = next_expert(0, expert_sums, rows_out)
    back = after(back, mark)

    grad_logits = own_gates * (
        gate_grads - jnp.sum(own_gates * gate_grads, axis=-1, keepdims=True)
    )
    grad_router_w = jnp.einsum("td,te->de", normed_moe.astype(F32), grad_logits, precision=PRECISE)
    grad_normed = back.astype(F32) + jnp.einsum(
        "te,de->td", grad_logits, router_full.astype(F32), precision=PRECISE
    )
    grad_hidden_n, grad_moe_gain = moe_pull(grad_normed)
    grad_hidden = cotangent[0].astype(F32) + grad_hidden_n
    grad_branch = grad_hidden.astype(BF16)
    branch_all = lax.all_gather(grad_branch, "dp", axis=0, tiled=True)
    expert_sums, mark = next_expert(1, expert_sums, grad_branch)
    branch_all = after(branch_all, mark)

    grad_output = dot("tm,td->md", attended_low, branch_all).astype(BF16)
    grad_attended = dot("td,md->tm", branch_all, out_w).astype(BF16)
    grad_attended = after(grad_attended, grad_output)
    grad_output = lax.psum_scatter(grad_output, "expert", scatter_dimension=0, tiled=True)
    rows_out = sum_cores(after(rows_out, branch_all))
    query_grad, key_grad, value_grad, head_grads = attend_back(
        query_low,
        key_low,
        value_low,
        grad_attended,
        log_total,
        segment,
        query_pre,
        key_pre,
        cos,
        sin,
        query_gain,
        key_gain,
    )
    qkv_grad = jnp.concatenate([query_grad, key_grad, value_grad], axis=1)
    grad_normed_attn = dot("tm,dm->td", qkv_grad, qkv_w).astype(BF16)
    expert_sums, mark = next_expert(2, expert_sums, grad_normed_attn, rows_out)
    moe_sum = sum_chips(rows_out)
    block_out = (hidden + moe_sum).astype(BF16)
    grad_normed_attn = lax.psum_scatter(
        grad_normed_attn, "dp", scatter_dimension=0, tiled=True
    )
    grad_normed_attn = after(grad_normed_attn, mark).astype(F32)
    _, attn_pull = jax.vjp(norm_rows, inputs, attn_gain)
    grad_inputs_n, grad_attn_gain = attn_pull(grad_normed_attn)
    grad_tokens = grad_hidden + grad_inputs_n

    whole_gains = jnp.stack([grad_attn_gain, grad_moe_gain], axis=1)
    head_gains = head_grads[:2].T
    head_gains = jnp.pad(
        head_gains.reshape(bands * peers, gain_rows, 2),
        ((0, 0), (0, band_rows - gain_rows), (0, 0)),
    )
    small_grad = jnp.concatenate(
        [grad_router_w, whole_gains, head_gains.reshape(width, 2)], axis=1
    )
    small_grad = jnp.pad(small_grad, ((0, 0), (0, 128 - small_grad.shape[1])))
    band_qkv = jnp.concatenate([dot("td,tm->dm", normed, qkv_grad), small_grad], axis=1)
    band_qkv = band_qkv.astype(BF16).reshape(bands, peers, band_rows, -1).transpose(1, 0, 2, 3)
    for number in range(3, owned):
        expert_sums, mark = next_expert(number, expert_sums, band_qkv)
    band_qkv = lax.psum_scatter(
        band_qkv.reshape(width, -1), "expert", scatter_dimension=0, tiled=True
    ).reshape(bands, band_rows, -1)
    band_qkv = after(band_qkv, mark)
    band_qkv = lax.all_to_all(band_qkv, "dp", split_axis=0, concat_axis=0, tiled=True).transpose(
        1, 0, 2
    )
    grad_query = band_qkv[:, :, :q_cols].astype(F32).reshape(band_rows, -1)
    grad_key = band_qkv[:, :, q_cols : q_cols + k_cols].astype(F32).reshape(band_rows, -1)
    grad_value = band_qkv[:, :, q_cols + k_cols : qkv_cols].astype(F32).reshape(band_rows, -1)
    smaller = jnp.sum(band_qkv[:, :, qkv_cols:].astype(F32), axis=1)
    return (
        block_out[None],
        grad_tokens[None],
        grad_query,
        grad_key,
        grad_value,
        grad_output.astype(F32),
        smaller[:, :experts],
        smaller[:, experts],
        smaller[:, experts + 1],
        smaller[:gain_rows, experts + 2],
        smaller[:gain_rows, experts + 3],
        expert_sums[0].astype(F32),
        expert_sums[1].astype(F32),
        expert_sums[2].astype(F32),
    )


def solution(mesh):
    both = ("dp", "expert")
    return jax.shard_map(
        on_device,
        mesh=mesh,
        in_specs=(
            P("expert", "dp", None),
            P("expert", None),
            P("expert", "dp", None),
            P(both, None),
            P(both, None),
            P(both, None),
            P(both, None),
            P(both, None),
            P(both),
            P(both),
            P(both),
            P(both),
            P("expert", None, None),
            P("expert", None, None),
            P("expert", None, None),
            P("expert", "dp", None),
        ),
        out_specs=(
            P("expert", "dp", None),
            P("expert", "dp", None),
            P(both, None),
            P(both, None),
            P(both, None),
            P(both, None),
            P(both, None),
            P(both),
            P(both),
            P(both),
            P(both),
            P("expert", None, None),
            P("expert", None, None),
            P("expert", None, None),
        ),
        check_vma=False,
    )
```

```python
import jax
import jax.numpy as jnp
from jax import lax
from jax.experimental import pallas as pl
from jax.experimental.pallas import tpu as pltpu
from jax.sharding import PartitionSpec as P

CAP = 80
Q_BLOCK = 256
HIDDEN_TILE = 256
OWN_ROWS = 8 * CAP
WIDTH_TILE = 512
SIDE = 128
ROW_PARTS = 2
VMEM_BYTES = 60 << 20


EPSILON = 1e-06
ROPE_BASE = 1000000.0
PRECISE = lax.Precision.HIGHEST
F32 = jnp.float32
BF16 = jnp.bfloat16
FREE = pl.CostEstimate(flops=0, bytes_accessed=0, transcendentals=0)


def norm_rows(values, gain_row):
    return (
        values * lax.rsqrt(jnp.mean(values * values, axis=-1, keepdims=True) + EPSILON) * gain_row
    )


def masked_softmax(logits, mask):
    kept = jnp.where(mask, logits, -jnp.inf)
    largest = jnp.max(kept, axis=-1, keepdims=True)
    raised = jnp.where(mask, jnp.exp(logits - largest), 0.0)
    return raised / jnp.sum(raised, axis=-1, keepdims=True)


def nothing(*refs):
    del refs


def after(value, *others):
    anywhere = pl.BlockSpec(memory_space=pl.ANY)
    return pl.pallas_call(
        nothing,
        out_shape=jax.ShapeDtypeStruct(value.shape, value.dtype),
        in_specs=[anywhere] * (1 + len(others)),
        out_specs=anywhere,
        input_output_aliases={0: 0},
    )(value, *others)


def traded(value, axis, step):
    return lax.ppermute(value, axis, [(i, i ^ step) for i in range(lax.axis_size(axis))])


def sum_blocks(blocks, axis):
    count, me = lax.axis_size(axis), lax.axis_index(axis)
    total = lax.dynamic_index_in_dim(blocks, me, 0, keepdims=False).astype(F32)
    for step in range(1, count):
        sent = lax.dynamic_index_in_dim(blocks, me ^ step, 0, keepdims=False)
        total = total + traded(sent, axis, step).astype(F32)
    return total


def dot(spec, left, right):
    return jnp.einsum(spec, left, right, preferred_element_type=F32)


def line_sems(chips):
    return [pltpu.SemaphoreType.DMA((chips,))] * 6 + [pltpu.SemaphoreType.DMA]


def send_to(source, target, send_sem, recv_sem, device):
    return pltpu.make_async_remote_copy(
        src_ref=source,
        dst_ref=target,
        send_sem=send_sem,
        recv_sem=recv_sem,
        device_id=device,
        device_id_type=pl.DeviceIdType.MESH,
    )


def greet(devices, conditions):
    barrier = pltpu.get_barrier_semaphore()
    for device, condition in zip(devices, conditions):

        @pl.when(condition)
        def _(device=device):
            pl.semaphore_signal(
                barrier, inc=1, device_id=device, device_id_type=pl.DeviceIdType.MESH
            )

    pl.semaphore_wait(barrier, sum(condition.astype(jnp.int32) for condition in conditions))


def expert_place():
    me = lax.axis_index("expert")
    return me, lax.div(me, 2), lax.rem(me, 2), lax.axis_size("expert") // 2


def line_partners():
    me, chip, core, chips = expert_place()
    band = lax.axis_index("dp")
    devices = [(band, me + 1 - 2 * core), (band, me + 2), (band, me - 2)]
    return devices, [chip >= 0, chip < chips - 1, chip > 0]


class Line:
    def __init__(self, own, slot, sems):
        self.own, self.slot = own, slot
        self.up_out, self.up_in, self.down_out, self.down_in, self.side_out, self.side_in, self.self_sem = sems
        self.me, self.chip, self.core, self.chips = expert_place()
        (self.twin, self.up, self.down), _ = line_partners()

    def local(self):
        return pltpu.make_async_copy(self.own, self.slot(self.me), self.self_sem)

    def side(self, source, block):
        return send_to(
            source,
            self.slot(2 * block + self.core),
            self.side_out.at[block],
            self.side_in.at[block],
            self.twin,
        )

    def upward(self, source, block, step):
        return send_to(
            source,
            self.slot(2 * block + self.core),
            self.up_out.at[step],
            self.up_in.at[step],
            self.up,
        )

    def downward(self, source, block, step):
        return send_to(
            source,
            self.slot(2 * block + self.core),
            self.down_out.at[step],
            self.down_in.at[step],
            self.down,
        )

    def begin(self):
        self.local().start()

        @pl.when(self.chip < self.chips - 1)
        def _():
            self.upward(self.own, self.chip, 0).start()

        @pl.when(self.chip > 0)
        def _():
            self.downward(self.own, self.chip, 0).start()

        self.side(self.own, self.chip).start()

    def advance(self, step):
        below, above = self.chip - 1 - step, self.chip + 1 + step

        @pl.when(below >= 0)
        def _():
            held = self.slot(2 * below + self.core)
            self.upward(held, below, step).wait_recv()

            if step + 1 < self.chips - 1:

                @pl.when(self.chip < self.chips - 1)
                def _():
                    self.upward(held, below, step + 1).start()

            self.side(held, below).start()

        @pl.when(above < self.chips)
        def _():
            held = self.slot(2 * above + self.core)
            self.downward(held, above, step).wait_recv()

            if step + 1 < self.chips - 1:

                @pl.when(self.chip > 0)
                def _():
                    self.downward(held, above, step + 1).start()

            self.side(held, above).start()

    def finish(self):
        self.local().wait()
        for step in range(self.chips - 1):

            @pl.when((self.chip < self.chips - 1) & (self.chip >= step))
            def _(step=step):
                block = self.chip - step
                self.upward(self.slot(2 * block + self.core), block, step).wait_send()

            @pl.when((self.chip > 0) & (self.chip + step < self.chips))
            def _(step=step):
                block = self.chip + step
                self.downward(self.slot(2 * block + self.core), block, step).wait_send()

        for block in range(self.chips):
            self.side(self.slot(2 * block + self.core), block).wait_send()
            send_to(
                self.slot(2 * block + self.core),
                self.slot(2 * block + 1 - self.core),
                self.side_out.at[block],
                self.side_in.at[block],
                self.twin,
            ).wait_recv()


def rows_kernel(own_ref, all_ref, *sems):
    greet(*line_partners())
    line = Line(own_ref, lambda i: all_ref.at[i], sems)
    line.begin()
    for step in range(line.chips - 1):
        line.advance(step)
    line.finish()


def gather_rows(own):
    peers = lax.axis_size("expert")
    anywhere = pl.BlockSpec(memory_space=pl.ANY)
    return pl.pallas_call(
        rows_kernel,
        out_shape=jax.ShapeDtypeStruct((peers, *own.shape), own.dtype),
        in_specs=[anywhere],
        out_specs=anywhere,
        scratch_shapes=line_sems(peers // 2),
        compiler_params=pltpu.CompilerParams(collective_id=1, has_side_effects=True),
    )(own)


def square_kernel(own_ref, all_ref, *sems):
    band, me = lax.axis_index("dp"), lax.axis_index("expert")
    outs, arrivals, twin_out, twin_in = sems[:3], sems[3:6], sems[6], sems[7]
    columns = [(band ^ 1, me), (band ^ 2, me)]
    devices, conditions = line_partners()
    greet(devices + columns, conditions + [band >= 0] * 2)
    line = Line(own_ref, lambda i: all_ref.at[band, i], sems[8:])
    chip, chips, core = line.chip, line.chips, line.core

    def across(source, block, step):
        return send_to(
            source,
            all_ref.at[band, 2 * block + core],
            outs[step - 1].at[block],
            arrivals[step - 1].at[block],
            (band ^ step, me),
        )

    def held(block, step):
        return all_ref.at[band ^ step, 2 * block + core]

    def arrive(block, step):
        send_to(
            own_ref,
            held(block, step),
            outs[step - 1].at[block],
            arrivals[step - 1].at[block],
            (band ^ step, me),
        ).wait_recv()

    def onward(block, step):
        return send_to(
            held(block, step),
            held(block, step),
            outs[2].at[block],
            arrivals[2].at[block],
            (band ^ (3 - step), me),
        )

    def twin(block, step):
        place = (step - 1) * chips + block
        return send_to(
            held(block, step),
            held(block, step),
            twin_out.at[place],
            twin_in.at[place],
            line.twin,
        )

    def spread(source, block):
        across(source, block, 1).start()
        across(source, block, 2).start()

    def receive(block):
        for step in (1, 2):
            arrive(block, step)

            @pl.when(lax.rem(block, 2) == step - 1)
            def _(step=step):
                onward(block, step).start()

            twin(block, step).start()

    line.begin()
    spread(own_ref, chip)
    for step in range(chips - 1):
        line.advance(step)
        below, above = chip - 1 - step, chip + 1 + step

        @pl.when(below >= 0)
        def _(below=below):
            spread(line.slot(2 * below + core), below)

        @pl.when(above < chips)
        def _(above=above):
            spread(line.slot(2 * above + core), above)

    receive(chip)
    for step in range(chips - 1):
        below, above = chip - 1 - step, chip + 1 + step

        @pl.when(below >= 0)
        def _(below=below):
            receive(below)

        @pl.when(above < chips)
        def _(above=above):
            receive(above)

    for block in range(chips):
        arrive(block, 3)
        twin(block, 3).start()
    line.finish()
    for block in range(chips):
        across(own_ref, block, 1).wait_send()
        across(own_ref, block, 2).wait_send()
        onward(block, 1).wait_send()
        for step in (1, 2, 3):
            place = (step - 1) * chips + block
            twin(block, step).wait_send()
            there = all_ref.at[band ^ step, 2 * block + 1 - core]
            send_to(there, there, twin_out.at[place], twin_in.at[place], line.twin).wait_recv()


def gather_square(own):
    bands, peers = lax.axis_size("dp"), lax.axis_size("expert")
    chips = peers // 2
    anywhere = pl.BlockSpec(memory_space=pl.ANY)
    return pl.pallas_call(
        square_kernel,
        out_shape=jax.ShapeDtypeStruct((bands, peers, *own.shape), own.dtype),
        in_specs=[anywhere],
        out_specs=anywhere,
        scratch_shapes=[pltpu.SemaphoreType.DMA((chips,))] * 6
        + [pltpu.SemaphoreType.DMA((3 * chips,))] * 2
        + line_sems(chips),
        compiler_params=pltpu.CompilerParams(collective_id=2, has_side_effects=True),
    )(own)


def start_kernel(
    tok_ref, pack_ref, wo_ref, tokens_ref, swap_ref, pack_all_ref, wo_all_ref, *sems
):
    bands, band = lax.axis_size("dp"), lax.axis_index("dp")
    me = lax.axis_index("expert")
    tok_out, tok_in, swap_out, swap_in, self_sems = sems[:5]
    pack_sems, wo_sems = sems[5:12], sems[12:]
    columns = [(band ^ step, me) for step in range(1, bands)]
    devices, conditions = line_partners()
    greet(devices + columns, conditions + [band >= 0] * (bands - 1))
    own_tok = pltpu.make_async_copy(tok_ref, tokens_ref.at[band], self_sems.at[0])
    own_swap = pltpu.make_async_copy(pack_ref.at[band], swap_ref.at[band], self_sems.at[1])
    own_swap.start()
    own_tok.start()

    def swap(step):
        other = band ^ step
        return send_to(
            pack_ref.at[other],
            swap_ref.at[band],
            swap_out.at[step - 1],
            swap_in.at[step - 1],
            (other, me),
        )

    def token(step):
        other = band ^ step
        return send_to(
            tok_ref, tokens_ref.at[band], tok_out.at[step - 1], tok_in.at[step - 1], (other, me)
        )

    def arrived(step, source, target, out, arrival):
        other = band ^ step
        send_to(
            source, target.at[other], out.at[step - 1], arrival.at[step - 1], (other, me)
        ).wait_recv()

    for step in range(1, bands):
        swap(step).start()
    wo_line = Line(wo_ref, lambda i: wo_all_ref.at[i], wo_sems)
    wo_line.begin()
    for step in range(1, bands):
        token(step).start()
    own_swap.wait()
    for step in range(1, bands):
        arrived(step, pack_ref.at[band], swap_ref, swap_out, swap_in)
    pack_line = Line(swap_ref, lambda i: pack_all_ref.at[:, i], pack_sems)
    pack_line.begin()
    for step in range(pack_line.chips - 1):
        wo_line.advance(step)
        pack_line.advance(step)
    wo_line.finish()
    pack_line.finish()
    own_tok.wait()
    for step in range(1, bands):
        arrived(step, tok_ref, tokens_ref, tok_out, tok_in)
        token(step).wait_send()
        swap(step).wait_send()


def start_moves(tokens, packed, w_output):
    bands, peers = lax.axis_size("dp"), lax.axis_size("expert")
    anywhere = pl.BlockSpec(memory_space=pl.ANY)
    chips = peers // 2
    shapes = [
        (bands, *tokens.shape),
        packed.shape,
        (bands, peers, *packed.shape[1:]),
        (peers, *w_output.shape),
    ]
    tokens_all, _, packed_all, output_all = pl.pallas_call(
        start_kernel,
        out_shape=[jax.ShapeDtypeStruct(shape, BF16) for shape in shapes],
        in_specs=[anywhere] * 3,
        out_specs=[anywhere] * 4,
        scratch_shapes=[pltpu.SemaphoreType.DMA((bands - 1,))] * 4
        + [pltpu.SemaphoreType.DMA((2,))]
        + line_sems(chips) * 2,
        compiler_params=pltpu.CompilerParams(collective_id=0, has_side_effects=True),
    )(tokens, packed, w_output)
    width = tokens.shape[1]
    return (
        tokens_all.reshape(-1, width),
        packed_all.reshape(-1, packed.shape[-1]),
        output_all.reshape(-1, width),
    )


def block_ranks(routes, peer, owned, experts):
    chosen = jnp.any(routes[..., None] == jnp.arange(experts, dtype=jnp.int32), axis=2)
    chosen = lax.dynamic_slice_in_dim(chosen, peer * owned, owned, axis=2)
    tok_count = chosen.shape[1]
    earlier = jnp.tril(jnp.ones((tok_count, tok_count), BF16), -1)
    ranks = dot("ts,bse->bet", earlier, chosen.astype(BF16)).astype(jnp.int32)
    return jnp.where(chosen.transpose(0, 2, 1), ranks, -1)


def slot_values(ranks, values):
    slots = jnp.arange(CAP, dtype=jnp.int32)
    chosen = ranks[:, :, None, :] == slots[None, None, :, None]
    return jnp.sum(jnp.where(chosen, values.transpose(0, 2, 1)[:, :, None, :], 0.0), axis=-1)


def place_kernel(_, rank_ref, block_ref, rows_ref):
    count, owned, tok_count = rank_ref.shape
    slots = lax.broadcasted_iota(jnp.int32, (CAP, tok_count), 0)
    width = block_ref.shape[-1]
    for block in range(count):
        ranks = rank_ref[block]
        hot = jnp.concatenate([ranks[e : e + 1] == slots for e in range(owned)], axis=0)
        hot = jnp.where(hot, 1.0, 0.0).astype(BF16)
        for start in range(0, width, WIDTH_TILE):
            cols = slice(start, start + WIDTH_TILE)
            rows = jnp.dot(hot, block_ref[0, block, :, cols], preferred_element_type=F32)
            rows_ref[:, block, :, cols] = rows.astype(BF16).reshape(owned, CAP, WIDTH_TILE)


def place_rows(ranks, columns, first):
    total, owned, tok_count = ranks.shape
    peers = columns.shape[1]
    width = columns.shape[-1] - SIDE
    several = 2
    steps = peers // several

    def block_at(b, at):
        return lax.bitwise_xor(at[0], lax.div(b, steps)), lax.rem(b, steps), 0, 0

    return pl.pallas_call(
        place_kernel,
        grid_spec=pltpu.PrefetchScalarGridSpec(
            num_scalar_prefetch=1,
            grid=(total // several,),
            in_specs=[
                pl.BlockSpec((several, owned, tok_count), lambda b, at: (b, 0, 0)),
                pl.BlockSpec((1, several, tok_count, width), block_at),
            ],
            out_specs=pl.BlockSpec((owned, several, CAP, width), lambda b, at: (0, b, 0, 0)),
        ),
        out_shape=jax.ShapeDtypeStruct((owned, total, CAP, width), BF16),
        compiler_params=pltpu.CompilerParams(vmem_limit_bytes=VMEM_BYTES),
        cost_estimate=FREE,
    )(jnp.asarray(first, jnp.int32).reshape(1), ranks, columns)


def combine_kernel(rank_ref, rows_ref, out_ref):
    tok_count, owned = rank_ref.shape[1:]
    slots = owned * CAP
    width = out_ref.shape[-1]
    lane = lax.broadcasted_iota(jnp.int32, (tok_count, slots), 1)
    hot = jnp.zeros((tok_count, slots), F32)
    for e in range(owned):
        ranks = rank_ref[0, :, e : e + 1]
        hot = jnp.where((ranks >= 0) & (lane == ranks + e * CAP), 1.0, hot)
    hot = hot.astype(BF16)
    for start in range(0, width, WIDTH_TILE):
        cols = slice(start, start + WIDTH_TILE)
        rows = rows_ref[:, 0, :, cols].reshape(slots, WIDTH_TILE)
        out_ref[0, :, cols] = jnp.dot(hot, rows, preferred_element_type=F32).astype(BF16)


def combine(ranks, rows):
    count, tok_count, owned = ranks.shape
    width = rows.shape[-1]
    return pl.pallas_call(
        combine_kernel,
        grid=(count,),
        out_shape=jax.ShapeDtypeStruct((count, tok_count, width), BF16),
        in_specs=[
            pl.BlockSpec((1, tok_count, owned), lambda b: (b, 0, 0)),
            pl.BlockSpec((owned, 1, CAP, width), lambda b: (0, b, 0, 0)),
        ],
        out_specs=pl.BlockSpec((1, tok_count, width), lambda b: (b, 0, 0)),
        compiler_params=pltpu.CompilerParams(vmem_limit_bytes=VMEM_BYTES),
        cost_estimate=FREE,
    )(ranks, rows.reshape(owned, count, CAP, width))


def dot_nt(left, right):
    return lax.dot_general(left, right, (((1,), (1,)), ((), ())), preferred_element_type=F32)


def hidden_grads(x, c, gates, wg_ref, wu_ref, wd_ref):
    gate_in = jnp.dot(x, wg_ref[0], preferred_element_type=F32)
    up_in = jnp.dot(x, wu_ref[0], preferred_element_type=F32)
    raw = dot_nt(c, wd_ref[0])
    sig = 1.0 / (1.0 + jnp.exp(-gate_in))
    silu = gate_in * sig
    active = silu * up_in
    grad = raw * gates
    gate_grad = grad * up_in * (sig + silu * (1.0 - sig))
    up_grad = grad * silu
    return (active * gates).astype(BF16), gate_grad.astype(BF16), up_grad.astype(BF16), active * raw


def own_kernel(
    x_ref,
    c_ref,
    g_ref,
    wg_ref,
    wu_ref,
    wd_ref,
    active_ref,
    gate_ref,
    up_ref,
    slot_ref,
    back_ref,
    out_ref,
    back_sum,
    out_sum,
):
    width = x_ref.shape[-1]
    step = pl.program_id(2)
    active, gate_grad, up_grad, slot = hidden_grads(
        x_ref[0], c_ref[0], g_ref[0], wg_ref, wu_ref, wd_ref
    )
    active_ref[0] = active
    gate_ref[0] = gate_grad
    up_ref[0] = up_grad
    slot = jnp.sum(slot, axis=1, keepdims=True)
    slot_ref[0] = jnp.where(step == 0, slot, slot_ref[0] + slot)
    for start in range(0, width, WIDTH_TILE):
        cols = slice(start, start + WIDTH_TILE)
        rows = dot_nt(gate_ref[0], wg_ref[0, cols, :]) + dot_nt(up_ref[0], wu_ref[0, cols, :])
        back_sum[:, cols] = jnp.where(step == 0, rows, back_sum[:, cols] + rows)
        rows = jnp.dot(active_ref[0], wd_ref[0, :, cols], preferred_element_type=F32)
        out_sum[:, cols] = jnp.where(step == 0, rows, out_sum[:, cols] + rows)

    @pl.when(step == pl.num_programs(2) - 1)
    def _():
        back_ref[0] = back_sum[...].astype(BF16)
        out_ref[0] = out_sum[...].astype(BF16)


def own_experts(x_rows, c_rows, gates, rows, w_gate, w_up, w_down):
    owned, _, width = x_rows.shape
    hidden = w_down.shape[1]
    tile = HIDDEN_TILE
    some = min(rows, OWN_ROWS)
    whole = pl.BlockSpec((1, some, width), lambda e, r, f: (e, r, 0))
    column = pl.BlockSpec((1, some, 1), lambda e, r, f: (e, r, 0))
    part = pl.BlockSpec((1, some, tile), lambda e, r, f: (e, r, f))
    inward = pl.BlockSpec((1, width, tile), lambda e, r, f: (e, 0, f))
    outward = pl.BlockSpec((1, tile, width), lambda e, r, f: (e, f, 0))
    return pl.pallas_call(
        own_kernel,
        grid=(owned, rows // some, hidden // tile),
        in_specs=[whole, whole, column, inward, inward, outward],
        out_specs=[part, part, part, column, whole, whole],
        out_shape=[jax.ShapeDtypeStruct((owned, rows, hidden), BF16)] * 3
        + [jax.ShapeDtypeStruct((owned, rows, 1), F32)]
        + [jax.ShapeDtypeStruct((owned, rows, width), BF16)] * 2,
        scratch_shapes=[pltpu.VMEM((some, width), F32)] * 2,
        compiler_params=pltpu.CompilerParams(vmem_limit_bytes=VMEM_BYTES),
        cost_estimate=pl.CostEstimate(
            flops=12 * owned * rows * width * hidden,
            bytes_accessed=owned * (8 * rows * width + 6 * width * hidden),
            transcendentals=owned * rows * hidden,
        ),
    )(x_rows, c_rows, gates, w_gate, w_up, w_down)


def grads_kernel(
    x_ref, c_ref, g_ref, active_ref, gate_ref, up_ref, wg_ref, wu_ref, wd_ref, *rest
):
    dg_ref, du_ref, dd_ref, mark_ref, sums, pair, actives = rest[-7:]
    mark_ref[...] = jnp.zeros_like(mark_ref)
    tile = HIDDEN_TILE
    rows, width = x_ref.shape[1:]
    own = active_ref.shape[1]
    step = pl.program_id(1)

    def keep(start, active, gate_grad, up_grad):
        part = slice(start, start + own)
        actives[:, part] = active.T
        pair[:tile, part] = gate_grad.T
        pair[tile:, part] = up_grad.T

    def work_out(start):
        part = slice(start, start + own)
        active, gate_grad, up_grad, _ = hidden_grads(
            x_ref[0, part], c_ref[0, part], g_ref[0, part], wg_ref, wu_ref, wd_ref
        )
        keep(start, active, gate_grad, up_grad)

    @pl.when(step == 0)
    def _():
        keep(0, active_ref[0], gate_ref[0], up_ref[0])

    @pl.when(step > 0)
    def _():
        work_out(0)

    for start in range(own, rows, own):
        work_out(start)

    @pl.loop(0, width // WIDTH_TILE)
    def _(c):
        cols = pl.ds(pl.multiple_of(c * WIDTH_TILE, WIDTH_TILE), WIDTH_TILE)
        grads = jnp.dot(pair[...], x_ref[0, :, cols], preferred_element_type=F32)
        sums[:, cols] = jnp.where(step == 0, grads, sums[:, cols] + grads)
        grads = jnp.dot(actives[...], c_ref[0, :, cols], preferred_element_type=F32)
        dd_ref[0, :, cols] = jnp.where(step == 0, grads, dd_ref[0, :, cols] + grads)

    @pl.when(step == pl.num_programs(1) - 1)
    def _():
        same = lax.broadcasted_iota(jnp.int32, (tile, tile), 0) == lax.broadcasted_iota(
            jnp.int32, (tile, tile), 1
        )
        same = jnp.where(same, 1.0, 0.0).astype(BF16)

        @pl.loop(0, width // tile)
        def _(c):
            cols = pl.ds(pl.multiple_of(c * tile, tile), tile)
            dg_ref[0, cols, :] = dot_nt(same, sums[:tile, cols].astype(BF16))
            du_ref[0, cols, :] = dot_nt(same, sums[tile:, cols].astype(BF16))


def expert_grads(x_rows, c_rows, gates, own, w_gate, w_up, w_down, expert, buffers=None):
    owned, rows, width = x_rows.shape
    hidden = w_down.shape[1]
    tile, parts = HIDDEN_TILE, ROW_PARTS
    part, own_rows = rows // parts, own[0].shape[1]
    shapes = [(owned, width, hidden)] * 2 + [(owned, hidden, width)]
    in_specs = [
        pl.BlockSpec((1, part, width), lambda f, r: (expert, r, 0)),
        pl.BlockSpec((1, part, width), lambda f, r: (expert, r, 0)),
        pl.BlockSpec((1, part, 1), lambda f, r: (expert, r, 0)),
        *[pl.BlockSpec((1, own_rows, tile), lambda f, r: (expert, 0, f))] * 3,
        pl.BlockSpec((1, width, tile), lambda f, r: (expert, 0, f)),
        pl.BlockSpec((1, width, tile), lambda f, r: (expert, 0, f)),
        pl.BlockSpec((1, tile, width), lambda f, r: (expert, f, 0)),
    ]
    given = (x_rows, c_rows, gates, *own, w_gate, w_up, w_down)
    aliases = {}
    if buffers is not None:
        aliases = {len(given) + i: i for i in range(3)}
        in_specs += [pl.BlockSpec(memory_space=pl.ANY)] * 3
        given += tuple(buffers)
    return pl.pallas_call(
        grads_kernel,
        grid=(hidden // tile, parts),
        out_shape=[jax.ShapeDtypeStruct(shape, F32) for shape in [*shapes, (8, 128)]],
        in_specs=in_specs,
        out_specs=[
            pl.BlockSpec((1, width, tile), lambda f, r: (expert, 0, f)),
            pl.BlockSpec((1, width, tile), lambda f, r: (expert, 0, f)),
            pl.BlockSpec((1, tile, width), lambda f, r: (expert, f, 0)),
            pl.BlockSpec((8, 128), lambda f, r: (0, 0)),
        ],
        scratch_shapes=[
            pltpu.VMEM((2 * tile, width), F32),
            pltpu.VMEM((2 * tile, part), BF16),
            pltpu.VMEM((tile, part), BF16),
        ],
        input_output_aliases=aliases,
        compiler_params=pltpu.CompilerParams(vmem_limit_bytes=VMEM_BYTES),
        cost_estimate=pl.CostEstimate(
            flops=12 * rows * width * hidden,
            bytes_accessed=12 * rows * width + 24 * width * hidden,
            transcendentals=rows * hidden,
        ),
    )(*given)


def turn(values, cos, sin):
    return values * cos + pltpu.roll(values, values.shape[-1] // 2, 1) * sin


def qkv_kernel(
    tok_ref,
    gain_ref,
    w_ref,
    cos_ref,
    sin_ref,
    gq_ref,
    gk_ref,
    normed_ref,
    qpre_ref,
    kpre_ref,
    qrot_ref,
    krot_ref,
    value_ref,
):
    head = cos_ref.shape[1]
    heads = qpre_ref.shape[1] // head
    normed = norm_rows(tok_ref[...].astype(F32), gain_ref[...]).astype(BF16)
    normed_ref[...] = normed
    cos, sin = cos_ref[...], sin_ref[...]
    for pair in range(0, heads, 2):
        cols = slice(pair * head, (pair + 2) * head)
        pre = jnp.dot(normed, w_ref[:, cols], preferred_element_type=F32)
        qpre_ref[:, cols] = pre
        for h in range(2):
            one = slice(h * head, (h + 1) * head)
            rot = turn(norm_rows(pre[:, one], gq_ref[...]), cos, sin)
            qrot_ref[:, (pair + h) * head : (pair + h + 1) * head] = rot.astype(BF16)
    cols = slice(heads * head, (heads + 2) * head)
    pre = jnp.dot(normed, w_ref[:, cols], preferred_element_type=F32)
    kpre_ref[...] = pre[:, :head]
    krot_ref[...] = turn(norm_rows(pre[:, :head], gk_ref[...]), cos, sin).astype(BF16)
    value_ref[...] = pre[:, head:].astype(BF16)


def make_qkv(tokens, gain, weight, cos, sin, query_gain, key_gain):
    length, width = tokens.shape
    head = cos.shape[1]
    cols = weight.shape[1]
    q_cols = cols - 3 * head
    block = Q_BLOCK

    def rows(size):
        return pl.BlockSpec((block, size), lambda i: (i, 0))

    def fixed(*shape):
        return pl.BlockSpec(shape, lambda i: (0, 0))

    return pl.pallas_call(
        qkv_kernel,
        grid=(length // block,),
        in_specs=[
            rows(width),
            fixed(1, width),
            fixed(width, cols),
            rows(head),
            rows(head),
            fixed(1, head),
            fixed(1, head),
        ],
        out_specs=[rows(width), rows(q_cols), rows(head), rows(q_cols), rows(head), rows(head)],
        out_shape=[
            jax.ShapeDtypeStruct((length, width), BF16),
            jax.ShapeDtypeStruct((length, q_cols), F32),
            jax.ShapeDtypeStruct((length, head), F32),
            jax.ShapeDtypeStruct((length, q_cols), BF16),
            jax.ShapeDtypeStruct((length, head), BF16),
            jax.ShapeDtypeStruct((length, head), BF16),
        ],
        compiler_params=pltpu.CompilerParams(vmem_limit_bytes=VMEM_BYTES),
        cost_estimate=FREE,
    )(tokens, gain[None], weight, cos, sin, query_gain[None], key_gain[None])


def masked_scores(q_ref, k_ref, seg_row_ref, seg_col_ref, block, keys):
    size = q_ref.shape[0]
    scores = dot_nt(k_ref[:keys], q_ref[...]) * q_ref.shape[1] ** (-0.5)
    key_at = lax.broadcasted_iota(jnp.int32, (keys, size), 0)
    query_at = lax.broadcasted_iota(jnp.int32, (keys, size), 1) + block * size
    allowed = (key_at <= query_at) & (seg_col_ref[:keys] == seg_row_ref[...])
    return jnp.where(allowed, scores, -1e30)


def attend_kernel(q_ref, k_ref, vt_ref, seg_row_ref, seg_col_ref, out_ref, log_ref):
    size = q_ref.shape[0]
    blocks = k_ref.shape[0] // size
    for block in range(blocks):

        @pl.when(pl.program_id(1) == block)
        def _(block=block):
            keys = (block + 1) * size
            scores = masked_scores(q_ref, k_ref, seg_row_ref, seg_col_ref, block, keys)
            largest = jnp.max(scores, axis=0, keepdims=True)
            raised = jnp.exp(scores - largest)
            total = jnp.sum(raised, axis=0, keepdims=True)
            weights = (raised * (1.0 / total)).astype(BF16)
            out = jnp.dot(vt_ref[:, :keys], weights, preferred_element_type=F32)
            out_ref[...] = out.T.astype(BF16)
            log_ref[0] = largest + jnp.log(total)


def attend(query, key, value, segment):
    length, cols = query.shape
    head = key.shape[1]
    block = Q_BLOCK
    heads = cols // head
    return pl.pallas_call(
        attend_kernel,
        grid=(heads, length // block),
        in_specs=[
            pl.BlockSpec((block, head), lambda h, i: (i, h)),
            pl.BlockSpec((length, head), lambda h, i: (0, 0)),
            pl.BlockSpec((head, length), lambda h, i: (0, 0)),
            pl.BlockSpec((1, block), lambda h, i: (0, i)),
            pl.BlockSpec((length, 1), lambda h, i: (0, 0)),
        ],
        out_specs=[
            pl.BlockSpec((block, head), lambda h, i: (i, h)),
            pl.BlockSpec((1, 1, block), lambda h, i: (h, 0, i)),
        ],
        out_shape=[
            jax.ShapeDtypeStruct((length, cols), BF16),
            jax.ShapeDtypeStruct((heads, 1, length), F32),
        ],
        compiler_params=pltpu.CompilerParams(vmem_limit_bytes=VMEM_BYTES),
        cost_estimate=FREE,
    )(query, key, value.T, segment[None], segment[:, None])


def attend_back_kernel(
    q_ref,
    k_ref,
    kt_ref,
    v_ref,
    do_ref,
    log_ref,
    seg_row_ref,
    seg_col_ref,
    qpre_ref,
    kpre_ref,
    cos_ref,
    sin_ref,
    gq_ref,
    gk_ref,
    dq_ref,
    dk_ref,
    dv_ref,
    dgain_ref,
    key_sum,
    value_sum,
):
    size, head = q_ref.shape
    blocks = k_ref.shape[0] // size
    scale = head ** (-0.5)
    first = (pl.program_id(0) == 0) & (pl.program_id(1) == 0)
    last = (pl.program_id(0) == pl.num_programs(0) - 1) & (pl.program_id(1) == blocks - 1)

    @pl.when(first)
    def _():
        key_sum[...] = jnp.zeros_like(key_sum)
        value_sum[...] = jnp.zeros_like(value_sum)
        dgain_ref[...] = jnp.zeros_like(dgain_ref)

    def pull(grad, pre, gain, cos, sin):
        grad = grad.astype(BF16).astype(F32)
        turned = grad * cos + pltpu.roll(grad * sin, head // 2, 1)
        scale_row = lax.rsqrt(jnp.mean(pre * pre, axis=-1, keepdims=True) + EPSILON)
        unit = pre * scale_row
        gain_grad = jnp.sum(turned * unit, axis=0, keepdims=True)
        turned = turned * gain
        inner = jnp.mean(turned * unit, axis=-1, keepdims=True)
        return scale_row * (turned - unit * inner), gain_grad

    for block in range(blocks):

        @pl.when(pl.program_id(1) == block)
        def _(block=block):
            keys = (block + 1) * size
            rows = slice(block * size, keys)
            scores = masked_scores(q_ref, k_ref, seg_row_ref, seg_col_ref, block, keys)
            weights = jnp.exp(scores - log_ref[0])
            grads = dot_nt(v_ref[:keys], do_ref[...])
            inner = jnp.sum(weights * grads, axis=0, keepdims=True)
            score_grads = (weights * (grads - inner)).astype(BF16)
            value_sum[:keys] += jnp.dot(
                weights.astype(BF16), do_ref[...], preferred_element_type=F32
            )
            key_sum[:keys] += jnp.dot(score_grads, q_ref[...], preferred_element_type=F32)
            query_grad = jnp.dot(kt_ref[:, :keys], score_grads, preferred_element_type=F32)
            pre_grad, gain_grad = pull(
                query_grad.T * scale, qpre_ref[...], gq_ref[...], cos_ref[rows], sin_ref[rows]
            )
            dq_ref[...] = pre_grad.astype(BF16)
            dgain_ref[0:1] += gain_grad

    @pl.when(last)
    def _():
        pre_grad, gain_grad = pull(
            key_sum[...] * scale, kpre_ref[...], gk_ref[...], cos_ref[...], sin_ref[...]
        )
        dk_ref[...] = pre_grad.astype(BF16)
        dgain_ref[1:2] = gain_grad
        dv_ref[...] = value_sum[...].astype(BF16)


def attend_back(query, key, value, grad, logs, segment, qpre, kpre, cos, sin, gq, gk):
    length, cols = query.shape
    head = key.shape[1]
    block = Q_BLOCK
    heads = cols // head
    tile = pl.BlockSpec((block, head), lambda h, i: (i, h))

    def fixed(*shape):
        return pl.BlockSpec(shape, lambda h, i: (0, 0))

    return pl.pallas_call(
        attend_back_kernel,
        grid=(heads, length // block),
        in_specs=[
            tile,
            fixed(length, head),
            fixed(head, length),
            fixed(length, head),
            tile,
            pl.BlockSpec((1, 1, block), lambda h, i: (h, 0, i)),
            pl.BlockSpec((1, block), lambda h, i: (0, i)),
            fixed(length, 1),
            tile,
            fixed(length, head),
            fixed(length, head),
            fixed(length, head),
            fixed(1, head),
            fixed(1, head),
        ],
        out_specs=[tile, fixed(length, head), fixed(length, head), fixed(8, head)],
        out_shape=[
            jax.ShapeDtypeStruct((length, cols), BF16),
            jax.ShapeDtypeStruct((length, head), BF16),
            jax.ShapeDtypeStruct((length, head), BF16),
            jax.ShapeDtypeStruct((8, head), F32),
        ],
        scratch_shapes=[pltpu.VMEM((length, head), F32), pltpu.VMEM((length, head), F32)],
        compiler_params=pltpu.CompilerParams(vmem_limit_bytes=VMEM_BYTES),
        cost_estimate=pl.CostEstimate(
            flops=14 * length * length * cols,
            bytes_accessed=12 * length * cols,
            transcendentals=length * length * heads,
        ),
    )(
        query,
        key,
        key.T,
        value,
        grad,
        logs,
        segment[None],
        segment[:, None],
        qpre,
        kpre,
        cos,
        sin,
        gq[None],
        gk[None],
    )


def on_device(
    tokens,
    segment_ids,
    routes,
    w_query,
    w_key,
    w_value,
    w_output,
    w_router,
    gain_attn,
    gain_moe,
    gain_query,
    gain_key,
    w_gate,
    w_up,
    w_down,
    cotangent,
):
    bands, peers = lax.axis_size("dp"), lax.axis_size("expert")
    band, peer = lax.axis_index("dp"), lax.axis_index("expert")
    own_tokens = tokens[0]
    tok_count, width = own_tokens.shape
    band_rows = w_query.shape[0]
    experts = w_router.shape[1]
    gain_rows = gain_query.shape[0]
    head_size = gain_rows * bands * peers
    heads = w_query.shape[1] // head_size // bands
    q_cols, k_cols = heads * head_size, head_size
    qkv_cols = q_cols + 2 * k_cols
    owned = experts // peers

    small = jnp.concatenate(
        [
            w_router,
            gain_attn[:, None],
            gain_moe[:, None],
            jnp.pad(gain_query, (0, band_rows - gain_rows))[:, None],
            jnp.pad(gain_key, (0, band_rows - gain_rows))[:, None],
        ],
        axis=1,
    )
    shared = owned >= bands == 4
    top = routes.shape[-1]
    ride = tok_count * top // band_rows
    if shared:
        small = jnp.concatenate([small, routes[0].reshape(band_rows, ride).astype(BF16)], axis=1)
    small = jnp.pad(small, ((0, 0), (0, 128 - small.shape[1])))
    packed = jnp.concatenate(
        [
            w_query.reshape(band_rows, bands, q_cols),
            w_key.reshape(band_rows, bands, k_cols),
            w_value.reshape(band_rows, bands, k_cols),
            jnp.broadcast_to(small[:, None], (band_rows, bands, 128)),
        ],
        axis=-1,
    ).transpose(1, 0, 2)
    tokens_all, packed_all, out_w = start_moves(own_tokens, packed, w_output)
    qkv_w = packed_all[:, :qkv_cols]
    small_all = packed_all[:, qkv_cols:]
    router_full = small_all[:, :experts]
    attn_gain = small_all[:, experts].astype(F32)
    moe_gain = small_all[:, experts + 1].astype(F32)
    head_gains = small_all.reshape(bands * peers, band_rows, 128)[:, :gain_rows]
    query_gain = head_gains[:, :, experts + 2].reshape(-1).astype(F32)
    key_gain = head_gains[:, :, experts + 3].reshape(-1).astype(F32)

    def beside(rows, *sides):
        used = sum(side.shape[-1] for side in sides)
        filler = jnp.zeros((tok_count, SIDE - used), BF16)
        return jnp.concatenate([rows, *(side.astype(BF16) for side in sides), filler], axis=1)

    def side_gates(sides):
        gates = sides[..., :experts].astype(F32)
        gates = gates + sides[..., experts : 2 * experts].astype(F32)
        return lax.dynamic_slice_in_dim(gates, peer * owned, owned, axis=2)

    cot_rows = beside(after(cotangent[0], out_w), routes[0])
    if shared:
        cot_all = lax.all_gather(cot_rows, ("dp", "expert"), axis=0, tiled=False)
        cot_all = cot_all.reshape(bands, peers, tok_count, -1)
    else:
        cot_all = lax.all_gather(cot_rows, "expert", axis=0)[None]
    here = band if shared else 0

    inputs = own_tokens.astype(F32)
    length = tokens_all.shape[0]
    half = head_size // 2
    frequency = ROPE_BASE ** (-jnp.arange(half, dtype=F32) * 2.0 / head_size)
    angles = jnp.arange(length, dtype=jnp.int32).astype(F32)[:, None] * frequency[None, :]
    cos = jnp.concatenate([jnp.cos(angles)] * 2, axis=-1)
    sin = jnp.concatenate([-jnp.sin(angles), jnp.sin(angles)], axis=-1)
    normed, query_pre, key_pre, query_low, key_low, value_low = make_qkv(
        tokens_all, attn_gain, packed_all, cos, sin, query_gain, key_gain
    )
    segment = segment_ids[0]
    attended_low, log_total = attend(query_low, key_low, value_low, segment)
    branch = dot("tm,md->td", attended_low, out_w).astype(BF16)
    branch = sum_blocks(branch.reshape(bands, tok_count, width), "dp")
    hidden = inputs + branch

    normed_moe_f, moe_pull = jax.vjp(norm_rows, hidden, moe_gain)
    normed_moe = normed_moe_f.astype(BF16)
    mask = jnp.any(routes[0][..., None] == jnp.arange(experts, dtype=jnp.int32), axis=1)
    own_gates = masked_softmax(dot("td,de->te", normed_moe, router_full), mask)
    high = own_gates.astype(BF16)
    low = own_gates - high.astype(F32)
    moe_rows = beside(normed_moe, high, low)

    def in_order(columns):
        pick = [
            lax.dynamic_index_in_dim(columns, here ^ i, 0, keepdims=False)
            for i in range(len(columns))
        ]
        return jnp.concatenate(pick)

    if shared:
        sides = small_all.reshape(bands, peers, band_rows, 128)
        routes_all = sides[..., experts + 4 : experts + 4 + ride]
        routes_all = in_order(routes_all.reshape(bands, peers, tok_count, top))
        ranks_all = block_ranks(routes_all.astype(jnp.int32), peer, owned, experts)
        moe_rows = after(moe_rows, ranks_all)
    moe_all = gather_square(moe_rows) if shared else gather_rows(moe_rows)[None]
    cot_all = after(cot_all, moe_all)
    if not shared:
        routes_all = cot_all[0, ..., width : width + top].astype(jnp.int32)
        ranks_all = block_ranks(routes_all, peer, owned, experts)
    own_ranks = ranks_all[:peers]
    token_ranks = own_ranks.transpose(0, 2, 1)
    cot_placed = place_rows(ranks_all, cot_all, here).reshape(owned, -1, width)
    x_placed = place_rows(ranks_all, moe_all, here).reshape(owned, -1, width)
    all_gates = slot_values(ranks_all, side_gates(in_order(moe_all[..., width:])))
    all_gates = all_gates.transpose(1, 0, 2).reshape(owned, -1, 1)
    *own, slot_grads, rows_back, rows_out = own_experts(
        x_placed,
        cot_placed,
        all_gates,
        peers * CAP,
        w_gate,
        w_up,
        w_down,
    )
    if not shared:
        active, gate_low, up_low = own
        expert_sums = lax.psum(
            (
                dot("erd,erf->edf", x_placed, gate_low).astype(BF16),
                dot("erd,erf->edf", x_placed, up_low).astype(BF16),
                dot("erf,erd->efd", active, cot_placed).astype(BF16),
            ),
            "dp",
        )
    rows_back = combine(token_ranks, rows_back)
    back = lax.psum_scatter(rows_back, "expert", scatter_dimension=0, tiled=True)[0]
    slot_grads = slot_grads.reshape(owned, peers, CAP).transpose(1, 0, 2)
    slots = jnp.arange(CAP, dtype=jnp.int32)[None, None, :, None]
    token_grads = jnp.where(own_ranks[:, :, None, :] == slots, slot_grads[..., None], 0.0)
    token_grads = jnp.sum(token_grads, axis=2)
    gate_grads = (
        lax.all_to_all(token_grads, "expert", split_axis=0, concat_axis=0, tiled=True)
        .reshape(experts, tok_count)
        .T
    )
    rows_out = combine(after(token_ranks, rows_back), rows_out)

    expert_sums = None if shared else expert_sums

    def next_expert(number, sums, *earlier):
        if not shared or number >= owned:
            return sums, earlier[0]
        *sums, mark = expert_grads(
            x_placed,
            cot_placed,
            after(all_gates, *earlier),
            own,
            w_gate,
            w_up,
            w_down,
            number,
            sums,
        )
        return sums, mark

    expert_sums, mark = next_expert(0, expert_sums, rows_out)
    back = after(back, mark)

    grad_logits = own_gates * (
        gate_grads - jnp.sum(own_gates * gate_grads, axis=-1, keepdims=True)
    )
    grad_router_w = jnp.einsum("td,te->de", normed_moe.astype(F32), grad_logits, precision=PRECISE)
    grad_normed = back.astype(F32) + jnp.einsum(
        "te,de->td", grad_logits, router_full.astype(F32), precision=PRECISE
    )
    grad_hidden_n, grad_moe_gain = moe_pull(grad_normed)
    grad_hidden = cotangent[0].astype(F32) + grad_hidden_n
    grad_branch = grad_hidden.astype(BF16)
    branch_all = lax.all_gather(grad_branch, "dp", axis=0, tiled=True)
    expert_sums, mark = next_expert(1, expert_sums, grad_branch)
    branch_all = after(branch_all, mark)

    grad_output = dot("tm,td->md", attended_low, branch_all).astype(BF16)
    grad_attended = dot("td,md->tm", branch_all, out_w).astype(BF16)
    grad_attended = after(grad_attended, grad_output)
    grad_output = lax.psum_scatter(grad_output, "expert", scatter_dimension=0, tiled=True)
    moe_sum = lax.psum_scatter(
        after(rows_out, branch_all), "expert", scatter_dimension=0, tiled=True
    )[0]
    block_out = (hidden + moe_sum.astype(F32)).astype(BF16)
    query_grad, key_grad, value_grad, head_grads = attend_back(
        query_low,
        key_low,
        value_low,
        grad_attended,
        log_total,
        segment,
        query_pre,
        key_pre,
        cos,
        sin,
        query_gain,
        key_gain,
    )
    qkv_grad = jnp.concatenate([query_grad, key_grad, value_grad], axis=1)
    grad_normed_attn = dot("tm,dm->td", qkv_grad, qkv_w).astype(BF16)
    expert_sums, mark = next_expert(2, expert_sums, grad_normed_attn, block_out)
    grad_normed_attn = lax.psum_scatter(
        grad_normed_attn, "dp", scatter_dimension=0, tiled=True
    )
    grad_normed_attn = after(grad_normed_attn, mark).astype(F32)
    _, attn_pull = jax.vjp(norm_rows, inputs, attn_gain)
    grad_inputs_n, grad_attn_gain = attn_pull(grad_normed_attn)
    grad_tokens = grad_hidden + grad_inputs_n

    whole_gains = jnp.stack([grad_attn_gain, grad_moe_gain], axis=1)
    head_gains = head_grads[:2].T
    head_gains = jnp.pad(
        head_gains.reshape(bands * peers, gain_rows, 2),
        ((0, 0), (0, band_rows - gain_rows), (0, 0)),
    )
    small_grad = jnp.concatenate(
        [grad_router_w, whole_gains, head_gains.reshape(width, 2)], axis=1
    )
    small_grad = jnp.pad(small_grad, ((0, 0), (0, 128 - small_grad.shape[1])))
    band_qkv = jnp.concatenate([dot("td,tm->dm", normed, qkv_grad), small_grad], axis=1)
    band_qkv = band_qkv.astype(BF16).reshape(bands, peers, band_rows, -1).transpose(1, 0, 2, 3)
    for number in range(3, owned):
        expert_sums, mark = next_expert(number, expert_sums, band_qkv)
    band_qkv = lax.psum_scatter(
        band_qkv.reshape(width, -1), "expert", scatter_dimension=0, tiled=True
    ).reshape(bands, band_rows, -1)
    band_qkv = after(band_qkv, mark)
    band_qkv = lax.all_to_all(band_qkv, "dp", split_axis=0, concat_axis=0, tiled=True).transpose(
        1, 0, 2
    )
    grad_query = band_qkv[:, :, :q_cols].astype(F32).reshape(band_rows, -1)
    grad_key = band_qkv[:, :, q_cols : q_cols + k_cols].astype(F32).reshape(band_rows, -1)
    grad_value = band_qkv[:, :, q_cols + k_cols : qkv_cols].astype(F32).reshape(band_rows, -1)
    smaller = jnp.sum(band_qkv[:, :, qkv_cols:].astype(F32), axis=1)
    return (
        block_out[None],
        grad_tokens[None],
        grad_query,
        grad_key,
        grad_value,
        grad_output.astype(F32),
        smaller[:, :experts],
        smaller[:, experts],
        smaller[:, experts + 1],
        smaller[:gain_rows, experts + 2],
        smaller[:gain_rows, experts + 3],
        expert_sums[0].astype(F32),
        expert_sums[1].astype(F32),
        expert_sums[2].astype(F32),
    )


def solution(mesh):
    both = ("dp", "expert")
    return jax.shard_map(
        on_device,
        mesh=mesh,
        in_specs=(
            P("expert", "dp", None),
            P("expert", None),
            P("expert", "dp", None),
            P(both, None),
            P(both, None),
            P(both, None),
            P(both, None),
            P(both, None),
            P(both),
            P(both),
            P(both),
            P(both),
            P("expert", None, None),
            P("expert", None, None),
            P("expert", None, None),
            P("expert", "dp", None),
        ),
        out_specs=(
            P("expert", "dp", None),
            P("expert", "dp", None),
            P(both, None),
            P(both, None),
            P(both, None),
            P(both, None),
            P(both, None),
            P(both),
            P(both),
            P(both),
            P(both),
            P("expert", None, None),
            P("expert", None, None),
            P("expert", None, None),
        ),
        check_vma=False,
    )
```
